32 devices in a mesh: section: 4 (over y, core), dp: 8 (over z, x).
Axes of the slice: x: 2, y: 2, z: 4, core: 2. Of those that a mesh axis runs over, the one named last changes fastest.
Arguments:
- tokens: bfloat16 [16, 280, 768], P('dp'), may hold values from -6 to 6
- lengths: int32 [16], P('dp'), may hold values from 5 to 40, as said below
- cotangent: bfloat16 [16, 280, 768], P('dp'), may hold values from -6 to 6
- attend_gain: float32 [4, 768], P('section', 'dp'), may hold values from 0.1 to 1.9
- attend_shift: float32 [4, 768], P('section', 'dp'), may hold values from -1.75 to 1.75
- joint_weight: float32 [4, 768, 2304], P('section', 'dp'), may hold values from -0.21875 to 0.21875
- joint_bias: float32 [4, 1536], P('section', 'dp'), may hold values from -3 to 3
- output_weight: float32 [4, 768, 768], P('section', 'dp'), may hold values from -1.25 to 1.25
- output_bias: float32 [4, 768], P('section', 'dp'), may hold values from -1.75 to 1.75
- feed_gain: float32 [4, 768], P('section', 'dp'), may hold values from 0.1 to 1.9
- feed_shift: float32 [4, 768], P('section', 'dp'), may hold values from -1.75 to 1.75
- up_weight: float32 [4, 768, 3072], P('section', 'dp'), may hold values from -0.21875 to 0.21875
- up_bias: float32 [4, 3072], P('section', 'dp'), may hold values from -3 to 3
- down_weight: float32 [4, 3072, 768], P('section', 'dp'), may hold values from -0.109375 to 0.109375
- down_bias: float32 [4, 768], P('section', 'dp'), may hold values from -1.75 to 1.75
Outputs:
- outputs: bfloat16 [16, 280, 768], P('dp', None, 'section')
- token_grad: bfloat16 [16, 280, 768], P('dp', None, 'section')
- grad_attend_gain: float32 [4, 768], P('section', 'dp')
- grad_attend_shift: float32 [4, 768], P('section', 'dp')
- grad_joint_weight: float32 [4, 768, 2304], P('section', 'dp')
- grad_joint_bias: float32 [4, 1536], P('section', 'dp')
- grad_output_weight: float32 [4, 768, 768], P('section', 'dp')
- grad_output_bias: float32 [4, 768], P('section', 'dp')
- grad_feed_gain: float32 [4, 768], P('section', 'dp')
- grad_feed_shift: float32 [4, 768], P('section', 'dp')
- grad_up_weight: float32 [4, 768, 3072], P('section', 'dp')
- grad_up_bias: float32 [4, 3072], P('section', 'dp')
- grad_down_weight: float32 [4, 3072, 768], P('section', 'dp')
- grad_down_bias: float32 [4, 768], P('section', 'dp')
The draws below stay inside these ranges and needn't reach their ends.
Inputs may be any that keep to these rules, and one draw needn't show every extreme that they name: `lengths`: in every draw some pair has a caption of exactly 40 rows and some pair one of exactly the least length.
All inputs are finite; a program needn't handle non-finite values.
Results may differ from the reference program's by a relative error of at most 0.015.
Values may be sent and summed in bfloat16 or wider, within the bound.
No kernel may reach another device: no remote copies, remote signals or barrier semaphores. Data moves between devices by JAX's collectives and lax.ppermute only.
A program may use at most 320 MiB of HBM per device.

```python
import jax
import jax.numpy as jnp
from jax import lax

D = 768
HEADS = 12
HEAD_DIM = 64
FF = 3072
CAPTION = 40
SEQ = 280
PAIRS_DEV = 2
PAIRS = 16
LAYERS = 4
N_DP = 8


def draw_lengths(key, part):
    key = jax.random.fold_in(key, 7)
    first, second = jax.random.split(key, 2)
    least = max(1, CAPTION // 8)
    drawn = jax.random.randint(first, (PAIRS,), least, CAPTION + 1)
    spots = jax.random.permutation(second, PAIRS)
    drawn = drawn.at[spots[0]].set(CAPTION)
    drawn = drawn.at[spots[1]].set(least)
    return drawn.astype(jnp.int32)


def steps_of(rng, dims, shards, smallest, top_value):
    def one(position, parts):
        heights = jax.random.uniform(jax.random.fold_in(jax.random.fold_in(rng, 6), position), (parts,), jnp.float32, smallest / len(shards), top_value / len(shards))
        return jnp.repeat(jnp.exp(heights), dims[position] // parts).reshape((-1,) + (1,) * (len(dims) - position - 1))

    level = one(*shards[0])
    for cut in shards[1:]:
        level = level * one(*cut)
    return level


def gaussian(stream_key, extent, width, bound, cuts=(), kind=jnp.bfloat16):
    level = steps_of(stream_key, extent, cuts, -0.22, 0.18) if cuts else 1.0
    values = jax.random.normal(stream_key, extent, jnp.float32) * width * level
    return jnp.minimum(jnp.maximum(values, -bound), bound).astype(kind)


def setup_inputs(seed: int = 0) -> dict:
    keys = jax.random.split(jax.random.key(seed), 16)
    return {
        "tokens": gaussian(keys[0], (PAIRS, SEQ, D), 1.0, 6.0, ((0, 8),)),
        "lengths": draw_lengths(jax.random.fold_in(keys[15], 71), 0),
        "cotangent": gaussian(keys[2], (PAIRS, SEQ, D), 1.0, 6.0, ((0, 8),)),
        "attend_gain": jnp.clip(1.0 + 0.18 * jax.random.normal(keys[3], (LAYERS, D), jnp.float32), 0.1, 1.9),
        "attend_shift": gaussian(keys[4], (LAYERS, D), 0.3, 1.75, ((0, 4), (1, 8)), jnp.float32),
        "joint_weight": gaussian(keys[5], (LAYERS, D, 3 * D), D ** -0.5, 0.21875, ((0, 4), (1, 8)), jnp.float32),
        "joint_bias": gaussian(keys[6], (LAYERS, 2 * D), 0.5, 3.0, ((0, 4), (1, 8)), jnp.float32),
        "output_weight": gaussian(keys[7], (LAYERS, D, D), (D // 32) ** -0.5, 1.25, ((0, 4), (1, 8)), jnp.float32),
        "output_bias": gaussian(keys[8], (LAYERS, D), 0.3, 1.75, ((0, 4), (1, 8)), jnp.float32),
        "feed_gain": jnp.clip(1.0 + 0.18 * jax.random.normal(keys[9], (LAYERS, D), jnp.float32), 0.1, 1.9),
        "feed_shift": gaussian(keys[10], (LAYERS, D), 0.3, 1.75, ((0, 4), (1, 8)), jnp.float32),
        "up_weight": gaussian(keys[11], (LAYERS, D, FF), D ** -0.5, 0.21875, ((0, 4), (1, 8)), jnp.float32),
        "up_bias": gaussian(keys[12], (LAYERS, FF), 0.5, 3.0, ((0, 4), (1, 8)), jnp.float32),
        "down_weight": gaussian(keys[13], (LAYERS, FF, D), FF ** -0.5, 0.109375, ((0, 4), (1, 8)), jnp.float32),
        "down_bias": gaussian(keys[14], (LAYERS, D), 0.3, 1.75, ((0, 4), (1, 8)), jnp.float32),
    }


@jax.custom_vjp
def low(v):
    return lax.optimization_barrier(v.astype(jnp.bfloat16)).astype(jnp.float32)

@jax.custom_vjp
def low_back(v):
    return v

def low_keep(v):
    return (low(v), None)

def low_pass(kept, grad):
    return (grad,)

def back_keep(v):
    return (v, None)

def back_low(kept, grad):
    return (low(grad),)
low.defvjp(low_keep, low_pass)
low_back.defvjp(back_keep, back_low)

def normalize(stream, gain, shift):
    average = lax.optimization_barrier(jnp.mean(stream, axis=-1, keepdims=True))
    centered = stream - average
    spread = lax.optimization_barrier(jnp.mean(centered * centered, axis=-1, keepdims=True))
    return centered * lax.rsqrt(spread + 1e-06) * gain + shift

def gelu_exact(entries):
    return jax.nn.gelu(entries, approximate=False)

def dense(left, right):
    return jnp.einsum('...d,df->...f', left, right, precision=lax.Precision.HIGHEST)

def one_layer(stream, usable, weights):
    attend_gain, attend_shift, joint_weight, joint_bias, output_weight, output_bias, feed_gain, feed_shift, up_weight, up_bias, down_weight, down_bias = tuple((low(item) for item in weights))
    pair_count, seq_len, model_width = stream.shape
    factor = HEAD_DIM ** (-0.5)
    normed = low(normalize(stream, attend_gain, attend_shift))
    bias_full = jnp.concatenate([joint_bias[:model_width], jnp.zeros((model_width,), jnp.float32), joint_bias[model_width:]])
    joined = low_back(low(dense(normed, joint_weight) + bias_full))
    shaped = joined.reshape(pair_count, seq_len, 3, HEADS, HEAD_DIM)
    query_rows = shaped[:, :, 0]
    key_rows = shaped[:, :, 1]
    value_rows = shaped[:, :, 2]
    scores = low_back(jnp.einsum('pqhe,pkhe->phqk', query_rows, key_rows, precision=lax.Precision.HIGHEST) * factor)
    scores = jnp.where(usable[:, None, None, :], scores, -1e+30)
    highest = lax.optimization_barrier(jnp.max(scores, axis=-1, keepdims=True))
    raised = jnp.exp(scores - highest)
    weights_soft = raised / lax.optimization_barrier(jnp.sum(raised, axis=-1, keepdims=True))
    context = jnp.einsum('phqk,pkhe->pqhe', low(weights_soft), value_rows, precision=lax.Precision.HIGHEST)
    context = low_back(low(context.reshape(pair_count, seq_len, model_width)))
    middle = stream + low_back(dense(context, output_weight) + output_bias)
    normed_two = low(normalize(middle, feed_gain, feed_shift))
    hidden = low_back(dense(normed_two, up_weight) + up_bias)
    activated = low(gelu_exact(hidden))
    return middle + low_back(dense(activated, down_weight) + down_bias)

def run_stack(block, lengths, weights):
    places = lax.broadcasted_iota(jnp.int32, (block.shape[0], block.shape[1]), 1)
    usable = (places < lengths[:, None]) | (places >= CAPTION)
    for layer in range(LAYERS):
        block = one_layer(block, usable, tuple((item[layer] for item in weights)))
        if layer + 1 < LAYERS:
            block = low_back(low(block))
    return low(block)

def forward(tokens, lengths, weights):
    grouped = tokens.reshape(N_DP, PAIRS_DEV, SEQ, D)
    length_groups = lengths.reshape(N_DP, PAIRS_DEV)
    group_fn = jax.checkpoint(lambda pieces: run_stack(pieces[0], pieces[1], weights))
    return lax.map(group_fn, (grouped, length_groups)).reshape(PAIRS, SEQ, D)

def reference(tokens, lengths, cotangent, attend_gain, attend_shift, joint_weight, joint_bias, output_weight, output_bias, feed_gain, feed_shift, up_weight, up_bias, down_weight, down_bias):
    weights = (attend_gain, attend_shift, joint_weight, joint_bias, output_weight, output_bias, feed_gain, feed_shift, up_weight, up_bias, down_weight, down_bias)
    outputs, pull = jax.vjp(lambda stream, params: forward(stream, lengths, params), tokens.astype(jnp.float32), weights)
    token_grad, grads = pull(cotangent.astype(jnp.float32))
    return (outputs.astype(jnp.bfloat16), token_grad.astype(jnp.bfloat16), grads[0], grads[1], grads[2], grads[3], grads[4], grads[5], grads[6], grads[7], grads[8], grads[9], grads[10], grads[11])
```

```python
import functools

import jax
import jax.numpy as jnp
from jax import lax
from jax.experimental import pallas as pl
from jax.experimental.pallas import tpu as pltpu
from jax.sharding import PartitionSpec as P

D = 768
HEADS = 12
FF = 3072
CAPTION = 40
ROWS = 288
CHUNKS = 12
HALF = 6
EPS = 1e-6
BF = jnp.bfloat16
F32 = jnp.float32
PAIRED = 2 * (D // HEADS)
VMEM_LIMIT = 58 * 2**20
WIDE = FF + 2 * D
AG, AS, BQ, BV, OB, FG, FS, DB, UB = 0, 1, 2, 3, 4, 5, 6, 7, 8


def dot(a, b, ca=1, cb=0):
    return lax.dot_general(a, b, (((ca,), (cb,)), ((), ())), preferred_element_type=F32)


def spread_of(v):
    mean = jnp.mean(v, axis=-1, keepdims=True)
    cent = v - mean
    return cent, lax.rsqrt(jnp.mean(cent * cent, axis=-1, keepdims=True) + EPS)


def gelu_pair(h):
    x = jnp.abs(h) * (0.5**0.5)
    t = 1.0 / (1.0 + 0.5 * x)
    poly = jnp.full_like(t, 0.17087277)
    for c in (-0.82215223, 1.48851587, -1.13520398, 0.27886807, -0.18628806, 0.09678418,
              0.37409196, 1.00002368, -1.26551223):
        poly = poly * t + c
    gauss = jnp.exp(-x * x)
    tail = 0.5 * t * gauss * jnp.exp(poly)
    phi = jnp.where(h < 0.0, tail, 1.0 - tail)
    return h * phi, phi + h * gauss * 0.3989422804014327


def square(block):
    return block.reshape(D, D)


def weight_copies(w, wv, wd, sems):
    per, q = wd.shape[1], wd.shape[2]
    out = [pltpu.make_async_copy(w.at[:, k], wv.at[k], sems.at[k]) for k in range(8)]
    for b in range(4):
        if q == 4:
            src = w.at[pl.ds(b * per, per), pl.ds(8, 4)]
        else:
            src = w.at[:, pl.ds(8 + b, 1)]
        out.append(pltpu.make_async_copy(src, wd.at[b], sems.at[8 + b]))
    return out


def start_weights(pick, wa, wb, wv, wd, sems, order):
    @pl.when(pick == 0)
    def _():
        c = weight_copies(wa, wv, wd, sems)
        for k in order:
            c[k].start()

    @pl.when(pick != 0)
    def _():
        c = weight_copies(wb, wv, wd, sems)
        for k in order:
            c[k].start()

    return weight_copies(wa, wv, wd, sems)


def handing(core, keep, send, sems, waits):
    def hand_on(src, first, at):
        wide = src.shape[1]
        sem = sems.at[len(waits)]
        mine = (core == 0) == first

        @pl.when(mine)
        def _():
            pltpu.make_async_copy(src, keep.at[:, pl.ds(at, wide)], sem).start()

        @pl.when(jnp.logical_not(mine))
        def _():
            pltpu.make_async_copy(src, send.at[:, pl.ds(at, wide)], sem).start()

        waits.append(pltpu.make_async_copy(src, keep.at[:, pl.ds(at, wide)], sem))

    return hand_on


def forward_kernel(save, pick_ref, core_ref, x_ref, mask_ref, vec_ref, wa, wb, *rest):
    outs = []
    if save:
        y_ref, lse_ref, mid_ref, j_hbm, gp_hbm, keep, send = rest[:7]
        wv, wd, jn, ctx, act, gp, nrm, nt, sems, osems = rest[7:]
        hand_on = handing(core_ref[0], keep, send, osems, outs)
    else:
        y_ref = rest[0]
        wv, wd, jn, ctx, act, gp, nrm, nt, sems, osems = rest[1:]
    copies = start_weights(pick_ref[0], wa, wb, wv, wd, sems, range(12))

    def flush(src, dst):
        c = pltpu.make_async_copy(src, dst, osems.at[len(outs)])
        c.start()
        outs.append(c)

    x = x_ref[...].astype(F32)
    cent, inv = spread_of(x)
    nrm[...] = (cent * inv * vec_ref[AG:AG + 1, :] + vec_ref[AS:AS + 1, :]).astype(BF)
    if save:
        hand_on(nrm, True, D)
        hand_on(nrm, False, FF + D)
    for k in range(3):
        copies[k].wait()
        r = dot(nrm[...], square(wv[k]))
        if k == 0:
            r = r + vec_ref[BQ:BQ + 1, :]
        if k == 2:
            r = r + vec_ref[BV:BV + 1, :]
        jn[:, k * D:(k + 1) * D] = r.astype(BF)
    if save:
        flush(jn, j_hbm)
    usable = mask_ref[0:1, :] > 0.5
    lane = lax.broadcasted_iota(jnp.int32, (ROWS, PAIRED), 1)
    low = lane < PAIRED // 2

    def heads(i, lse):
        at = pl.multiple_of(i * PAIRED, PAIRED)
        q2 = jn[:, pl.ds(at, PAIRED)] * BF(0.125)
        k2 = jn[:, pl.ds(D + at, PAIRED)]
        v2 = jn[:, pl.ds(2 * D + at, PAIRED)]
        zero = jnp.zeros_like(q2)
        both = []
        for h in range(2):
            s = dot(jnp.where(low == (h == 0), q2, zero), k2, 1, 1)
            s = jnp.where(usable, s, -1e30)
            top = jnp.max(s, axis=-1, keepdims=True)
            e = jnp.exp(s - top)
            total = jnp.sum(e, axis=-1, keepdims=True)
            p = (e * (1.0 / total)).astype(BF)
            both.append(dot(p, v2))
            if save:
                lse = jnp.where(lane == 2 * i + h, top + jnp.log(total), lse)
        ctx[:, pl.ds(at, PAIRED)] = jnp.where(low, both[0], both[1]).astype(BF)
        return lse

    lse = lax.fori_loop(0, HEADS // 2, heads, jnp.zeros((ROWS, PAIRED), F32))
    if save:
        lse_ref[...] = lse
        hand_on(ctx, False, FF)
    copies[3].wait()
    middle = x_ref[...].astype(F32) + dot(ctx[...], square(wv[3])) + vec_ref[OB:OB + 1, :]
    if save:
        mid_ref[...] = middle
    cent, inv = spread_of(middle)
    nt[...] = (cent * inv * vec_ref[FG:FG + 1, :] + vec_ref[FS:FS + 1, :]).astype(BF)
    if save:
        hand_on(nt, True, 0)
    acc = middle + vec_ref[DB:DB + 1, :]
    for b in range(4):
        copies[4 + b].wait()
        h = dot(nt[...], square(wv[4 + b])) + vec_ref[UB + b:UB + b + 1, :]
        a, g = gelu_pair(h)
        act[:, b * D:(b + 1) * D] = a.astype(BF)
        if save:
            gp[:, b * D:(b + 1) * D] = g.astype(BF)
        copies[8 + b].wait()
        acc = acc + dot(act[:, b * D:(b + 1) * D], square(wd[b]))
    y_ref[...] = acc.astype(BF)
    if save:
        hand_on(act, False, 0)
        flush(gp, gp_hbm)
        for c in outs:
            c.wait()


def weight_scratch(shape):
    n, _, r, _ = shape
    per, q = (n // 4, 4) if n > 1 else (1, 1)
    return [pltpu.VMEM((8, n, r, D), BF), pltpu.VMEM((4, per, q, r, D), BF)]


ANYS = pl.BlockSpec(memory_space=pl.ANY)
VM = pl.BlockSpec(memory_space=pltpu.VMEM)
SM = pl.BlockSpec(memory_space=pltpu.SMEM)


def forward_layer(save, pick, core, x, mask, vec, wa, wb):
    def sd(cols, t=BF):
        return jax.ShapeDtypeStruct((ROWS, cols), t)

    shapes, specs = [sd(D)], [VM]
    if save:
        shapes += [sd(PAIRED, F32), sd(D, F32), sd(3 * D), sd(FF), sd(WIDE), sd(WIDE)]
        specs += [VM, VM] + [ANYS] * 4
    return pl.pallas_call(
        functools.partial(forward_kernel, save),
        out_shape=shapes,
        in_specs=[SM, SM, VM, VM, VM, ANYS, ANYS],
        out_specs=specs,
        scratch_shapes=weight_scratch(wa.shape) + [
            pltpu.VMEM((ROWS, 3 * D), BF), pltpu.VMEM((ROWS, D), BF), pltpu.VMEM((ROWS, FF), BF),
            pltpu.VMEM((ROWS, FF), BF), pltpu.VMEM((ROWS, D), BF), pltpu.VMEM((ROWS, D), BF),
            pltpu.SemaphoreType.DMA((12,)), pltpu.SemaphoreType.DMA((7,))],
        compiler_params=pltpu.CompilerParams(vmem_limit_bytes=VMEM_LIMIT),
        cost_estimate=pl.CostEstimate(flops=2 * ROWS * D * D * 13, bytes_accessed=24 * D * D + 2**22, transcendentals=0),
        name="forward_layer",
    )(pick, core, x, mask, vec, wa, wb)


def backward_kernel(save, pick_ref, core_ref, g_ref, x_ref, lse_ref, mid_ref, mask_ref, vec_ref, wa, wb,
                    j_hbm, gp_hbm, *rest):
    if save:
        ds_ref, gv_ref, keep_hbm, send_hbm = rest[:4]
        wv, wd, jn, gp, dh, dj, b1, sems, isems, osems = rest[4:]
    else:
        ds_ref = rest[0]
        wv, wd, jn, gp, dh, dj, b1, sems, isems, osems = rest[1:]
    gp_in = pltpu.make_async_copy(gp_hbm, gp, isems.at[0])
    gp_in.start()
    copies = start_weights(pick_ref[0], wa, wb, wv, wd, sems, (8, 4, 9, 5, 10, 6, 11, 7, 3, 0, 1, 2))
    j_in = pltpu.make_async_copy(j_hbm, jn, isems.at[1])
    j_in.start()
    waits = []
    hand_on = handing(core_ref[0], keep_hbm, send_hbm, osems, waits) if save else lambda *a: None
    hand_on(g_ref, False, 0)
    g = g_ref[...]
    d_nt = jnp.zeros((ROWS, D), F32)
    gp_in.wait()
    for b in range(4):
        copies[8 + b].wait()
        da = dot(g, square(wd[b]), 1, 1)
        cols = slice(b * D, (b + 1) * D)
        d = da * gp[:, cols].astype(F32)
        dh[:, cols] = d.astype(BF)
        if save:
            gv_ref[UB + b:UB + b + 1, :] = jnp.sum(dh[:, cols].astype(F32), axis=0, keepdims=True)
        copies[4 + b].wait()
        d_nt = d_nt + dot(dh[:, cols], square(wv[4 + b]), 1, 1)
    hand_on(dh, True, 0)

    def norm_back(v, dy, gain, row):
        cent, inv = spread_of(v)
        hat = cent * inv
        if save:
            gv_ref[row:row + 1, :] = jnp.sum(dy * hat, axis=0, keepdims=True)
            gv_ref[row + 1:row + 2, :] = jnp.sum(dy, axis=0, keepdims=True)
        t = dy * gain
        return inv * (t - jnp.mean(t, axis=-1, keepdims=True) - hat * jnp.mean(t * hat, axis=-1, keepdims=True))

    d_mid = g_ref[...].astype(F32) + norm_back(mid_ref[...], d_nt, vec_ref[FG:FG + 1, :], FG)
    b1[...] = d_mid.astype(BF)
    if save:
        gv_ref[DB:DB + 1, :] = jnp.sum(g_ref[...].astype(F32), axis=0, keepdims=True)
        gv_ref[OB:OB + 1, :] = jnp.sum(b1[...].astype(F32), axis=0, keepdims=True)
    hand_on(b1, False, D)
    copies[3].wait()
    dj[:, :D] = dot(b1[...], square(wv[3]), 1, 1).astype(BF)
    j_in.wait()
    usable = mask_ref[0:1, :] > 0.5
    lane = lax.broadcasted_iota(jnp.int32, (ROWS, PAIRED), 1)
    low = lane < PAIRED // 2

    def heads(i, carry):
        at = pl.multiple_of(i * PAIRED, PAIRED)
        q2 = jn[:, pl.ds(at, PAIRED)] * BF(0.125)
        k2 = jn[:, pl.ds(D + at, PAIRED)]
        v2 = jn[:, pl.ds(2 * D + at, PAIRED)]
        do2 = dj[:, pl.ds(at, PAIRED)]
        zero = jnp.zeros_like(q2)
        lse_all = lse_ref[...]
        res = []
        for h in range(2):
            here = low == (h == 0)
            lse = jnp.sum(jnp.where(lane == 2 * i + h, lse_all, 0.0), axis=-1, keepdims=True)
            s = dot(jnp.where(here, q2, zero), k2, 1, 1)
            p = jnp.where(usable, jnp.exp(s - lse), 0.0)
            dp = dot(jnp.where(here, do2, zero), v2, 1, 1)
            inner = jnp.sum(p * dp, axis=-1, keepdims=True)
            dsc = (p * (dp - inner)).astype(BF)
            res.append((dot(dsc, k2) * 0.125, dot(dsc, q2, 0, 0), dot(p.astype(BF), do2, 0, 0)))
        for c in range(3):
            dj[:, pl.ds(c * D + at, PAIRED)] = jnp.where(low, res[0][c], res[1][c]).astype(BF)
        return carry

    lax.fori_loop(0, HEADS // 2, heads, 0)
    hand_on(dj.at[:, pl.ds(0, 2 * D)], True, FF)
    hand_on(dj.at[:, pl.ds(2 * D, D)], False, 2 * D)
    if save:
        gv_ref[BQ:BQ + 1, :] = jnp.sum(dj[:, :D].astype(F32), axis=0, keepdims=True)
        gv_ref[BV:BV + 1, :] = jnp.sum(dj[:, 2 * D:].astype(F32), axis=0, keepdims=True)
        gv_ref[UB + 4:, :] = jnp.zeros((4, D), F32)
    d_n = jnp.zeros((ROWS, D), F32)
    for k in range(3):
        copies[k].wait()
        d_n = d_n + dot(dj[:, k * D:(k + 1) * D], square(wv[k]), 1, 1)
    ds_ref[...] = (d_mid + norm_back(x_ref[...].astype(F32), d_n, vec_ref[AG:AG + 1, :], AG)).astype(BF)
    for c in waits:
        c.wait()


def backward_layer(save, pick, core, g, x, mask, vec, wa, wb, saved):
    lse, mid, jn, gp = saved

    def sd(cols, t=BF, rows=ROWS):
        return jax.ShapeDtypeStruct((rows, cols), t)

    shapes, specs = [sd(D)], [VM]
    if save:
        shapes += [sd(D, F32, 16), sd(WIDE), sd(WIDE)]
        specs += [VM, ANYS, ANYS]
    return pl.pallas_call(
        functools.partial(backward_kernel, save),
        out_shape=shapes,
        in_specs=[SM, SM] + [VM] * 6 + [ANYS] * 4,
        out_specs=specs,
        scratch_shapes=weight_scratch(wa.shape) + [
            pltpu.VMEM((ROWS, 3 * D), BF), pltpu.VMEM((ROWS, FF), BF), pltpu.VMEM((ROWS, FF), BF),
            pltpu.VMEM((ROWS, 3 * D), BF), pltpu.VMEM((ROWS, D), BF),
            pltpu.SemaphoreType.DMA((12,)), pltpu.SemaphoreType.DMA((2,)), pltpu.SemaphoreType.DMA((5,))],
        compiler_params=pltpu.CompilerParams(vmem_limit_bytes=VMEM_LIMIT),
        cost_estimate=pl.CostEstimate(flops=2 * ROWS * D * D * 14, bytes_accessed=24 * D * D + 2**23, transcendentals=0),
        name="backward_layer",
    )(pick, core, g, x, lse, mid, mask, vec, wa, wb, jn, gp)


def product_kernel(core_ref, fk, bk, fr, br, out_ref):
    n, _, r, _ = out_ref.shape

    def both(a, b, at, wide=D):
        return jnp.concatenate([a[:, at:at + wide], b[:, at:at + wide]], axis=0)

    @pl.when(core_ref[0] == 0)
    def _():
        for c in range(HALF):
            left = both(fk, fr, 0 if c < 4 else D)
            out_ref[:, c] = dot(left, both(bk, br, c * D), 0, 0).astype(BF).reshape(n, r, D)

    @pl.when(core_ref[0] != 0)
    def _():
        for c in range(HALF):
            left = both(fk, fr, c * D)
            val = dot(left, both(bk, br, 0 if c < 4 else (c - 3) * D), 0, 0).astype(BF)
            if c < 4 and n > 1:
                out_ref[c * (n // 4):(c + 1) * (n // 4), 0:4] = val.reshape(n // 4, 4, r, D)
            else:
                out_ref[:, c] = val.reshape(n, r, D)


def weight_products(n, core, fk, bk, fr, br):
    return pl.pallas_call(
        product_kernel,
        out_shape=jax.ShapeDtypeStruct((n, HALF, D // n, D), BF),
        in_specs=[SM] + [VM] * 4,
        out_specs=VM,
        compiler_params=pltpu.CompilerParams(vmem_limit_bytes=VMEM_LIMIT),
        cost_estimate=pl.CostEstimate(flops=2 * 2 * ROWS * D * D * 6, bytes_accessed=2**24, transcendentals=0),
        name="weight_products",
    )(core, fk, bk, fr, br)


def moved(value, axis, by):
    peers = lax.axis_size(axis)
    return lax.ppermute(value, axis, [(i, i + by) for i in range(peers) if 0 <= i + by < peers])


def swapped(value):
    peers = lax.axis_size("section")
    return lax.ppermute(value, "section", [(i, i ^ 1) for i in range(peers)])


def pack_shard(joint, output, up, down):
    r = output.shape[0]
    pieces = [joint[:, k * D:(k + 1) * D] for k in range(3)] + [output]
    pieces += [up[:, k * D:(k + 1) * D] for k in range(4)]
    return jnp.concatenate([jnp.stack(pieces), down.reshape(4, r, D)]).astype(BF)


def kernel_form(n, g):
    r = D // n
    if r % 16 == 0:
        return g
    cut = jnp.swapaxes(g[:, :8], 0, 1).reshape(8, D, D)
    return jnp.concatenate([cut, g[:, 8:].reshape(4, D, D)])[None]


def vector_block(v, n):
    r = D // n
    parts = [v[:, 0:r], v[:, r:2 * r], v[:, 2 * r:4 * r], v[:, 4 * r:5 * r], v[:, 5 * r:6 * r], v[:, 6 * r:7 * r],
             v[:, 7 * r:8 * r], v[:, 8 * r:]]
    rows = jnp.concatenate([p.reshape(-1) for p in parts]).reshape(12, D)
    return jnp.concatenate([rows, jnp.zeros((4, D), v.dtype)]).astype(F32)


def vector_parts(rows, n):
    cuts = [rows[0:1], rows[1:2], rows[2:4], rows[4:5], rows[5:6], rows[6:7], rows[7:8], rows[8:12]]
    return jnp.concatenate([c.reshape(n, -1) for c in cuts], axis=1)


def shards(tokens, lengths, cotangent, attend_gain, attend_shift, joint_weight, joint_bias, output_weight,
           output_bias, feed_gain, feed_shift, up_weight, up_bias, down_weight, down_bias):
    n = lax.axis_size("dp")
    r = D // n
    nk = n if r % 16 == 0 else 1
    sections = lax.axis_size("section")
    stages = sections // 2
    index = lax.axis_index("section")
    core, stage = index % 2, index // 2
    seq = tokens.shape[1]
    coref = core.reshape(1)
    picks = [(core != s).astype(jnp.int32).reshape(1) for s in range(2)]

    packed = pack_shard(joint_weight[0], output_weight[0], up_weight[0], down_weight[0])
    small = jnp.concatenate([v[0] for v in (attend_gain, attend_shift, joint_bias, output_bias, feed_gain, feed_shift,
                                            down_bias, up_bias)]).astype(BF)
    small = lax.all_gather(small, "dp")
    mine = lax.all_gather(packed, "dp")
    small_other = swapped(small)
    vec_own, vec_oth = vector_block(small, n), vector_block(small_other, n)
    vecs = [jnp.where(core == s, vec_own, vec_oth) for s in range(2)]
    other = swapped(mine)
    wa, wb = kernel_form(n, mine), kernel_form(n, other)

    def own_pair(a):
        return lax.dynamic_index_in_dim(a, core, 0, False)

    def padded(a):
        return jnp.pad(a, ((0, ROWS - seq), (0, 0)))

    places = lax.broadcasted_iota(jnp.int32, (8, ROWS), 1)
    mask = (((places < own_pair(lengths)) | (places >= CAPTION)) & (places < seq)).astype(F32)
    own_tokens = padded(own_pair(tokens))
    own_cotangent = padded(own_pair(cotangent))

    x = own_tokens
    for t in range(stages):
        last = t == stages - 1
        start, saved = x, []
        for s in range(2):
            got = forward_layer(last, picks[s], coref, x, mask, vecs[s], wa, wb)
            saved.append((x,) + tuple(got[1:]))
            x = got[0]
        if not last:
            x = jnp.where(stage == 0, own_tokens, moved(x, "section", 2))
    leaving = x
    forward_got = [swapped(saved[s][6]) for s in range(2)]

    g = own_cotangent
    products, vec_grads = [None, None], [None, None]
    for t in range(stages):
        last = t == stages - 1
        for s in (1, 0):
            xin, lse, mid, jn, gp, fk, _ = saved[s]
            got = backward_layer(last, picks[s], coref, g, xin, mask, vecs[s], wa, wb, (lse, mid, jn, gp))
            g = got[0]
            if last:
                vec_grads[s] = got[1]
                products[s] = weight_products(nk, coref, fk, got[2], forward_got[s], swapped(got[3]))
        if not last:
            g = jnp.where(stage == stages - 1, own_cotangent, moved(g, "section", -2))

    reduced = [None, None]
    for s in (1, 0):
        p = products[s]
        if nk == 1:
            col = jnp.swapaxes(p[0].reshape(HALF, n, r, D), 0, 1)
            row = jnp.concatenate([jnp.swapaxes(p[0, :4].reshape(n, 4, r, D), 0, 0), col[:, 4:]], axis=1)
            p = jnp.where(core == 0, col, row)
        reduced[s] = lax.psum_scatter(p, "dp", scatter_dimension=0)
    keep = jnp.where(core == 0, reduced[0], reduced[1])
    away = swapped(jnp.where(core == 0, reduced[1], reduced[0]))
    first = jnp.where(core == 0, keep, away).astype(F32)
    second = jnp.where(core == 0, away, keep).astype(F32)
    grad_up = jnp.concatenate([first[k] for k in range(4)], axis=1)
    grad_joint = jnp.concatenate([first[4], first[5], second[5]], axis=1)
    grad_down = second[:4].reshape(4 * r, D)
    grad_out = second[4]

    vec_keep = jnp.where(core == 0, vec_grads[0], vec_grads[1])
    vec_send = jnp.where(core == 0, vec_grads[1], vec_grads[0])
    vec_sum = vec_keep + swapped(vec_send)
    v = lax.psum_scatter(vector_parts(vec_sum, n), "dp", scatter_dimension=0)

    ends = jnp.where(stage == 0, g, leaving)[:seq].reshape(seq, sections, D // sections)
    pieces = lax.all_to_all(ends, "section", split_axis=1, concat_axis=0, tiled=True).reshape(sections, seq, D // sections)
    outputs = pieces[sections - 2:]
    token_grad = pieces[:2]
    return (outputs, token_grad, v[None, 0:r], v[None, r:2 * r], grad_joint[None], v[None, 2 * r:4 * r], grad_out[None],
            v[None, 4 * r:5 * r], v[None, 5 * r:6 * r], v[None, 6 * r:7 * r], grad_up[None], v[None, 8 * r:],
            grad_down[None], v[None, 7 * r:8 * r])


def solution(mesh):
    vec, mat = P("section", "dp"), P("section", "dp", None)
    rows = P("dp", None, None)
    out = P("dp", None, "section")
    return jax.shard_map(
        shards,
        mesh=mesh,
        in_specs=(rows, P("dp"), rows, vec, vec, mat, vec, mat, vec, vec, vec, mat, vec, mat, vec),
        out_specs=(out, out, vec, vec, mat, vec, mat, vec, vec, vec, mat, vec, mat, vec),
        check_vma=False,
    )
```

```python
import functools

import jax
import jax.numpy as jnp
from jax import lax
from jax.experimental import pallas as pl
from jax.experimental.pallas import tpu as pltpu
from jax.sharding import PartitionSpec as P

D = 768
HEADS = 12
FF = 3072
CAPTION = 40
ROWS = 288
HALF = 6
TAIL = 16
EPS = 1e-6
BF = jnp.bfloat16
F32 = jnp.float32
PAIRED = 2 * (D // HEADS)
VMEM_LIMIT = 60 * 2**20
WIDE = FF + 2 * D
AG, AS, BQ, BV, OB, FG, FS, DB, UB = 0, 1, 2, 3, 4, 5, 6, 7, 8

ANYS = pl.BlockSpec(memory_space=pl.ANY)
VM = pl.BlockSpec(memory_space=pltpu.VMEM)
SM = pl.BlockSpec(memory_space=pltpu.SMEM)


def dot(a, b, ca=1, cb=0):
    return lax.dot_general(a, b, (((ca,), (cb,)), ((), ())), preferred_element_type=F32)


def spread_of(v):
    mean = jnp.mean(v, axis=-1, keepdims=True)
    cent = v - mean
    return cent, lax.rsqrt(jnp.mean(cent * cent, axis=-1, keepdims=True) + EPS)


def square(block):
    return block.reshape(D, D)


def weight_scratch(count):
    n, r, per = (8, D // 8, 2) if count > 1 else (1, D, 1)
    return [pltpu.VMEM((8, n, r, D), BF), pltpu.VMEM((4, per, D // per, D), BF), pltpu.VMEM((n, TAIL, D), BF),
            pltpu.SemaphoreType.DMA((13,))]


def start_weights(which, info, sets, scratch, order):
    wv, wd, tv, sems = scratch
    r = wv.shape[2]

    def start(block, j, part):
        if part == 12:
            pltpu.make_async_copy(block.at[pl.ds(12 * r, TAIL)], tv.at[j], sems.at[12]).start()
        elif part < 8:
            pltpu.make_async_copy(block.at[pl.ds(part * r, r)], wv.at[part, j], sems.at[part]).start()
        elif len(sets[0]) == 1:
            pltpu.make_async_copy(block.at[pl.ds(part * r, r)], wd.at[part - 8, 0], sems.at[part]).start()
        elif part == 8:
            b = j // 2
            pltpu.make_async_copy(block.at[pl.ds(8 * r, 4 * r)], wd.at[b, j % 2], sems.at[8 + b]).start()

    for number, blocks in enumerate(sets):
        if len(blocks) == 1:

            @pl.when(info[which] == number)
            def _():
                for part in order:
                    start(blocks[0], 0, part)

            continue
        for middle in (0, 1):

            @pl.when((info[which] == number) & (info[4] == middle))
            def _():
                held = [(0, 0), (1, 1), (2, 3), (4, 2)] if middle else [(0, 0), (1, 1), (3, 2), (5, 3)]
                spots = [(blocks[far * 6 + at], (info[2] ^ flip) * 2 + (info[3] ^ far)) for far in (0, 1) for at, flip in held]
                for part in order:
                    for block, j in spots:
                        start(block, j, part)

    waits = [pltpu.make_async_copy(wv.at[k], wv.at[k], sems.at[k]) for k in range(8)]
    waits += [pltpu.make_async_copy(wd.at[b], wd.at[b], sems.at[8 + b]) for b in range(4)]
    return waits + [pltpu.make_async_copy(tv, tv, sems.at[12])]


def vectors(tv):
    total = tv[0].astype(F32)
    for j in range(1, tv.shape[0]):
        total = total + tv[j].astype(F32)
    return total


def handing(core, keep, send, sems, waits):
    def hand_on(src, first, at):
        wide = src.shape[1]
        sem = sems.at[len(waits)]
        mine = (core == 0) == first

        @pl.when(mine)
        def _():
            pltpu.make_async_copy(src, keep.at[:, pl.ds(at, wide)], sem).start()

        @pl.when(jnp.logical_not(mine))
        def _():
            pltpu.make_async_copy(src, send.at[:, pl.ds(at, wide)], sem).start()

        waits.append(pltpu.make_async_copy(src, keep.at[:, pl.ds(at, wide)], sem))

    return hand_on


def forward_one(save, core, x, usable, copies, scratch, work, osems, saved, outs):
    wv, wd, tv, _ = scratch
    jn, ctx, act, gp, nrm, nt, vec = work
    if save:
        lse_ref, mid_ref, j_hbm, gp_hbm, keep, send = saved
        hand_on = handing(core, keep, send, osems, outs)

        def flush(src, dst):
            c = pltpu.make_async_copy(src, dst, osems.at[len(outs)])
            c.start()
            outs.append(c)

    copies[12].wait()
    vec[...] = vectors(tv)
    cent, inv = spread_of(x)
    nrm[...] = (cent * inv * vec[AG:AG + 1, :] + vec[AS:AS + 1, :]).astype(BF)
    if save:
        hand_on(nrm, True, D)
        hand_on(nrm, False, FF + D)
    for k in range(3):
        copies[k].wait()
        r = dot(nrm[...], square(wv[k]))
        if k == 0:
            r = r + vec[BQ:BQ + 1, :]
        if k == 2:
            r = r + vec[BV:BV + 1, :]
        jn[:, k * D:(k + 1) * D] = r.astype(BF)
    if save:
        flush(jn, j_hbm)
    lane = lax.broadcasted_iota(jnp.int32, (ROWS, PAIRED), 1)
    low = lane < PAIRED // 2
    lse = jnp.zeros((ROWS, PAIRED), F32)
    for i in range(HEADS // 2):
        at = i * PAIRED
        q2 = jn[:, at:at + PAIRED] * BF(0.125)
        k2 = jn[:, D + at:D + at + PAIRED]
        v2 = jn[:, 2 * D + at:2 * D + at + PAIRED]
        zero = jnp.zeros_like(q2)
        both = []
        for h in range(2):
            s = dot(jnp.where(low == (h == 0), q2, zero), k2, 1, 1)
            s = jnp.where(usable, s, -1e30)
            top = jnp.max(s, axis=-1, keepdims=True)
            e = jnp.exp(s - top)
            total = jnp.sum(e, axis=-1, keepdims=True)
            both.append(dot(e.astype(BF), v2) * (1.0 / total))
            if save:
                lse = jnp.where(lane == 2 * i + h, top + jnp.log(total), lse)
        ctx[:, at:at + PAIRED] = jnp.where(low, both[0], both[1]).astype(BF)
    if save:
        lse_ref[...] = lse
        hand_on(ctx, False, FF)
    for k in range(3, 12):
        copies[k].wait()
    middle = x + dot(ctx[...], square(wv[3])) + vec[OB:OB + 1, :]
    if save:
        mid_ref[...] = middle
    cent, inv = spread_of(middle)
    nt[...] = (cent * inv * vec[FG:FG + 1, :] + vec[FS:FS + 1, :]).astype(BF)
    if save:
        hand_on(nt, True, 0)
    acc = middle + vec[DB:DB + 1, :]
    for b in range(4):
        cols = slice(b * D, (b + 1) * D)
        h = dot(nt[...], square(wv[4 + b])) + vec[UB + b:UB + b + 1, :]
        phi = 0.5 + 0.5 * lax.erf(h * (0.5**0.5))
        a = (h * phi).astype(BF)
        if save:
            act[:, cols] = a
            gp[:, cols] = (phi + h * jnp.exp(-0.5 * h * h) * 0.3989422804014327).astype(BF)
        acc = acc + dot(a, square(wd[b]))
    if save:
        hand_on(act, False, 0)
        flush(gp, gp_hbm)
    return acc.astype(BF)


def forward_kernel(save, count, info, x_ref, mask_ref, *rest):
    sets, rest = (rest[:count], rest[count:2 * count]), rest[2 * count:]
    wide = 14 if save else 2
    results, rest = rest[:wide], rest[wide:]
    scratch = [rest[0:4], rest[4:8]]
    rest = rest[8:]
    copies = [start_weights(s, info, sets, scratch[s], (12,) + tuple(range(12))) for s in range(2)]
    usable = mask_ref[0:1, :] > 0.5
    outs = []
    x = x_ref[...]
    for s in range(2):
        work, rest = rest[:7], rest[7:]
        saved = results[2 + 6 * s:8 + 6 * s] if save else ()
        x = forward_one(save, info[5], x.astype(F32), usable, copies[s], scratch[s], work, rest[7 * (1 - s)], saved, outs)
        results[s][...] = x
    for c in outs:
        c.wait()


def forward_stage(save, info, x, mask, wa, wb):
    def sd(cols, t=BF):
        return jax.ShapeDtypeStruct((ROWS, cols), t)

    shapes, specs = [sd(D)] * 2, [VM] * 2
    if save:
        shapes += [sd(PAIRED, F32), sd(D, F32), sd(3 * D), sd(FF), sd(WIDE), sd(WIDE)] * 2
        specs += ([VM, VM] + [ANYS] * 4) * 2
    work = [pltpu.VMEM((ROWS, 3 * D), BF), pltpu.VMEM((ROWS, D), BF), pltpu.VMEM((ROWS, FF), BF),
            pltpu.VMEM((ROWS, FF), BF), pltpu.VMEM((ROWS, D), BF), pltpu.VMEM((ROWS, D), BF), pltpu.VMEM((16, D), F32)]
    return pl.pallas_call(
        functools.partial(forward_kernel, save, len(wa)),
        out_shape=shapes,
        in_specs=[SM, VM, VM] + [ANYS] * (2 * len(wa)),
        out_specs=specs,
        scratch_shapes=weight_scratch(len(wa)) * 2 + work * 2 + [pltpu.SemaphoreType.DMA((14,))],
        compiler_params=pltpu.CompilerParams(vmem_limit_bytes=VMEM_LIMIT),
        cost_estimate=pl.CostEstimate(flops=2 * ROWS * D * D * 26, bytes_accessed=48 * D * D + 2**23, transcendentals=0),
        name="forward_stage",
    )(info, x, mask, *wa, *wb)


def backward_one(save, core, g_ref, x_ref, lse_ref, mid_ref, j_hbm, gp_hbm, usable, copies, scratch, work, isems, osems, results,
                 waits):
    wv, wd, tv, _ = scratch
    jn, gp, dh, dj, b1, vec = work
    hand_on = lambda *a: None
    if save:
        gv_ref, keep_hbm, send_hbm = results
        hand_on = handing(core, keep_hbm, send_hbm, osems, waits)
    hand_on(g_ref, False, 0)
    copies[12].wait()
    vec[...] = vectors(tv)
    d_nt = None
    for b in range(4):
        cols = slice(b * D, (b + 1) * D)
        copies[8 + b].wait()
        if b == 0:
            pltpu.make_async_copy(gp_hbm, gp, isems.at[0]).wait()
        da = dot(g_ref[...], square(wd[b]), 1, 1)
        d = (da * gp[:, cols].astype(F32)).astype(BF)
        dh[:, cols] = d
        copies[4 + b].wait()
        part = dot(d, square(wv[4 + b]), 1, 1)
        d_nt = part if d_nt is None else d_nt + part
    hand_on(dh, True, 0)

    def norm_back(v, dy, gain, row):
        cent, inv = spread_of(v)
        hat = cent * inv
        if save:
            gv_ref[row:row + 1, :] = jnp.sum(dy * hat, axis=0, keepdims=True)
            gv_ref[row + 1:row + 2, :] = jnp.sum(dy, axis=0, keepdims=True)
        t = dy * gain
        return inv * (t - jnp.mean(t, axis=-1, keepdims=True) - hat * jnp.mean(t * hat, axis=-1, keepdims=True))

    d_mid = g_ref[...].astype(F32) + norm_back(mid_ref[...], d_nt, vec[FG:FG + 1, :], FG)
    b1[...] = d_mid.astype(BF)
    hand_on(b1, False, D)
    if save:
        for b in range(4):
            gv_ref[UB + b:UB + b + 1, :] = jnp.sum(dh[:, b * D:(b + 1) * D].astype(F32), axis=0, keepdims=True)
        gv_ref[DB:DB + 1, :] = jnp.sum(g_ref[...].astype(F32), axis=0, keepdims=True)
        gv_ref[OB:OB + 1, :] = jnp.sum(b1[...].astype(F32), axis=0, keepdims=True)
    copies[3].wait()
    d_ctx = dot(b1[...], square(wv[3]), 1, 1).astype(BF)
    pltpu.make_async_copy(j_hbm, jn, isems.at[1]).wait()
    for k in range(3):
        copies[k].wait()
    lane = lax.broadcasted_iota(jnp.int32, (ROWS, PAIRED), 1)
    low = lane < PAIRED // 2
    for i in range(HEADS // 2):
        at = i * PAIRED
        q2 = jn[:, at:at + PAIRED] * BF(0.125)
        k2 = jn[:, D + at:D + at + PAIRED]
        v2 = jn[:, 2 * D + at:2 * D + at + PAIRED]
        do2 = d_ctx[:, at:at + PAIRED]
        zero = jnp.zeros_like(q2)
        res = []
        for h in range(2):
            here = low == (h == 0)
            s = dot(jnp.where(here, q2, zero), k2, 1, 1)
            p = jnp.where(usable, jnp.exp(s - lse_ref[:, 2 * i + h:2 * i + h + 1]), 0.0)
            dp = dot(jnp.where(here, do2, zero), v2, 1, 1)
            inner = jnp.sum(p * dp, axis=-1, keepdims=True)
            dsc = (p * (dp - inner)).astype(BF)
            res.append((dot(dsc, k2) * 0.125, dot(dsc, q2, 0, 0), dot(p.astype(BF), do2, 0, 0)))
        for c in range(3):
            dj[:, c * D + at:c * D + at + PAIRED] = jnp.where(low, res[0][c], res[1][c]).astype(BF)
    hand_on(dj.at[:, pl.ds(0, 2 * D)], True, FF)
    hand_on(dj.at[:, pl.ds(2 * D, D)], False, 2 * D)
    if save:
        gv_ref[BQ:BQ + 1, :] = jnp.sum(dj[:, :D].astype(F32), axis=0, keepdims=True)
        gv_ref[BV:BV + 1, :] = jnp.sum(dj[:, 2 * D:].astype(F32), axis=0, keepdims=True)
        gv_ref[UB + 4:, :] = jnp.zeros((4, D), F32)
    d_n = dot(dj[:, :D], square(wv[0]), 1, 1)
    for k in (1, 2):
        d_n = d_n + dot(dj[:, k * D:(k + 1) * D], square(wv[k]), 1, 1)
    return (d_mid + norm_back(x_ref[...].astype(F32), d_n, vec[AG:AG + 1, :], AG)).astype(BF)


def backward_kernel(save, layers, count, info, g_ref, mask_ref, *rest):
    m = len(layers)
    kept, rest = [rest[5 * i:5 * i + 5] for i in range(m)], rest[5 * m:]
    rest = rest[1:] if save else rest
    sets, rest = (rest[:count], rest[count:2 * count]), rest[2 * count:]
    wide = 4 if save else 1
    results, rest = rest[:wide], rest[wide:]
    scratch, rest = [rest[4 * i:4 * i + 4] for i in range(m)], rest[4 * m:]
    work, (gs, isems, osems) = [rest[6 * i:6 * i + 6] for i in range(m)], rest[6 * m:]
    copies = []
    for i in range(m):
        pltpu.make_async_copy(kept[i][4], work[i][1], isems.at[i, 0]).start()
        copies.append(start_weights(layers[i], info, sets, scratch[i], (12, 8, 9, 10, 11, 4, 5, 6, 7, 3, 0, 1, 2)))
        pltpu.make_async_copy(kept[i][3], work[i][0], isems.at[i, 1]).start()
    usable = mask_ref[0:1, :] > 0.5
    waits = []
    for i in range(m):
        x_ref, lse_ref, mid_ref, j_hbm, gp_hbm = kept[i]
        g = backward_one(save, info[5], g_ref if i == 0 else gs, x_ref, lse_ref, mid_ref, j_hbm, gp_hbm, usable, copies[i],
                         scratch[i], work[i], isems.at[i], osems, results[1:], waits)
        if i + 1 < m:
            gs[...] = g
        else:
            results[0][...] = g
    for c in waits:
        c.wait()


def backward_layers(save, layers, info, g, mask, saved, wa, wb, behind):
    def sd(cols, t=BF, rows=ROWS):
        return jax.ShapeDtypeStruct((rows, cols), t)

    shapes, specs = [sd(D)], [VM]
    if save:
        shapes += [sd(D, F32, 16), sd(WIDE), sd(WIDE)]
        specs += [VM, ANYS, ANYS]
    m = len(layers)
    work = [pltpu.VMEM((ROWS, 3 * D), BF), pltpu.VMEM((ROWS, FF), BF), pltpu.VMEM((ROWS, FF), BF),
            pltpu.VMEM((ROWS, 3 * D), BF), pltpu.VMEM((ROWS, D), BF), pltpu.VMEM((16, D), F32)]
    kept = [a for s in layers for a in saved[s]]
    return pl.pallas_call(
        functools.partial(backward_kernel, save, layers, len(wa)),
        out_shape=shapes,
        in_specs=[SM, VM, VM] + [VM, VM, VM, ANYS, ANYS] * m + [ANYS] * (save + 2 * len(wa)),
        out_specs=specs,
        scratch_shapes=weight_scratch(len(wa)) * m + work * m + [
            pltpu.VMEM((ROWS, D), BF), pltpu.SemaphoreType.DMA((m, 2)), pltpu.SemaphoreType.DMA((5,))],
        compiler_params=pltpu.CompilerParams(vmem_limit_bytes=VMEM_LIMIT),
        cost_estimate=pl.CostEstimate(flops=2 * ROWS * D * D * 14 * m, bytes_accessed=m * (24 * D * D + 2**23), transcendentals=0),
        name="backward_layers",
    )(info, g, mask, *kept, *([behind] if save else []), *wa, *wb)


def product_kernel(n, info, slots, gv, fk, bk, fr, br, *rest):
    outs, (held, sems) = rest[:-2], rest[-2:]
    r = D // n

    def both(a, b, at):
        return jnp.concatenate([a[:, at:at + D], b[:, at:at + D]], axis=0)

    for j in range(n):
        held[j, HALF * r:] = gv[...].astype(BF)

    @pl.when(info[5] == 0)
    def _():
        for c in range(HALF):
            val = dot(both(fk, fr, 0 if c < 4 else D), both(bk, br, c * D), 0, 0).astype(BF)
            for j in range(n):
                held[slots[j], c * r:(c + 1) * r] = val[j * r:(j + 1) * r]

    @pl.when(info[5] != 0)
    def _():
        for c in range(HALF):
            val = dot(both(fk, fr, c * D), both(bk, br, 0 if c < 4 else (c - 3) * D), 0, 0).astype(BF)
            if c < 4 and n > 1:
                for i in range(n // 4):
                    held[slots[c * (n // 4) + i], :4 * r] = val[i * 4 * r:(i + 1) * 4 * r]
            else:
                for j in range(n):
                    held[slots[j], c * r:(c + 1) * r] = val[j * r:(j + 1) * r]

    for j in range(n):
        pltpu.make_async_copy(held.at[j], outs[j], sems.at[j]).start()
    for j in range(n):
        pltpu.make_async_copy(held.at[j], outs[j], sems.at[j]).wait()


def weight_products(n, info, slots, gv, fk, bk, fr, br):
    shape = (HALF * (D // n) + TAIL, D)
    return pl.pallas_call(
        functools.partial(product_kernel, n),
        out_shape=[jax.ShapeDtypeStruct(shape, BF)] * n,
        in_specs=[SM, SM] + [VM] * 5,
        out_specs=[ANYS] * n,
        scratch_shapes=[pltpu.VMEM((n,) + shape, BF), pltpu.SemaphoreType.DMA((n,))],
        compiler_params=pltpu.CompilerParams(vmem_limit_bytes=VMEM_LIMIT),
        cost_estimate=pl.CostEstimate(flops=2 * 2 * ROWS * D * D * 6, bytes_accessed=2**24, transcendentals=0),
        name="weight_products",
    )(info, slots, gv, fk, bk, fr, br)


def moved(value, axis, by):
    peers = lax.axis_size(axis)
    return lax.ppermute(value, axis, [(i, i + by) for i in range(peers) if 0 <= i + by < peers])


def swapped(value):
    peers = lax.axis_size("section")
    return lax.ppermute(value, "section", [(i, i ^ 1) for i in range(peers)])


def vector_tail(n, spot, attend_gain, attend_shift, joint_bias, output_bias, feed_gain, feed_shift, down_bias, up_bias):
    lane = jnp.arange(D)

    def row(v, times, at, live=True):
        return jnp.where((lane // v.shape[0] == at) & live, jnp.tile(v, times), 0.0)

    half, quarter = n // 2, n // 4
    rows = [row(attend_gain, n, spot), row(attend_shift, n, spot)]
    rows += [row(joint_bias, half, spot % half, spot // half == k) for k in range(2)]
    rows += [row(v, n, spot) for v in (output_bias, feed_gain, feed_shift, down_bias)]
    rows += [row(up_bias, quarter, spot % quarter, spot // quarter == k) for k in range(4)]
    return jnp.concatenate([jnp.stack(rows), jnp.zeros((4, D), F32)])


def pack_shard(joint, output, up, down, tail):
    pieces = [joint[:, k * D:(k + 1) * D] for k in range(3)] + [output]
    pieces += [up[:, k * D:(k + 1) * D] for k in range(4)]
    return jnp.concatenate(pieces + [down, tail]).astype(BF)


def kernel_form(n, g, tail):
    r = D // n
    cut = jnp.swapaxes(g[:, :8 * r].reshape(n, 8, r, D), 0, 1).reshape(8 * D, D)
    return [jnp.concatenate([cut, g[:, 8 * r:12 * r].reshape(FF, D), tail.astype(BF)])]


IN, OUT, MID, PAIR = ((0, 1), (3, 2)), ((1, 0), (2, 3)), ((1, 2), (2, 1)), ((0, 1), (1, 0), (2, 3), (3, 2))
ENDS, MIDS = (0, 3), (1, 2)


def along(value, moves):
    return lax.ppermute(value, "dp", [(2 * a + x, 2 * b + x) for a, b in moves for x in range(2)])


def across(value, lines=(0, 1, 2, 3)):
    return lax.ppermute(value, "dp", [(2 * z + x, 2 * z + 1 - x) for z in lines for x in range(2)])


def core_swap(value, lines=(0, 1, 2, 3)):
    n, peers = lax.axis_size("dp"), lax.axis_size("section")
    pairs = [(s * n + 2 * z + x, (s ^ 1) * n + 2 * z + x) for s in range(peers) for z in lines for x in range(2)]
    return lax.ppermute(value, ("section", "dp"), pairs)


def gather_blocks(own):
    one = along(own, PAIR)
    mid = along(own, MID)
    far = along(mid, OUT)
    back = along(one, MID)
    last = along(back, OUT)
    column = [own, one, mid, far, back, last]
    lines = [(0, 1, 2, 3), (0, 1, 2, 3), MIDS, ENDS, MIDS, ENDS]
    mine = column + [across(b, l) for b, l in zip(column, lines)]
    return mine, [core_swap(b, l) for b, l in zip(mine, lines * 2)]


def add(*terms):
    total = terms[0].astype(F32)
    for t in terms[1:]:
        total = total + t.astype(F32)
    return total.astype(BF)


def scatter_blocks(blocks):
    s = [add(blocks[k], across(blocks[4 + k])) for k in range(4)]
    a1 = along(s[0], IN)
    a2 = along(s[1], IN)
    b2 = along(add(s[0], a1), MID)
    a3 = along(s[2], IN)
    b3 = along(add(s[1], a2), MID)
    c3 = along(add(s[2], b2), OUT)
    return add(s[3], a3, b3, c3)


def shards(tokens, lengths, cotangent, attend_gain, attend_shift, joint_weight, joint_bias, output_weight,
           output_bias, feed_gain, feed_shift, up_weight, up_bias, down_weight, down_bias):
    n = lax.axis_size("dp")
    r = D // n
    lined = n == 8
    nk = n if lined else 1
    sections = lax.axis_size("section")
    stages = sections // 2
    index = lax.axis_index("section")
    core, stage = index % 2, index // 2
    seq = tokens.shape[1]
    spot = lax.axis_index("dp")
    z, column = spot // 2, spot % 2
    middle = (z == 1) | (z == 2)
    info = jnp.stack([core, 1 - core, z, column, middle.astype(jnp.int32), core]).astype(jnp.int32)
    if lined:
        order = jnp.array([[3, 2, 1, 0], [2, 3, 1, 0], [0, 1, 3, 2], [0, 1, 2, 3]], jnp.int32)[z]
        slots = jnp.stack([order[j // 2] + jnp.where(column == j % 2, 0, 4) for j in range(8)]).astype(jnp.int32)
    else:
        slots = jnp.zeros((1,), jnp.int32)

    tail = vector_tail(n, spot, attend_gain[0], attend_shift[0], joint_bias[0], output_bias[0], feed_gain[0], feed_shift[0],
                       down_bias[0], up_bias[0])
    packed = pack_shard(joint_weight[0], output_weight[0], up_weight[0], down_weight[0], tail)
    if lined:
        wa, wb = gather_blocks(packed)
    else:
        gathered = lax.all_gather(packed, "dp")
        tails = lax.psum(tail.astype(BF).astype(F32), "dp")
        wa, wb = kernel_form(n, gathered, tails), kernel_form(n, swapped(gathered), swapped(tails))

    def own_pair(a):
        return lax.dynamic_index_in_dim(a, core, 0, False)

    def padded(a):
        return jnp.pad(a, ((0, ROWS - seq), (0, 0)))

    places = lax.broadcasted_iota(jnp.int32, (8, ROWS), 1)
    mask = (((places < own_pair(lengths)) | (places >= CAPTION)) & (places < seq)).astype(F32)
    own_tokens = padded(own_pair(tokens))
    own_cotangent = padded(own_pair(cotangent))

    x = own_tokens
    for t in range(stages):
        last = t == stages - 1
        got = forward_stage(last, info, x, mask, wa, wb)
        if not last:
            x = jnp.where(stage == 0, own_tokens, moved(got[1], "section", 2))
    leaving = got[1]
    saved = [(x, *got[2:6]), (got[0], *got[8:12])]
    kept = [got[6], got[12]]
    received = [swapped(got[7]), swapped(got[13])]

    g = own_cotangent
    for t in range(stages - 1):
        g = backward_layers(False, (1, 0), info, g, mask, saved, wa, wb, None)[0]
        g = jnp.where(stage == stages - 1, own_cotangent, moved(g, "section", -2))
    products = [None, None]
    behind = mask
    for s in (1, 0):
        g, gv, bk, bs = backward_layers(True, (s,), info, g, mask, saved, wa, wb, behind)
        products[s] = weight_products(nk, info, slots, gv, kept[s], bk, received[s], swapped(bs))
        behind = products[s][0]

    ends = jnp.where(stage == 0, g, leaving)[:seq].reshape(seq, sections, D // sections)
    pieces = lax.all_to_all(ends, "section", split_axis=1, concat_axis=0, tiled=True).reshape(sections, seq, D // sections)
    outputs = pieces[sections - 2:]
    token_grad = pieces[:2]

    reduced = [None, None]
    for s in (1, 0):
        if lined:
            reduced[s] = scatter_blocks(products[s])
        else:
            p = products[s][0]
            col = jnp.swapaxes(p[:HALF * D].reshape(HALF, n, r, D), 0, 1).reshape(n, HALF * r, D)
            row = jnp.concatenate([p[:4 * D].reshape(n, 4 * r, D), col[:, 4 * r:]], axis=1)
            total = lax.psum_scatter(jnp.where(core == 0, col, row), "dp", scatter_dimension=0)
            reduced[s] = jnp.concatenate([total, lax.psum(p[HALF * D:], "dp")])
    sent = [lax.ppermute(reduced[s], "section", [(i, i ^ 1) for i in range(sections) if i % 2 != s]) for s in range(2)]
    keep = jnp.where(core == 0, reduced[0], reduced[1])
    away = jnp.where(core == 0, sent[0], sent[1])
    first = jnp.where(core == 0, keep, away).astype(F32)
    second = jnp.where(core == 0, away, keep).astype(F32)
    grad_up = jnp.concatenate([first[k * r:(k + 1) * r] for k in range(4)], axis=1)
    grad_joint = jnp.concatenate([first[4 * r:5 * r], first[5 * r:6 * r], second[5 * r:6 * r]], axis=1)
    grad_down = second[:4 * r]
    grad_out = second[4 * r:5 * r]
    v = first[6 * r:] + second[6 * r:]
    half, quarter = n // 2, n // 4
    vec = lax.dynamic_slice(v, (0, r * spot), (16, r))
    grad_jb = lax.dynamic_slice(v, (BQ + spot // half, 2 * r * (spot % half)), (1, 2 * r))
    grad_ub = lax.dynamic_slice(v, (UB + spot // quarter, 4 * r * (spot % quarter)), (1, 4 * r))
    return (outputs, token_grad, vec[AG:AG + 1], vec[AS:AS + 1], grad_joint[None], grad_jb, grad_out[None],
            vec[OB:OB + 1], vec[FG:FG + 1], vec[FS:FS + 1], grad_up[None], grad_ub, grad_down[None], vec[DB:DB + 1])


def solution(mesh):
    vec, mat = P("section", "dp"), P("section", "dp", None)
    rows = P("dp", None, None)
    out = P("dp", None, "section")
    return jax.shard_map(
        shards,
        mesh=mesh,
        in_specs=(rows, P("dp"), rows, vec, vec, mat, vec, mat, vec, vec, vec, mat, vec, mat, vec),
        out_specs=(out, out, vec, vec, mat, vec, mat, vec, vec, vec, mat, vec, mat, vec),
        check_vma=False,
    )
```

```python
import functools

import jax
import jax.numpy as jnp
from jax import lax
from jax.experimental import pallas as pl
from jax.experimental.pallas import tpu as pltpu
from jax.sharding import PartitionSpec as P

D = 768
HEADS = 12
FF = 3072
CAPTION = 40
ROWS = 288
HALF = 6
TAIL = 16
EPS = 1e-6
BF = jnp.bfloat16
F32 = jnp.float32
PAIRED = 2 * (D // HEADS)
VMEM_LIMIT = 60 * 2**20
WIDE = FF + 2 * D
AG, AS, BQ, BV, OB, FG, FS, DB, UB = 0, 1, 2, 3, 4, 5, 6, 7, 8

ANYS = pl.BlockSpec(memory_space=pl.ANY)
VM = pl.BlockSpec(memory_space=pltpu.VMEM)
SM = pl.BlockSpec(memory_space=pltpu.SMEM)


def dot(a, b, ca=1, cb=0):
    return lax.dot_general(a, b, (((ca,), (cb,)), ((), ())), preferred_element_type=F32)


def spread_of(v):
    mean = jnp.mean(v, axis=-1, keepdims=True)
    cent = v - mean
    return cent, lax.rsqrt(jnp.mean(cent * cent, axis=-1, keepdims=True) + EPS)


def square(block):
    return block.reshape(D, D)


def weight_scratch(count):
    n, r, per = (8, D // 8, 2) if count > 1 else (1, D, 1)
    return [pltpu.VMEM((8, n, r, D), BF), pltpu.VMEM((4, per, D // per, D), BF), pltpu.VMEM((n, TAIL, D), BF),
            pltpu.SemaphoreType.DMA((13,))]


def start_weights(which, info, sets, scratch, order):
    wv, wd, tv, sems = scratch
    r = wv.shape[2]

    def start(block, j, part):
        if len(sets[0]) == 1:
            rows = block.at[pl.ds(part * r, r if part < 12 else TAIL)]
            dst = wv.at[part, 0] if part < 8 else wd.at[part - 8, 0] if part < 12 else tv.at[0]
            pltpu.make_async_copy(rows, dst, sems.at[part]).start()
        elif part == 12:
            pltpu.make_async_copy(block.at[pl.ds(10 * r, TAIL)], tv.at[j], sems.at[12]).start()
        elif part < 6:
            pltpu.make_async_copy(block.at[pl.ds(part * r, r)], wv.at[part, j], sems.at[part]).start()
        elif part == 8:
            b = j // 2
            pltpu.make_async_copy(block.at[pl.ds(6 * r, 4 * r)], wd.at[b, j % 2], sems.at[8 + b]).start()

    for number, blocks in enumerate(sets):

        @pl.when(info[which] == number)
        def _():
            if len(blocks) == 1:
                for part in order:
                    start(blocks[0], 0, part)
                return
            lines = [info[2], info[2] ^ 1, info[2] ^ info[6], info[2] ^ (info[6] ^ 1)]
            spots = [(blocks[4 * far + k], lines[k] * 2 + (info[3] ^ far)) for far in (0, 1) for k in range(4)]
            for part in order:
                if part in (6, 7):
                    for far in (0, 1):
                        for k in range(4):
                            rows = blocks[8 + k].at[pl.ds((2 * far + part - 6) * r, r)]
                            pltpu.make_async_copy(rows, wv.at[part, lines[k] * 2 + (info[3] ^ far)], sems.at[part]).start()
                    continue
                for block, j in spots:
                    start(block, j, part)

    waits = [pltpu.make_async_copy(wv.at[k], wv.at[k], sems.at[k]) for k in range(8)]
    waits += [pltpu.make_async_copy(wd.at[b], wd.at[b], sems.at[8 + b]) for b in range(4)]
    return waits + [pltpu.make_async_copy(tv, tv, sems.at[12])]


def vectors(tv):
    total = tv[0].astype(F32)
    for j in range(1, tv.shape[0]):
        total = total + tv[j].astype(F32)
    return total


def handing(core, keep, send, sems, waits):
    def hand_on(src, first, at):
        wide = src.shape[1]
        sem = sems.at[len(waits)]
        mine = (core == 0) == first

        @pl.when(mine)
        def _():
            pltpu.make_async_copy(src, keep.at[:, pl.ds(at, wide)], sem).start()

        @pl.when(jnp.logical_not(mine))
        def _():
            pltpu.make_async_copy(src, send.at[:, pl.ds(at, wide)], sem).start()

        waits.append(pltpu.make_async_copy(src, keep.at[:, pl.ds(at, wide)], sem))

    return hand_on


def forward_one(save, core, x, usable, copies, scratch, work, osems, saved, outs):
    wv, wd, tv, _ = scratch
    jn, ctx, act, gp, nrm, nt, vec = work
    if save:
        lse_ref, mid_ref, j_hbm, gp_hbm, keep, send = saved
        hand_on = handing(core, keep, send, osems, outs)

        def flush(src, dst):
            c = pltpu.make_async_copy(src, dst, osems.at[len(outs)])
            c.start()
            outs.append(c)

    copies[12].wait()
    vec[...] = vectors(tv)
    cent, inv = spread_of(x)
    nrm[...] = (cent * inv * vec[AG:AG + 1, :] + vec[AS:AS + 1, :]).astype(BF)
    if save:
        hand_on(nrm, True, D)
        hand_on(nrm, False, FF + D)
    for k in range(3):
        copies[k].wait()
        r = dot(nrm[...], square(wv[k]))
        if k == 0:
            r = r + vec[BQ:BQ + 1, :]
        if k == 2:
            r = r + vec[BV:BV + 1, :]
        jn[:, k * D:(k + 1) * D] = r.astype(BF)
    if save:
        flush(jn, j_hbm)
    lane = lax.broadcasted_iota(jnp.int32, (ROWS, PAIRED), 1)
    low = lane < PAIRED // 2
    lse = jnp.zeros((ROWS, PAIRED), F32)
    for i in range(HEADS // 2):
        at = i * PAIRED
        q2 = jn[:, at:at + PAIRED] * BF(0.125)
        k2 = jn[:, D + at:D + at + PAIRED]
        v2 = jn[:, 2 * D + at:2 * D + at + PAIRED]
        zero = jnp.zeros_like(q2)
        both = []
        for h in range(2):
            s = dot(jnp.where(low == (h == 0), q2, zero), k2, 1, 1)
            s = jnp.where(usable, s, -1e30)
            top = jnp.max(s, axis=-1, keepdims=True)
            e = jnp.exp(s - top)
            total = jnp.sum(e, axis=-1, keepdims=True)
            both.append(dot(e.astype(BF), v2) * (1.0 / total))
            if save:
                lse = jnp.where(lane == 2 * i + h, top + jnp.log(total), lse)
        ctx[:, at:at + PAIRED] = jnp.where(low, both[0], both[1]).astype(BF)
    if save:
        lse_ref[...] = lse
        hand_on(ctx, False, FF)
    for k in range(3, 12):
        copies[k].wait()
    middle = x + dot(ctx[...], square(wv[3])) + vec[OB:OB + 1, :]
    if save:
        mid_ref[...] = middle
    cent, inv = spread_of(middle)
    nt[...] = (cent * inv * vec[FG:FG + 1, :] + vec[FS:FS + 1, :]).astype(BF)
    if save:
        hand_on(nt, True, 0)
    acc = middle + vec[DB:DB + 1, :]
    for b in range(4):
        cols = slice(b * D, (b + 1) * D)
        h = dot(nt[...], square(wv[4 + b])) + vec[UB + b:UB + b + 1, :]
        phi = 0.5 + 0.5 * lax.erf(h * (0.5**0.5))
        a = (h * phi).astype(BF)
        if save:
            act[:, cols] = a
            gp[:, cols] = (phi + h * jnp.exp(-0.5 * h * h) * 0.3989422804014327).astype(BF)
        acc = acc + dot(a, square(wd[b]))
    if save:
        hand_on(act, False, 0)
        flush(gp, gp_hbm)
    return acc.astype(BF)


def forward_kernel(save, count, info, x_ref, mask_ref, *rest):
    sets, rest = (rest[:count], rest[count:2 * count]), rest[2 * count:]
    wide = 14 if save else 2
    results, rest = rest[:wide], rest[wide:]
    scratch = [rest[0:4], rest[4:8]]
    rest = rest[8:]
    copies = [start_weights(s, info, sets, scratch[s], (12,) + tuple(range(12))) for s in range(2)]
    usable = mask_ref[0:1, :] > 0.5
    outs = []
    x = x_ref[...]
    for s in range(2):
        work, rest = rest[:7], rest[7:]
        saved = results[2 + 6 * s:8 + 6 * s] if save else ()
        x = forward_one(save, info[5], x.astype(F32), usable, copies[s], scratch[s], work, rest[7 * (1 - s)], saved, outs)
        results[s][...] = x
    for c in outs:
        c.wait()


def forward_stage(save, info, x, mask, wa, wb):
    def sd(cols, t=BF):
        return jax.ShapeDtypeStruct((ROWS, cols), t)

    shapes, specs = [sd(D)] * 2, [VM] * 2
    if save:
        shapes += [sd(PAIRED, F32), sd(D, F32), sd(3 * D), sd(FF), sd(WIDE), sd(WIDE)] * 2
        specs += ([VM, VM] + [ANYS] * 4) * 2
    work = [pltpu.VMEM((ROWS, 3 * D), BF), pltpu.VMEM((ROWS, D), BF), pltpu.VMEM((ROWS, FF), BF),
            pltpu.VMEM((ROWS, FF), BF), pltpu.VMEM((ROWS, D), BF), pltpu.VMEM((ROWS, D), BF), pltpu.VMEM((16, D), F32)]
    return pl.pallas_call(
        functools.partial(forward_kernel, save, len(wa)),
        out_shape=shapes,
        in_specs=[SM, VM, VM] + [ANYS] * (2 * len(wa)),
        out_specs=specs,
        scratch_shapes=weight_scratch(len(wa)) * 2 + work * 2 + [pltpu.SemaphoreType.DMA((14,))],
        compiler_params=pltpu.CompilerParams(vmem_limit_bytes=VMEM_LIMIT),
        cost_estimate=pl.CostEstimate(flops=2 * ROWS * D * D * 26, bytes_accessed=48 * D * D + 2**23, transcendentals=0),
        name="forward_stage",
    )(info, x, mask, *wa, *wb)


def backward_one(save, core, g_ref, x_ref, lse_ref, mid_ref, j_hbm, gp_hbm, usable, copies, scratch, work, isems, osems, results,
                 waits):
    wv, wd, tv, _ = scratch
    jn, gp, dh, dj, b1, vec = work
    hand_on = lambda *a: None
    if save:
        gv_ref, keep_hbm, send_hbm = results
        hand_on = handing(core, keep_hbm, send_hbm, osems, waits)
    hand_on(g_ref, False, 0)
    copies[12].wait()
    vec[...] = vectors(tv)
    d_nt = None
    for b in range(4):
        cols = slice(b * D, (b + 1) * D)
        copies[8 + b].wait()
        if b == 0:
            pltpu.make_async_copy(gp_hbm, gp, isems.at[0]).wait()
        da = dot(g_ref[...], square(wd[b]), 1, 1)
        d = (da * gp[:, cols].astype(F32)).astype(BF)
        dh[:, cols] = d
        copies[4 + b].wait()
        part = dot(d, square(wv[4 + b]), 1, 1)
        d_nt = part if d_nt is None else d_nt + part
    hand_on(dh, True, 0)

    def norm_back(v, dy, gain, row):
        cent, inv = spread_of(v)
        hat = cent * inv
        if save:
            gv_ref[row:row + 1, :] = jnp.sum(dy * hat, axis=0, keepdims=True)
            gv_ref[row + 1:row + 2, :] = jnp.sum(dy, axis=0, keepdims=True)
        t = dy * gain
        return inv * (t - jnp.mean(t, axis=-1, keepdims=True) - hat * jnp.mean(t * hat, axis=-1, keepdims=True))

    d_mid = g_ref[...].astype(F32) + norm_back(mid_ref[...], d_nt, vec[FG:FG + 1, :], FG)
    b1[...] = d_mid.astype(BF)
    hand_on(b1, False, D)
    if save:
        for b in range(4):
            gv_ref[UB + b:UB + b + 1, :] = jnp.sum(dh[:, b * D:(b + 1) * D].astype(F32), axis=0, keepdims=True)
        gv_ref[DB:DB + 1, :] = jnp.sum(g_ref[...].astype(F32), axis=0, keepdims=True)
        gv_ref[OB:OB + 1, :] = jnp.sum(b1[...].astype(F32), axis=0, keepdims=True)
    copies[3].wait()
    d_ctx = dot(b1[...], square(wv[3]), 1, 1).astype(BF)
    pltpu.make_async_copy(j_hbm, jn, isems.at[1]).wait()
    for k in range(3):
        copies[k].wait()
    lane = lax.broadcasted_iota(jnp.int32, (ROWS, PAIRED), 1)
    low = lane < PAIRED // 2
    for i in range(HEADS // 2):
        at = i * PAIRED
        q2 = jn[:, at:at + PAIRED] * BF(0.125)
        k2 = jn[:, D + at:D + at + PAIRED]
        v2 = jn[:, 2 * D + at:2 * D + at + PAIRED]
        do2 = d_ctx[:, at:at + PAIRED]
        zero = jnp.zeros_like(q2)
        res = []
        for h in range(2):
            here = low == (h == 0)
            s = dot(jnp.where(here, q2, zero), k2, 1, 1)
            p = jnp.where(usable, jnp.exp(s - lse_ref[:, 2 * i + h:2 * i + h + 1]), 0.0)
            dp = dot(jnp.where(here, do2, zero), v2, 1, 1)
            inner = jnp.sum(p * dp, axis=-1, keepdims=True)
            dsc = (p * (dp - inner)).astype(BF)
            res.append((dot(dsc, k2) * 0.125, dot(dsc, q2, 0, 0), dot(p.astype(BF), do2, 0, 0)))
        for c in range(3):
            dj[:, c * D + at:c * D + at + PAIRED] = jnp.where(low, res[0][c], res[1][c]).astype(BF)
    hand_on(dj.at[:, pl.ds(0, 2 * D)], True, FF)
    hand_on(dj.at[:, pl.ds(2 * D, D)], False, 2 * D)
    if save:
        gv_ref[BQ:BQ + 1, :] = jnp.sum(dj[:, :D].astype(F32), axis=0, keepdims=True)
        gv_ref[BV:BV + 1, :] = jnp.sum(dj[:, 2 * D:].astype(F32), axis=0, keepdims=True)
        gv_ref[UB + 4:, :] = jnp.zeros((4, D), F32)
    d_n = dot(dj[:, :D], square(wv[0]), 1, 1)
    for k in (1, 2):
        d_n = d_n + dot(dj[:, k * D:(k + 1) * D], square(wv[k]), 1, 1)
    return (d_mid + norm_back(x_ref[...].astype(F32), d_n, vec[AG:AG + 1, :], AG)).astype(BF)


def backward_kernel(save, layers, count, info, g_ref, mask_ref, *rest):
    m = len(layers)
    kept, rest = [rest[5 * i:5 * i + 5] for i in range(m)], rest[5 * m:]
    rest = rest[1:] if save else rest
    sets, rest = (rest[:count], rest[count:2 * count]), rest[2 * count:]
    wide = 4 if save else 1
    results, rest = rest[:wide], rest[wide:]
    scratch, rest = [rest[4 * i:4 * i + 4] for i in range(m)], rest[4 * m:]
    work, (gs, isems, osems) = [rest[6 * i:6 * i + 6] for i in range(m)], rest[6 * m:]
    copies = []
    for i in range(m):
        pltpu.make_async_copy(kept[i][4], work[i][1], isems.at[i, 0]).start()
        copies.append(start_weights(layers[i], info, sets, scratch[i], (12, 8, 9, 10, 11, 4, 5, 6, 7, 3, 0, 1, 2)))
        pltpu.make_async_copy(kept[i][3], work[i][0], isems.at[i, 1]).start()
    usable = mask_ref[0:1, :] > 0.5
    waits = []
    for i in range(m):
        x_ref, lse_ref, mid_ref, j_hbm, gp_hbm = kept[i]
        g = backward_one(save, info[5], g_ref if i == 0 else gs, x_ref, lse_ref, mid_ref, j_hbm, gp_hbm, usable, copies[i],
                         scratch[i], work[i], isems.at[i], osems, results[1:], waits)
        if i + 1 < m:
            gs[...] = g
        else:
            results[0][...] = g
    for c in waits:
        c.wait()


def backward_layers(save, layers, info, g, mask, saved, wa, wb, behind):
    def sd(cols, t=BF, rows=ROWS):
        return jax.ShapeDtypeStruct((rows, cols), t)

    shapes, specs = [sd(D)], [VM]
    if save:
        shapes += [sd(D, F32, 16), sd(WIDE), sd(WIDE)]
        specs += [VM, ANYS, ANYS]
    m = len(layers)
    work = [pltpu.VMEM((ROWS, 3 * D), BF), pltpu.VMEM((ROWS, FF), BF), pltpu.VMEM((ROWS, FF), BF),
            pltpu.VMEM((ROWS, 3 * D), BF), pltpu.VMEM((ROWS, D), BF), pltpu.VMEM((16, D), F32)]
    kept = [a for s in layers for a in saved[s]]
    return pl.pallas_call(
        functools.partial(backward_kernel, save, layers, len(wa)),
        out_shape=shapes,
        in_specs=[SM, VM, VM] + [VM, VM, VM, ANYS, ANYS] * m + [ANYS] * (save + 2 * len(wa)),
        out_specs=specs,
        scratch_shapes=weight_scratch(len(wa)) * m + work * m + [
            pltpu.VMEM((ROWS, D), BF), pltpu.SemaphoreType.DMA((m, 2)), pltpu.SemaphoreType.DMA((5,))],
        compiler_params=pltpu.CompilerParams(vmem_limit_bytes=VMEM_LIMIT),
        cost_estimate=pl.CostEstimate(flops=2 * ROWS * D * D * 14 * m, bytes_accessed=m * (24 * D * D + 2**23), transcendentals=0),
        name="backward_layers",
    )(info, g, mask, *kept, *([behind] if save else []), *wa, *wb)


def product_kernel(n, joined, info, slots, gv, fk_hbm, bk_hbm, fr_hbm, br_hbm, *rest):
    outs = [rest[0].at[j] for j in range(n)] if joined else rest[:n]
    f, b, held, isems, osems = rest[-5:]
    r = D // n
    flat = HALF
    loads = {}

    def load(first, core):
        mine = range(2 if core == 0 else HALF) if first else range(HALF if core == 0 else 3)
        for k in mine:
            dst, own, other = (f, fk_hbm, fr_hbm) if first else (b, bk_hbm, br_hbm)
            sem = isems.at[0 if first else 1, k]
            for half, src in enumerate((own, other)):
                pltpu.make_async_copy(src.at[:, pl.ds(k * D, D)], dst.at[k, pl.ds(half * ROWS, ROWS)], sem).start()
            loads[core, first, k] = pltpu.make_async_copy(dst.at[k], dst.at[k], sem)

    def operand(first, core, k):
        wait = loads.pop((core, first, k), None)
        if wait is not None:
            wait.wait()
        return (f if first else b)[k]

    for j in range(n):
        held[j, flat * r:] = gv[...].astype(BF)
        pltpu.make_async_copy(held.at[j, pl.ds(flat * r, TAIL)], outs[j].at[pl.ds(flat * r, TAIL)], osems.at[0]).start()

    def store(c, val):
        for j in range(n):
            held[slots[j], c * r:(c + 1) * r] = val[j * r:(j + 1) * r]
        for j in range(n):
            rows = pl.ds(c * r, r)
            pltpu.make_async_copy(held.at[j, rows], outs[j].at[rows], osems.at[0]).start()

    def store_rows(c, val):
        for i in range(n // 4):
            held[slots[c * (n // 4) + i], :4 * r] = val[i * 4 * r:(i + 1) * 4 * r]
        if c == 3:
            for j in range(n):
                rows = pl.ds(0, 4 * r)
                pltpu.make_async_copy(held.at[j, rows], outs[j].at[rows], osems.at[0]).start()

    @pl.when(info[5] == 0)
    def _():
        load(True, 0)
        load(False, 0)
        for c in range(HALF):
            val = dot(operand(True, 0, 0 if c < 4 else 1), operand(False, 0, c), 0, 0).astype(BF)
            store(c, val)

    @pl.when(info[5] != 0)
    def _():
        load(False, 1)
        load(True, 1)
        for c in range(HALF):
            val = dot(operand(True, 1, c), operand(False, 1, 0 if c < 4 else c - 3), 0, 0).astype(BF)
            if c < 4 and n > 1:
                store_rows(c, val)
            else:
                store(c, val)

    for j in range(n):
        pltpu.make_async_copy(held.at[j], outs[j], osems.at[0]).wait()


def weight_products(n, joined, info, slots, gv, fk, bk, fr, br):
    shape = (HALF * (D // n) + TAIL, D)
    shapes = [jax.ShapeDtypeStruct((n,) + shape, BF)] if joined else [jax.ShapeDtypeStruct(shape, BF)] * n
    scratch = [pltpu.VMEM((HALF, 2 * ROWS, D), BF), pltpu.VMEM((HALF, 2 * ROWS, D), BF), pltpu.VMEM((n,) + shape, BF),
               pltpu.SemaphoreType.DMA((2, HALF)), pltpu.SemaphoreType.DMA((1,))]
    return pl.pallas_call(
        functools.partial(product_kernel, n, joined),
        out_shape=shapes,
        in_specs=[SM, SM, VM] + [ANYS] * 4,
        out_specs=[ANYS] * len(shapes),
        scratch_shapes=scratch,
        compiler_params=pltpu.CompilerParams(vmem_limit_bytes=VMEM_LIMIT),
        cost_estimate=pl.CostEstimate(flops=2 * 2 * ROWS * D * D * 6, bytes_accessed=2**24, transcendentals=0),
        name="weight_products",
    )(info, slots, gv, fk, bk, fr, br)


def pack_kernel(info, joint, output, up, down, ag, as_, jb, ob, fg, fs, db, ub, block_ref, pair_ref):
    r = output.shape[0]
    spot = info[2] * 2 + info[3]
    for k in range(3):
        block_ref[k * r:(k + 1) * r, :] = joint[:, k * D:(k + 1) * D].astype(BF)
    block_ref[3 * r:4 * r, :] = output[...].astype(BF)
    for k in range(2):
        block_ref[(4 + k) * r:(5 + k) * r, :] = up[:, k * D:(k + 1) * D].astype(BF)
        pair_ref[k * r:(k + 1) * r, :] = up[:, (2 + k) * D:(3 + k) * D].astype(BF)
    block_ref[6 * r:10 * r, :] = down[...].astype(BF)

    def placed(ref, at):
        wide = ref.shape[1]
        lane = lax.broadcasted_iota(jnp.int32, (wide, D), 1)
        entry = lax.broadcasted_iota(jnp.int32, (wide, D), 0)
        return dot(ref[...].astype(BF), (lane == entry + at * wide).astype(BF))

    zero = jnp.zeros((1, D), F32)
    jrow = placed(jb, spot % 4)
    urow = placed(ub, spot % 2)
    rows = [placed(ag, spot), placed(as_, spot)]
    rows += [jnp.where(spot // 4 == k, jrow, zero) for k in range(2)]
    rows += [placed(v, spot) for v in (ob, fg, fs, db)]
    rows += [jnp.where(spot // 2 == k, urow, zero) for k in range(4)] + [zero] * 4
    block_ref[10 * r:, :] = jnp.concatenate(rows).astype(BF)


def pack(info, *params):
    r = params[1].shape[0]
    return pl.pallas_call(
        pack_kernel,
        out_shape=[jax.ShapeDtypeStruct((10 * r + TAIL, D), BF), jax.ShapeDtypeStruct((2 * r, D), BF)],
        in_specs=[SM] + [VM] * 12,
        out_specs=[VM, VM],
        compiler_params=pltpu.CompilerParams(vmem_limit_bytes=VMEM_LIMIT),
        name="pack",
    )(info, *params)


def moved(value, axis, by):
    peers = lax.axis_size(axis)
    return lax.ppermute(value, axis, [(i, i + by) for i in range(peers) if 0 <= i + by < peers])


def swapped(value):
    peers = lax.axis_size("section")
    return lax.ppermute(value, "section", [(i, i ^ 1) for i in range(peers)])


def vector_tail(n, spot, attend_gain, attend_shift, joint_bias, output_bias, feed_gain, feed_shift, down_bias, up_bias):
    lane = jnp.arange(D)

    def row(v, times, at, live=True):
        return jnp.where((lane // v.shape[0] == at) & live, jnp.tile(v, times), 0.0)

    half, quarter = n // 2, n // 4
    rows = [row(attend_gain, n, spot), row(attend_shift, n, spot)]
    rows += [row(joint_bias, half, spot % half, spot // half == k) for k in range(2)]
    rows += [row(v, n, spot) for v in (output_bias, feed_gain, feed_shift, down_bias)]
    rows += [row(up_bias, quarter, spot % quarter, spot // quarter == k) for k in range(4)]
    return jnp.concatenate([jnp.stack(rows), jnp.zeros((4, D), F32)])


def pack_shard(joint, output, up, down, tail):
    pieces = [joint[:, k * D:(k + 1) * D] for k in range(3)] + [output]
    pieces += [up[:, k * D:(k + 1) * D] for k in range(4)]
    return jnp.concatenate(pieces + [down, tail]).astype(BF)


def kernel_form(n, g, tail):
    r = D // n
    cut = jnp.swapaxes(g[:, :8 * r].reshape(n, 8, r, D), 0, 1).reshape(8 * D, D)
    return [jnp.concatenate([cut, g[:, 8 * r:12 * r].reshape(FF, D), tail.astype(BF)])]


IN, OUT, MID, PAIR = ((0, 1), (3, 2)), ((1, 0), (2, 3)), ((1, 2), (2, 1)), ((0, 1), (1, 0), (2, 3), (3, 2))


class Links:
    def __init__(self, **depth):
        self.depth = {"x": depth["x"], "in": depth["z"], "mid": depth["z"], "out": depth["z"]}
        self.ended = {"x": [], "in": [], "mid": [], "out": []}

    def send(self, value, names, axis, pairs):
        for name in names:
            done = self.ended[name]
            if len(done) >= self.depth[name]:
                value = lax.optimization_barrier((value, done[-self.depth[name]]))[0]
        got = lax.ppermute(value, axis, pairs)
        for name in names:
            self.ended[name].append(got)
        return got

    def along(self, value, moves):
        names = {IN: ("in",), OUT: ("out",), MID: ("mid",), PAIR: ("out",)}[moves]
        return self.send(value, names, "dp", [(2 * a + x, 2 * b + x) for a, b in moves for x in range(2)])

    def across(self, value, core=None):
        if core is None:
            return self.send(value, ("x",), "dp", [(i, i ^ 1) for i in range(8)])
        places = [8 * s + i for s in range(lax.axis_size("section")) if s % 2 == core for i in range(8)]
        return self.send(value, ("x",), ("section", "dp"), [(i, i ^ 1) for i in places])


def gather_blocks(own, pair, middle):
    net = Links(x=1, z=9)
    one, mid = net.along(own, PAIR), net.along(own, MID)
    first = net.across(pair, 0)
    sent = [net.across(own)]
    first = first + net.across(pair, 1)
    both = jnp.concatenate([pair, first])
    far, back = net.along(mid, OUT), net.along(one, MID)
    sent.append(net.across(one))
    both_one, both_mid = net.along(both, PAIR), net.along(both, MID)
    last = net.along(back, OUT)
    third = jnp.where(middle, mid, far)
    sent.append(net.across(third))
    both_far, both_back = net.along(both_mid, OUT), net.along(both_one, MID)
    fourth = jnp.where(middle, back, last)
    sent.append(net.across(fourth))
    both_last = net.along(both_back, OUT)
    mine = [own, one, third, fourth] + sent
    mine += [both, both_one, jnp.where(middle, both_mid, both_far), jnp.where(middle, both_back, both_last)]
    return mine, [swapped(b) for b in mine]


def add(*terms):
    total = terms[0].astype(F32)
    for t in terms[1:]:
        total = total + t.astype(F32)
    return total.astype(BF)


def scatter_steps(net, blocks, across, zero=None):
    def own(k):
        extra = [zero] if zero is not None and k == 1 else []
        return add(blocks[k], net.across(blocks[4 + k]), *extra) if across else blocks[k]

    s0 = own(0)
    a1 = net.along(s0, IN)
    yield
    s1 = own(1)
    a2 = net.along(s1, IN)
    b2 = net.along(add(s0, a1), MID)
    yield
    s2 = own(2)
    a3 = net.along(s2, IN)
    b3 = net.along(add(s1, a2), MID)
    c3 = net.along(add(s2, b2), OUT)
    yield
    total = add(own(3), a3, b3, c3)
    if not across:
        half = total.shape[0] // 2
        total = add(total[:half], net.across(total[half:]))
    yield total


def shards(tokens, lengths, cotangent, attend_gain, attend_shift, joint_weight, joint_bias, output_weight,
           output_bias, feed_gain, feed_shift, up_weight, up_bias, down_weight, down_bias):
    n = lax.axis_size("dp")
    r = D // n
    lined = n == 8
    nk = n if lined else 1
    sections = lax.axis_size("section")
    stages = sections // 2
    index = lax.axis_index("section")
    core, stage = index % 2, index // 2
    seq = tokens.shape[1]
    spot = lax.axis_index("dp")
    z, column = spot // 2, spot % 2
    middle = (z == 1) | (z == 2)
    info = jnp.stack([core, 1 - core, z, column, middle.astype(jnp.int32), core, 2 + middle]).astype(jnp.int32)
    if lined:
        order = jnp.array([[3, 2, 1, 0], [2, 3, 1, 0], [0, 1, 3, 2], [0, 1, 2, 3]], jnp.int32)[z]
        slots = jnp.stack([order[j // 2] + jnp.where(column == j % 2, 0, 4) for j in range(8)]).astype(jnp.int32)
    else:
        slots = jnp.zeros((1,), jnp.int32)

    if lined:
        packed, pair = pack(info, joint_weight[0], output_weight[0], up_weight[0], down_weight[0], attend_gain, attend_shift,
                            joint_bias, output_bias, feed_gain, feed_shift, down_bias, up_bias)
        wa, wb = gather_blocks(packed, pair, middle)
    else:
        tail = vector_tail(n, spot, attend_gain[0], attend_shift[0], joint_bias[0], output_bias[0], feed_gain[0],
                           feed_shift[0], down_bias[0], up_bias[0])
        packed = pack_shard(joint_weight[0], output_weight[0], up_weight[0], down_weight[0], tail)
        gathered = lax.all_gather(packed, "dp")
        tails = lax.psum(tail.astype(BF).astype(F32), "dp")
        wa, wb = kernel_form(n, gathered, tails), kernel_form(n, swapped(gathered), swapped(tails))

    def own_pair(a):
        return lax.dynamic_index_in_dim(a, core, 0, False)

    def padded(a):
        return jnp.pad(a, ((0, ROWS - seq), (0, 0)))

    places = lax.broadcasted_iota(jnp.int32, (8, ROWS), 1)
    mask = (((places < own_pair(lengths)) | (places >= CAPTION)) & (places < seq)).astype(F32)
    own_tokens = padded(own_pair(tokens))
    own_cotangent = padded(own_pair(cotangent))

    x = own_tokens
    for t in range(stages):
        last = t == stages - 1
        got = forward_stage(last, info, x, mask, wa, wb)
        if not last:
            x = jnp.where(stage == 0, own_tokens, moved(got[1], "section", 2))
    leaving = got[1]
    saved = [(x, *got[2:6]), (got[0], *got[8:12])]
    kept = [got[6], got[12]]
    received = [swapped(got[7]), swapped(got[13])]

    g = own_cotangent
    for t in range(stages - 1):
        g = backward_layers(False, (1, 0), info, g, mask, saved, wa, wb, None)[0]
        g = jnp.where(stage == stages - 1, own_cotangent, moved(g, "section", -2))
    products = [None, None]
    behind = mask
    for s in (1, 0):
        g, gv, bk, bs = backward_layers(True, (s,), info, g, mask, saved, wa, wb, behind)
        products[s] = weight_products(nk, s == 1 and lined, info, slots if s == 0 else jnp.arange(nk, dtype=jnp.int32),
                                      gv, kept[s], bk, received[s], swapped(bs))
        behind = products[s][0]

    ends = jnp.where(stage == 0, g, leaving)[:seq].reshape(seq, sections, D // sections)
    swept = lax.all_to_all(ends, "section", split_axis=1, concat_axis=0, tiled=True)
    pieces = swept.reshape(sections, seq, D // sections)
    outputs = pieces[sections - 2:]
    token_grad = pieces[:2]
    zero = jnp.minimum(jnp.abs(swept[0, 0, 0].astype(F32)), 0.0)

    reduced = [None, None]
    if lined:
        net = Links(x=2, z=9)
        reduced[1] = lax.psum_scatter(products[1][0], "dp", scatter_dimension=0)
        reduced[0] = list(scatter_steps(net, products[0], True, zero))[-1]
    else:
        for s in range(2):
            p = products[s][0]
            col = jnp.swapaxes(p[:HALF * D].reshape(HALF, n, r, D), 0, 1).reshape(n, HALF * r, D)
            row = jnp.concatenate([p[:4 * D].reshape(n, 4 * r, D), col[:, 4 * r:]], axis=1)
            total = lax.psum_scatter(jnp.where(core == 0, col, row), "dp", scatter_dimension=0)
            reduced[s] = jnp.concatenate([total, lax.psum(p[HALF * D:], "dp")])
    sent = [lax.ppermute(reduced[s], "section", [(i, i ^ 1) for i in range(sections) if i % 2 != s]) for s in range(2)]
    keep = jnp.where(core == 0, reduced[0], reduced[1])
    away = jnp.where(core == 0, sent[0], sent[1])
    first = jnp.where(core == 0, keep, away).astype(F32)
    second = jnp.where(core == 0, away, keep).astype(F32)
    grad_up = jnp.concatenate([first[k * r:(k + 1) * r] for k in range(4)], axis=1)
    grad_joint = jnp.concatenate([first[4 * r:5 * r], first[5 * r:6 * r], second[5 * r:6 * r]], axis=1)
    grad_down = second[:4 * r]
    grad_out = second[4 * r:5 * r]
    v = first[6 * r:] + second[6 * r:]
    half, quarter = n // 2, n // 4
    vec = lax.dynamic_slice(v, (0, r * spot), (16, r))
    grad_jb = lax.dynamic_slice(v, (BQ + spot // half, 2 * r * (spot % half)), (1, 2 * r))
    grad_ub = lax.dynamic_slice(v, (UB + spot // quarter, 4 * r * (spot % quarter)), (1, 4 * r))
    return (outputs, token_grad, vec[AG:AG + 1], vec[AS:AS + 1], grad_joint[None], grad_jb, grad_out[None],
            vec[OB:OB + 1], vec[FG:FG + 1], vec[FS:FS + 1], grad_up[None], grad_ub, grad_down[None], vec[DB:DB + 1])


def solution(mesh):
    vec, mat = P("section", "dp"), P("section", "dp", None)
    rows = P("dp", None, None)
    out = P("dp", None, "section")
    return jax.shard_map(
        shards,
        mesh=mesh,
        in_specs=(rows, P("dp"), rows, vec, vec, mat, vec, mat, vec, vec, vec, mat, vec, mat, vec),
        out_specs=(out, out, vec, vec, mat, vec, mat, vec, vec, vec, mat, vec, mat, vec),
        check_vma=False,
    )
```

```python
import functools

import jax
import jax.numpy as jnp
from jax import lax
from jax.experimental import pallas as pl
from jax.experimental.pallas import tpu as pltpu
from jax.sharding import PartitionSpec as P

D = 768
HEADS = 12
FF = 3072
CAPTION = 40
ROWS = 288
HALF = 6
TAIL = 16
EPS = 1e-6
BF = jnp.bfloat16
F32 = jnp.float32
PAIRED = 2 * (D // HEADS)
VMEM_LIMIT = 60 * 2**20
WIDE = FF + 2 * D
AG, AS, BQ, BV, OB, FG, FS, DB, UB = 0, 1, 2, 3, 4, 5, 6, 7, 8

ANYS = pl.BlockSpec(memory_space=pl.ANY)
VM = pl.BlockSpec(memory_space=pltpu.VMEM)


def dot(a, b, ca=1, cb=0):
    return lax.dot_general(a, b, (((ca,), (cb,)), ((), ())), preferred_element_type=F32)


def spread_of(v):
    mean = jnp.mean(v, axis=-1, keepdims=True)
    cent = v - mean
    return cent, lax.rsqrt(jnp.mean(cent * cent, axis=-1, keepdims=True) + EPS)


def here():
    spot, core = lax.axis_index("dp"), lax.axis_index("section") % 2
    z, column = spot // 2, spot % 2
    middle = jnp.where((z == 1) | (z == 2), 1, 0)
    return [core, 1 - core, z, column, middle, core, 2 + middle]


def sending_slots(z, column):
    orders = ((3, 2, 1, 0), (2, 3, 1, 0), (0, 1, 3, 2), (0, 1, 2, 3))
    slots = []
    for j in range(8):
        a, b, c, d = (o[j // 2] for o in orders)
        slot = jnp.where(z == 0, a, jnp.where(z == 1, b, jnp.where(z == 2, c, d)))
        slots.append(slot + jnp.where(column == j % 2, 0, 4))
    return slots


def square(block):
    return block.reshape(D, D)


def weight_scratch(count):
    n, r, per = (8, D // 8, 2) if count > 1 else (1, D, 1)
    return [pltpu.VMEM((8, n, r, D), BF), pltpu.VMEM((4, per, D // per, D), BF), pltpu.VMEM((n, TAIL, D), BF),
            pltpu.SemaphoreType.DMA((13,))]


def start_weights(which, info, sets, scratch, order):
    wv, wd, tv, sems = scratch
    r = wv.shape[2]

    def start(block, j, part):
        if len(sets[0]) == 1:
            rows = block.at[pl.ds(part * r, r if part < 12 else TAIL)]
            dst = wv.at[part, 0] if part < 8 else wd.at[part - 8, 0] if part < 12 else tv.at[0]
            pltpu.make_async_copy(rows, dst, sems.at[part]).start()
        elif part == 12:
            pltpu.make_async_copy(block.at[pl.ds(10 * r, TAIL)], tv.at[j], sems.at[12]).start()
        elif part < 6:
            pltpu.make_async_copy(block.at[pl.ds(part * r, r)], wv.at[part, j], sems.at[part]).start()
        elif part == 8:
            b = j // 2
            pltpu.make_async_copy(block.at[pl.ds(6 * r, 4 * r)], wd.at[b, j % 2], sems.at[8 + b]).start()

    for number, blocks in enumerate(sets):

        @pl.when(info[which] == number)
        def _():
            if len(blocks) == 1:
                for part in order:
                    start(blocks[0], 0, part)
                return
            lines = [info[2], info[2] ^ 1, info[2] ^ info[6], info[2] ^ (info[6] ^ 1)]
            spots = [(blocks[4 * far + k], lines[k] * 2 + (info[3] ^ far)) for far in (0, 1) for k in range(4)]
            for part in order:
                if part in (6, 7):
                    for far in (0, 1):
                        for k in range(4):
                            rows = blocks[8 + k].at[pl.ds((2 * far + part - 6) * r, r)]
                            pltpu.make_async_copy(rows, wv.at[part, lines[k] * 2 + (info[3] ^ far)], sems.at[part]).start()
                    continue
                for block, j in spots:
                    start(block, j, part)

    waits = [pltpu.make_async_copy(wv.at[k], wv.at[k], sems.at[k]) for k in range(8)]
    waits += [pltpu.make_async_copy(wd.at[b], wd.at[b], sems.at[8 + b]) for b in range(4)]
    return waits + [pltpu.make_async_copy(tv, tv, sems.at[12])]


def vectors(tv):
    total = tv[0].astype(F32)
    for j in range(1, tv.shape[0]):
        total = total + tv[j].astype(F32)
    return total


def handing(core, keep, send, sems, waits):
    def hand_on(src, first, at):
        wide = src.shape[1]
        sem = sems.at[len(waits)]
        mine = (core == 0) == first

        @pl.when(mine)
        def _():
            pltpu.make_async_copy(src, keep.at[:, pl.ds(at, wide)], sem).start()

        @pl.when(jnp.logical_not(mine))
        def _():
            pltpu.make_async_copy(src, send.at[:, pl.ds(at, wide)], sem).start()

        waits.append(pltpu.make_async_copy(src, keep.at[:, pl.ds(at, wide)], sem))

    return hand_on


def forward_one(save, core, x, usable, copies, scratch, work, osems, saved, outs):
    wv, wd, tv, _ = scratch
    jn, ctx, act, gp, nrm, nt, vec = work
    if save:
        lse_ref, mid_ref, j_hbm, gp_hbm, keep, send = saved
        hand_on = handing(core, keep, send, osems, outs)

        def flush(src, dst):
            c = pltpu.make_async_copy(src, dst, osems.at[len(outs)])
            c.start()
            outs.append(c)

    copies[12].wait()
    vec[...] = vectors(tv)
    cent, inv = spread_of(x)
    nrm[...] = (cent * inv * vec[AG:AG + 1, :] + vec[AS:AS + 1, :]).astype(BF)
    if save:
        hand_on(nrm, True, D)
        hand_on(nrm, False, FF + D)
    for k in range(3):
        copies[k].wait()
        r = dot(nrm[...], square(wv[k]))
        if k == 0:
            r = r + vec[BQ:BQ + 1, :]
        if k == 2:
            r = r + vec[BV:BV + 1, :]
        jn[:, k * D:(k + 1) * D] = r.astype(BF)
    if save:
        flush(jn, j_hbm)
    lane = lax.broadcasted_iota(jnp.int32, (ROWS, PAIRED), 1)
    low = lane < PAIRED // 2
    lse = jnp.zeros((ROWS, PAIRED), F32)
    for i in range(HEADS // 2):
        at = i * PAIRED
        q2 = jn[:, at:at + PAIRED] * BF(0.125)
        k2 = jn[:, D + at:D + at + PAIRED]
        v2 = jn[:, 2 * D + at:2 * D + at + PAIRED]
        zero = jnp.zeros_like(q2)
        both = []
        for h in range(2):
            s = dot(jnp.where(low == (h == 0), q2, zero), k2, 1, 1)
            s = jnp.where(usable, s, -1e30)
            top = jnp.max(s, axis=-1, keepdims=True)
            e = jnp.exp(s - top)
            total = jnp.sum(e, axis=-1, keepdims=True)
            both.append(dot(e.astype(BF), v2) * (1.0 / total))
            if save:
                lse = jnp.where(lane == 2 * i + h, top + jnp.log(total), lse)
        ctx[:, at:at + PAIRED] = jnp.where(low, both[0], both[1]).astype(BF)
    if save:
        lse_ref[...] = lse
        hand_on(ctx, False, FF)
    for k in range(3, 12):
        copies[k].wait()
    middle = x + dot(ctx[...], square(wv[3])) + vec[OB:OB + 1, :]
    if save:
        mid_ref[...] = middle
    cent, inv = spread_of(middle)
    nt[...] = (cent * inv * vec[FG:FG + 1, :] + vec[FS:FS + 1, :]).astype(BF)
    if save:
        hand_on(nt, True, 0)
    acc = middle + vec[DB:DB + 1, :]
    for b in range(4):
        cols = slice(b * D, (b + 1) * D)
        h = dot(nt[...], square(wv[4 + b])) + vec[UB + b:UB + b + 1, :]
        phi = 0.5 + 0.5 * lax.erf(h * (0.5**0.5))
        a = (h * phi).astype(BF)
        if save:
            act[:, cols] = a
            gp[:, cols] = (phi + h * jnp.exp(-0.5 * h * h) * 0.3989422804014327).astype(BF)
        acc = acc + dot(a, square(wd[b]))
    if save:
        hand_on(act, False, 0)
        flush(gp, gp_hbm)
    return acc.astype(BF)


def forward_kernel(save, count, x_ref, mask_ref, *rest):
    info = here()
    sets, rest = (rest[:count], rest[count:2 * count]), rest[2 * count:]
    wide = 14 if save else 2
    results, rest = rest[:wide], rest[wide:]
    scratch = [rest[0:4], rest[4:8]]
    rest = rest[8:]
    copies = [start_weights(s, info, sets, scratch[s], (12,) + tuple(range(12))) for s in range(2)]
    usable = mask_ref[0:1, :] > 0.5
    outs = []
    x = x_ref[...]
    for s in range(2):
        work, rest = rest[:7], rest[7:]
        saved = results[2 + 6 * s:8 + 6 * s] if save else ()
        x = forward_one(save, info[5], x.astype(F32), usable, copies[s], scratch[s], work, rest[7 * (1 - s)], saved, outs)
        results[s][...] = x
    for c in outs:
        c.wait()


def forward_stage(save, x, mask, wa, wb):
    def sd(cols, t=BF):
        return jax.ShapeDtypeStruct((ROWS, cols), t)

    shapes, specs = [sd(D)] * 2, [VM] * 2
    if save:
        shapes += [sd(PAIRED, F32), sd(D, F32), sd(3 * D), sd(FF), sd(WIDE), sd(WIDE)] * 2
        specs += ([VM, VM] + [ANYS] * 4) * 2
    work = [pltpu.VMEM((ROWS, 3 * D), BF), pltpu.VMEM((ROWS, D), BF), pltpu.VMEM((ROWS, FF), BF),
            pltpu.VMEM((ROWS, FF), BF), pltpu.VMEM((ROWS, D), BF), pltpu.VMEM((ROWS, D), BF), pltpu.VMEM((16, D), F32)]
    return pl.pallas_call(
        functools.partial(forward_kernel, save, len(wa)),
        out_shape=shapes,
        in_specs=[VM, VM] + [ANYS] * (2 * len(wa)),
        out_specs=specs,
        scratch_shapes=weight_scratch(len(wa)) * 2 + work * 2 + [pltpu.SemaphoreType.DMA((14,))],
        compiler_params=pltpu.CompilerParams(vmem_limit_bytes=VMEM_LIMIT),
        cost_estimate=pl.CostEstimate(flops=2 * ROWS * D * D * 26, bytes_accessed=48 * D * D + 2**23, transcendentals=0),
        name="forward_stage",
    )(x, mask, *wa, *wb)


def backward_one(save, core, g_ref, x_ref, lse_ref, mid_ref, j_hbm, gp_hbm, usable, copies, scratch, work, isems, osems, results,
                 waits):
    wv, wd, tv, _ = scratch
    jn, gp, dh, dj, b1, vec = work
    hand_on = lambda *a: None
    if save:
        gv_ref, keep_hbm, send_hbm = results
        hand_on = handing(core, keep_hbm, send_hbm, osems, waits)
    hand_on(g_ref, False, 0)
    copies[12].wait()
    vec[...] = vectors(tv)
    d_nt = None
    for b in range(4):
        cols = slice(b * D, (b + 1) * D)
        copies[8 + b].wait()
        if b == 0:
            pltpu.make_async_copy(gp_hbm, gp, isems.at[0]).wait()
        da = dot(g_ref[...], square(wd[b]), 1, 1)
        d = (da * gp[:, cols].astype(F32)).astype(BF)
        dh[:, cols] = d
        copies[4 + b].wait()
        part = dot(d, square(wv[4 + b]), 1, 1)
        d_nt = part if d_nt is None else d_nt + part
    hand_on(dh, True, 0)

    def norm_back(v, dy, gain, row):
        cent, inv = spread_of(v)
        hat = cent * inv
        if save:
            gv_ref[row:row + 1, :] = jnp.sum(dy * hat, axis=0, keepdims=True)
            gv_ref[row + 1:row + 2, :] = jnp.sum(dy, axis=0, keepdims=True)
        t = dy * gain
        return inv * (t - jnp.mean(t, axis=-1, keepdims=True) - hat * jnp.mean(t * hat, axis=-1, keepdims=True))

    d_mid = g_ref[...].astype(F32) + norm_back(mid_ref[...], d_nt, vec[FG:FG + 1, :], FG)
    b1[...] = d_mid.astype(BF)
    hand_on(b1, False, D)
    if save:
        for b in range(4):
            gv_ref[UB + b:UB + b + 1, :] = jnp.sum(dh[:, b * D:(b + 1) * D].astype(F32), axis=0, keepdims=True)
        gv_ref[DB:DB + 1, :] = jnp.sum(g_ref[...].astype(F32), axis=0, keepdims=True)
        gv_ref[OB:OB + 1, :] = jnp.sum(b1[...].astype(F32), axis=0, keepdims=True)
    copies[3].wait()
    d_ctx = dot(b1[...], square(wv[3]), 1, 1).astype(BF)
    pltpu.make_async_copy(j_hbm, jn, isems.at[1]).wait()
    for k in range(3):
        copies[k].wait()
    lane = lax.broadcasted_iota(jnp.int32, (ROWS, PAIRED), 1)
    low = lane < PAIRED // 2
    for i in range(HEADS // 2):
        at = i * PAIRED
        q2 = jn[:, at:at + PAIRED] * BF(0.125)
        k2 = jn[:, D + at:D + at + PAIRED]
        v2 = jn[:, 2 * D + at:2 * D + at + PAIRED]
        do2 = d_ctx[:, at:at + PAIRED]
        zero = jnp.zeros_like(q2)
        res = []
        for h in range(2):
            here = low == (h == 0)
            s = dot(jnp.where(here, q2, zero), k2, 1, 1)
            p = jnp.where(usable, jnp.exp(s - lse_ref[:, 2 * i + h:2 * i + h + 1]), 0.0)
            dp = dot(jnp.where(here, do2, zero), v2, 1, 1)
            inner = jnp.sum(p * dp, axis=-1, keepdims=True)
            dsc = (p * (dp - inner)).astype(BF)
            res.append((dot(dsc, k2) * 0.125, dot(dsc, q2, 0, 0), dot(p.astype(BF), do2, 0, 0)))
        for c in range(3):
            dj[:, c * D + at:c * D + at + PAIRED] = jnp.where(low, res[0][c], res[1][c]).astype(BF)
    hand_on(dj.at[:, pl.ds(0, 2 * D)], True, FF)
    hand_on(dj.at[:, pl.ds(2 * D, D)], False, 2 * D)
    if save:
        gv_ref[BQ:BQ + 1, :] = jnp.sum(dj[:, :D].astype(F32), axis=0, keepdims=True)
        gv_ref[BV:BV + 1, :] = jnp.sum(dj[:, 2 * D:].astype(F32), axis=0, keepdims=True)
        gv_ref[UB + 4:, :] = jnp.zeros((4, D), F32)
    d_n = dot(dj[:, :D], square(wv[0]), 1, 1)
    for k in (1, 2):
        d_n = d_n + dot(dj[:, k * D:(k + 1) * D], square(wv[k]), 1, 1)
    return (d_mid + norm_back(x_ref[...].astype(F32), d_n, vec[AG:AG + 1, :], AG)).astype(BF)


def backward_kernel(save, layers, count, g_ref, mask_ref, *rest):
    info = here()
    m = len(layers)
    kept, rest = [rest[5 * i:5 * i + 5] for i in range(m)], rest[5 * m:]
    rest = rest[1:] if save else rest
    sets, rest = (rest[:count], rest[count:2 * count]), rest[2 * count:]
    wide = 4 if save else 1
    results, rest = rest[:wide], rest[wide:]
    scratch, rest = [rest[4 * i:4 * i + 4] for i in range(m)], rest[4 * m:]
    work, (gs, isems, osems) = [rest[6 * i:6 * i + 6] for i in range(m)], rest[6 * m:]
    copies = []
    for i in range(m):
        pltpu.make_async_copy(kept[i][4], work[i][1], isems.at[i, 0]).start()
        copies.append(start_weights(layers[i], info, sets, scratch[i], (12, 8, 9, 10, 11, 4, 5, 6, 7, 3, 0, 1, 2)))
        pltpu.make_async_copy(kept[i][3], work[i][0], isems.at[i, 1]).start()
    usable = mask_ref[0:1, :] > 0.5
    waits = []
    for i in range(m):
        x_ref, lse_ref, mid_ref, j_hbm, gp_hbm = kept[i]
        g = backward_one(save, info[5], g_ref if i == 0 else gs, x_ref, lse_ref, mid_ref, j_hbm, gp_hbm, usable, copies[i],
                         scratch[i], work[i], isems.at[i], osems, results[1:], waits)
        if i + 1 < m:
            gs[...] = g
        else:
            results[0][...] = g
    for c in waits:
        c.wait()


def backward_layers(save, layers, g, mask, saved, wa, wb, behind):
    def sd(cols, t=BF, rows=ROWS):
        return jax.ShapeDtypeStruct((rows, cols), t)

    shapes, specs = [sd(D)], [VM]
    if save:
        shapes += [sd(D, F32, 16), sd(WIDE), sd(WIDE)]
        specs += [VM, ANYS, ANYS]
    m = len(layers)
    work = [pltpu.VMEM((ROWS, 3 * D), BF), pltpu.VMEM((ROWS, FF), BF), pltpu.VMEM((ROWS, FF), BF),
            pltpu.VMEM((ROWS, 3 * D), BF), pltpu.VMEM((ROWS, D), BF), pltpu.VMEM((16, D), F32)]
    kept = [a for s in layers for a in saved[s]]
    return pl.pallas_call(
        functools.partial(backward_kernel, save, layers, len(wa)),
        out_shape=shapes,
        in_specs=[VM, VM] + [VM, VM, VM, ANYS, ANYS] * m + [ANYS] * (save + 2 * len(wa)),
        out_specs=specs,
        scratch_shapes=weight_scratch(len(wa)) * m + work * m + [
            pltpu.VMEM((ROWS, D), BF), pltpu.SemaphoreType.DMA((m, 2)), pltpu.SemaphoreType.DMA((5,))],
        compiler_params=pltpu.CompilerParams(vmem_limit_bytes=VMEM_LIMIT),
        cost_estimate=pl.CostEstimate(flops=2 * ROWS * D * D * 14 * m, bytes_accessed=m * (24 * D * D + 2**23), transcendentals=0),
        name="backward_layers",
    )(g, mask, *kept, *([behind] if save else []), *wa, *wb)


def product_kernel(n, direct, behind, gv, fk_hbm, bk_hbm, fr_hbm, br_hbm, *rest):
    wide = n + 4 * (direct > 0)
    outs, rest = rest[:wide], rest[wide:]
    f, b, held, isems, osems = rest[:5]
    info = here()
    slots = sending_slots(info[2], info[3]) if n > 1 else [0]
    r = D // n
    flat = HALF - direct
    loads = {}

    def load(first, core):
        mine = range(2 if core == 0 else HALF) if first else range(HALF if core == 0 else 3)
        for k in mine:
            dst, own, other = (f, fk_hbm, fr_hbm) if first else (b, bk_hbm, br_hbm)
            sem = isems.at[0 if first else 1, k]
            for half, src in enumerate((own, other)):
                pltpu.make_async_copy(src.at[:, pl.ds(k * D, D)], dst.at[k, pl.ds(half * ROWS, ROWS)], sem).start()
            loads[core, first, k] = pltpu.make_async_copy(dst.at[k], dst.at[k], sem)

    def operand(first, core, k):
        wait = loads.pop((core, first, k), None)
        if wait is not None:
            wait.wait()
        return (f if first else b)[k]

    for j in range(n):
        held[j, flat * r:] = gv[...].astype(BF)
        pltpu.make_async_copy(held.at[j, pl.ds(flat * r, TAIL)], outs[j].at[pl.ds(flat * r, TAIL)], osems.at[0]).start()

    def store(c, val):
        if c >= flat:
            for j in range(n):
                rest[5][slots[j] % 4, slots[j] // 4, (c - flat) * r:(c - flat + 1) * r] = val[j * r:(j + 1) * r]
            if c == HALF - 1:
                for k in range(4):
                    for far in (0, 1):
                        rows = pl.ds(far * direct * r, direct * r)
                        pltpu.make_async_copy(rest[5].at[k, far], outs[n + k].at[rows], osems.at[0]).start()
            return
        for j in range(n):
            held[slots[j], c * r:(c + 1) * r] = val[j * r:(j + 1) * r]
        for j in range(n):
            rows = pl.ds(c * r, r)
            pltpu.make_async_copy(held.at[j, rows], outs[j].at[rows], osems.at[0]).start()

    def store_rows(c, val):
        for i in range(n // 4):
            held[slots[c * (n // 4) + i], :4 * r] = val[i * 4 * r:(i + 1) * 4 * r]
        if c == 3:
            for j in range(n):
                rows = pl.ds(0, 4 * r)
                pltpu.make_async_copy(held.at[j, rows], outs[j].at[rows], osems.at[0]).start()

    @pl.when(info[5] == 0)
    def _():
        load(True, 0)
        load(False, 0)
        for c in range(HALF):
            val = dot(operand(True, 0, 0 if c < 4 else 1), operand(False, 0, c), 0, 0).astype(BF)
            store(c, val)

    @pl.when(info[5] != 0)
    def _():
        load(False, 1)
        load(True, 1)
        for c in range(HALF):
            val = dot(operand(True, 1, c), operand(False, 1, 0 if c < 4 else c - 3), 0, 0).astype(BF)
            if c < 4 and n > 1:
                store_rows(c, val)
            else:
                store(c, val)

    for j in range(n):
        pltpu.make_async_copy(held.at[j], outs[j], osems.at[0]).wait()
    if direct:
        pltpu.make_async_copy(rest[5], rest[5], osems.at[0]).wait()


def weight_products(n, direct, behind, gv, fk, bk, fr, br):
    shape = ((HALF - direct) * (D // n) + TAIL, D)
    shapes = [jax.ShapeDtypeStruct(shape, BF)] * n
    scratch = [pltpu.VMEM((HALF, 2 * ROWS, D), BF), pltpu.VMEM((HALF, 2 * ROWS, D), BF), pltpu.VMEM((n,) + shape, BF),
               pltpu.SemaphoreType.DMA((2, HALF)), pltpu.SemaphoreType.DMA((1,))]
    if direct:
        shapes += [jax.ShapeDtypeStruct((2 * direct * (D // n), D), BF)] * 4
        scratch.append(pltpu.VMEM((4, 2, direct * (D // n), D), BF))
    return pl.pallas_call(
        functools.partial(product_kernel, n, direct),
        out_shape=shapes,
        in_specs=[ANYS, VM] + [ANYS] * 4,
        out_specs=[ANYS] * len(shapes),
        scratch_shapes=scratch,
        compiler_params=pltpu.CompilerParams(vmem_limit_bytes=VMEM_LIMIT),
        cost_estimate=pl.CostEstimate(flops=2 * 2 * ROWS * D * D * 6, bytes_accessed=2**24, transcendentals=0),
        name="weight_products",
    )(behind, gv, fk, bk, fr, br)


def pack_kernel(joint, output, up, down, ag, as_, jb, ob, fg, fs, db, ub, block_ref, pair_ref):
    r = output.shape[0]
    spot = lax.axis_index("dp")
    for k in range(3):
        block_ref[k * r:(k + 1) * r, :] = joint[:, k * D:(k + 1) * D].astype(BF)
    block_ref[3 * r:4 * r, :] = output[...].astype(BF)
    for k in range(2):
        block_ref[(4 + k) * r:(5 + k) * r, :] = up[:, k * D:(k + 1) * D].astype(BF)
        pair_ref[k * r:(k + 1) * r, :] = up[:, (2 + k) * D:(3 + k) * D].astype(BF)
    block_ref[6 * r:10 * r, :] = down[...].astype(BF)

    def placed(ref, at):
        wide = ref.shape[1]
        lane = lax.broadcasted_iota(jnp.int32, (wide, D), 1)
        entry = lax.broadcasted_iota(jnp.int32, (wide, D), 0)
        return dot(ref[...].astype(BF), (lane == entry + at * wide).astype(BF))

    zero = jnp.zeros((1, D), F32)
    jrow = placed(jb, spot % 4)
    urow = placed(ub, spot % 2)
    rows = [placed(ag, spot), placed(as_, spot)]
    rows += [jnp.where(spot // 4 == k, jrow, zero) for k in range(2)]
    rows += [placed(v, spot) for v in (ob, fg, fs, db)]
    rows += [jnp.where(spot // 2 == k, urow, zero) for k in range(4)] + [zero] * 4
    block_ref[10 * r:, :] = jnp.concatenate(rows).astype(BF)


def pack(*params):
    r = params[1].shape[0]
    return pl.pallas_call(
        pack_kernel,
        out_shape=[jax.ShapeDtypeStruct((10 * r + TAIL, D), BF), jax.ShapeDtypeStruct((2 * r, D), BF)],
        in_specs=[VM] * 12,
        out_specs=[VM, VM],
        compiler_params=pltpu.CompilerParams(vmem_limit_bytes=VMEM_LIMIT),
        name="pack",
    )(*params)


def moved(value, axis, by):
    peers = lax.axis_size(axis)
    return lax.ppermute(value, axis, [(i, i + by) for i in range(peers) if 0 <= i + by < peers])


def flipped(value, bit):
    peers = lax.axis_size("section")
    return lax.ppermute(value, "section", [(i, i ^ bit) for i in range(peers)])


def swapped(value):
    return flipped(value, 1)


def vector_tail(n, spot, attend_gain, attend_shift, joint_bias, output_bias, feed_gain, feed_shift, down_bias, up_bias):
    lane = jnp.arange(D)

    def row(v, times, at, live=True):
        return jnp.where((lane // v.shape[0] == at) & live, jnp.tile(v, times), 0.0)

    half, quarter = n // 2, n // 4
    rows = [row(attend_gain, n, spot), row(attend_shift, n, spot)]
    rows += [row(joint_bias, half, spot % half, spot // half == k) for k in range(2)]
    rows += [row(v, n, spot) for v in (output_bias, feed_gain, feed_shift, down_bias)]
    rows += [row(up_bias, quarter, spot % quarter, spot // quarter == k) for k in range(4)]
    return jnp.concatenate([jnp.stack(rows), jnp.zeros((4, D), F32)])


def pack_shard(joint, output, up, down, tail):
    pieces = [joint[:, k * D:(k + 1) * D] for k in range(3)] + [output]
    pieces += [up[:, k * D:(k + 1) * D] for k in range(4)]
    return jnp.concatenate(pieces + [down, tail]).astype(BF)


def kernel_form(n, g, tail):
    r = D // n
    cut = jnp.swapaxes(g[:, :8 * r].reshape(n, 8, r, D), 0, 1).reshape(8 * D, D)
    return [jnp.concatenate([cut, g[:, 8 * r:12 * r].reshape(FF, D), tail.astype(BF)])]


IN, OUT, MID, PAIR = ((0, 1), (3, 2)), ((1, 0), (2, 3)), ((1, 2), (2, 1)), ((0, 1), (1, 0), (2, 3), (3, 2))


class Links:
    def __init__(self, **depth):
        self.depth = {"x": depth["x"], "in": depth["z"], "mid": depth["z"], "out": depth["z"]}
        self.ended = {"x": [], "in": [], "mid": [], "out": []}

    def send(self, value, names, axis, pairs):
        for name in names:
            done = self.ended[name]
            if len(done) >= self.depth[name]:
                value = lax.optimization_barrier((value, done[-self.depth[name]]))[0]
        got = lax.ppermute(value, axis, pairs)
        for name in names:
            self.ended[name].append(got)
        return got

    def along(self, value, moves):
        names = {IN: ("in",), OUT: ("out",), MID: ("mid",), PAIR: ("out",)}[moves]
        return self.send(value, names, "dp", [(2 * a + x, 2 * b + x) for a, b in moves for x in range(2)])

    def across(self, value, core=None):
        if core is None:
            return self.send(value, ("x",), "dp", [(i, i ^ 1) for i in range(8)])
        places = [8 * s + i for s in range(lax.axis_size("section")) if s % 2 == core for i in range(8)]
        return self.send(value, ("x",), ("section", "dp"), [(i, i ^ 1) for i in places])


def gather_blocks(own, pair, middle):
    net = Links(x=1, z=9)
    one, mid = net.along(own, PAIR), net.along(own, MID)
    first = net.across(pair, 0)
    sent = [net.across(own)]
    first = first + net.across(pair, 1)
    both = jnp.concatenate([pair, first])
    far, back = net.along(mid, OUT), net.along(one, MID)
    sent.append(net.across(one))
    both_one, both_mid = net.along(both, PAIR), net.along(both, MID)
    last = net.along(back, OUT)
    third = jnp.where(middle, mid, far)
    sent.append(net.across(third))
    both_far, both_back = net.along(both_mid, OUT), net.along(both_one, MID)
    fourth = jnp.where(middle, back, last)
    sent.append(net.across(fourth))
    both_last = net.along(both_back, OUT)
    mine = [own, one, third, fourth] + sent
    mine += [both, both_one, jnp.where(middle, both_mid, both_far), jnp.where(middle, both_back, both_last)]
    return mine, [swapped(b) for b in mine]


def add(*terms):
    total = terms[0].astype(F32)
    for t in terms[1:]:
        total = total + t.astype(F32)
    return total.astype(BF)


def scatter_rounds(blocks, wide=None, extra=None):
    net = Links(x=9, z=9)
    x0 = net.across(blocks[4])
    s0 = add(blocks[0], x0)
    b, s0 = lax.optimization_barrier((blocks[5], s0))
    x1, a1 = net.across(b), net.along(s0, IN)
    s1, t0 = add(blocks[1], x1), add(s0, a1)
    if extra is None:
        b, s1, t0 = lax.optimization_barrier((blocks[6], s1, t0))
    else:
        b, s1, t0, extra = lax.optimization_barrier((blocks[6], s1, t0, extra))
    x2, a2, b2 = net.across(b), net.along(s1, IN), net.along(t0, MID)
    s2, t1 = add(blocks[2], x2), add(s1, a2)
    u = add(s2, b2)
    b, s2, t1, u = lax.optimization_barrier((blocks[7], s2, t1, u))
    x3, a3, b3, c3 = net.across(b), net.along(s2, IN), net.along(t1, MID), net.along(u, OUT)
    return add(blocks[3], x3, a3, b3, c3), extra


def scatter_steps(net, blocks, across):
    def own(k):
        return add(blocks[k], net.across(blocks[4 + k])) if across else blocks[k]

    s0 = own(0)
    a1 = net.along(s0, IN)
    yield
    s1 = own(1)
    a2 = net.along(s1, IN)
    b2 = net.along(add(s0, a1), MID)
    yield
    s2 = own(2)
    a3 = net.along(s2, IN)
    b3 = net.along(add(s1, a2), MID)
    c3 = net.along(add(s2, b2), OUT)
    yield
    total = add(own(3), a3, b3, c3)
    if not across:
        half = total.shape[0] // 2
        total = add(total[:half], net.across(total[half:]))
    yield total


def shards(tokens, lengths, cotangent, attend_gain, attend_shift, joint_weight, joint_bias, output_weight,
           output_bias, feed_gain, feed_shift, up_weight, up_bias, down_weight, down_bias):
    n = lax.axis_size("dp")
    r = D // n
    lined = n == 8
    nk = n if lined else 1
    sections = lax.axis_size("section")
    stages = sections // 2
    index = lax.axis_index("section")
    core, stage = index % 2, index // 2
    seq = tokens.shape[1]
    spot = lax.axis_index("dp")
    z = spot // 2
    middle = (z == 1) | (z == 2)
    if lined:
        packed, pair = pack(joint_weight[0], output_weight[0], up_weight[0], down_weight[0], attend_gain, attend_shift,
                            joint_bias, output_bias, feed_gain, feed_shift, down_bias, up_bias)
        wa, wb = gather_blocks(packed, pair, middle)
    else:
        tail = vector_tail(n, spot, attend_gain[0], attend_shift[0], joint_bias[0], output_bias[0], feed_gain[0],
                           feed_shift[0], down_bias[0], up_bias[0])
        packed = pack_shard(joint_weight[0], output_weight[0], up_weight[0], down_weight[0], tail)
        gathered = lax.all_gather(packed, "dp")
        tails = lax.psum(tail.astype(BF).astype(F32), "dp")
        wa, wb = kernel_form(n, gathered, tails), kernel_form(n, swapped(gathered), swapped(tails))

    def own_pair(a):
        return lax.dynamic_index_in_dim(a, core, 0, False)

    def padded(a):
        return jnp.pad(a, ((0, ROWS - seq), (0, 0)))

    places = lax.broadcasted_iota(jnp.int32, (8, ROWS), 1)
    mask = (((places < own_pair(lengths)) | (places >= CAPTION)) & (places < seq)).astype(F32)
    own_tokens = padded(own_pair(tokens))
    own_cotangent = padded(own_pair(cotangent))

    x = own_tokens
    for t in range(stages):
        last = t == stages - 1
        got = forward_stage(last, x, mask, wa, wb)
        if not last:
            x = jnp.where(stage == 0, own_tokens, moved(got[1], "section", 2))
    leaving = got[1]
    saved = [(x, *got[2:6]), (got[0], *got[8:12])]
    kept = [got[6], got[12]]
    received = [swapped(got[7]), swapped(got[13])]

    g = own_cotangent
    for t in range(stages - 1):
        g = backward_layers(False, (1, 0), g, mask, saved, wa, wb, None)[0]
        g = jnp.where(stage == stages - 1, own_cotangent, moved(g, "section", -2))
    products, operands = [None, None], [None, None]
    behind = mask
    for s in (1, 0):
        g, gv, bk, bs = backward_layers(True, (s,), g, mask, saved, wa, wb, behind)
        operands[s] = gv, kept[s], bk, received[s], swapped(bs)
    behind = g
    for s in (1, 0):
        products[s] = list(weight_products(nk, 0 if lined else 0, behind, *operands[s]))
        behind = products[s][0]

    g, products[0][-1] = lax.optimization_barrier((g, products[0][-1]))
    ends = jnp.where(stage == 0, g, leaving)[:seq].reshape(seq, stages, 2, D // sections)
    kept_half = lax.dynamic_index_in_dim(ends, stage, 1, False)
    got_half = flipped(lax.dynamic_index_in_dim(ends, 1 - stage, 1, False), 2)
    halves = jnp.stack([jnp.where(stage == 0, got_half, kept_half), jnp.where(stage == 0, kept_half, got_half)])
    kept_part = lax.dynamic_index_in_dim(halves, core, 2, False)
    got_part = flipped(lax.dynamic_index_in_dim(halves, 1 - core, 2, False), 1)
    parts = jnp.stack([jnp.where(core == 0, kept_part, got_part), jnp.where(core == 0, got_part, kept_part)], axis=1)

    reduced = [None, None]
    if lined:
        net = Links(x=1, z=9)
        products[1][5], products[0][0] = lax.optimization_barrier((products[1][5], products[0][0]))
        reduced[1] = list(scatter_steps(net, products[1], True))[-1]
        reduced[0], parts = scatter_rounds(products[0], None, parts)
    else:
        for s in range(2):
            p = products[s][0]
            col = jnp.swapaxes(p[:HALF * D].reshape(HALF, n, r, D), 0, 1).reshape(n, HALF * r, D)
            row = jnp.concatenate([p[:4 * D].reshape(n, 4 * r, D), col[:, 4 * r:]], axis=1)
            total = lax.psum_scatter(jnp.where(core == 0, col, row), "dp", scatter_dimension=0)
            reduced[s] = jnp.concatenate([total, lax.psum(p[HALF * D:], "dp")])
    sent = [lax.ppermute(reduced[s], "section", [(i, i ^ 1) for i in range(sections) if i % 2 != s]) for s in range(2)]
    keep = jnp.where(core == 0, reduced[0], reduced[1])
    away = jnp.where(core == 0, sent[0], sent[1])
    first = jnp.where(core == 0, keep, away).astype(F32)
    second = jnp.where(core == 0, away, keep).astype(F32)
    grad_up = jnp.concatenate([first[k * r:(k + 1) * r] for k in range(4)], axis=1)
    grad_joint = jnp.concatenate([first[4 * r:5 * r], first[5 * r:6 * r], second[5 * r:6 * r]], axis=1)
    grad_down = second[:4 * r]
    grad_out = second[4 * r:5 * r]
    v = first[6 * r:] + second[6 * r:]
    half, quarter = n // 2, n // 4
    vec = lax.dynamic_slice(v, (0, r * spot), (16, r))
    grad_jb = lax.dynamic_slice(v, (BQ + spot // half, 2 * r * (spot % half)), (1, 2 * r))
    grad_ub = lax.dynamic_slice(v, (UB + spot // quarter, 4 * r * (spot % quarter)), (1, 4 * r))
    outputs, token_grad = parts[0], parts[1]
    return (outputs, token_grad, vec[AG:AG + 1], vec[AS:AS + 1], grad_joint[None], grad_jb, grad_out[None],
            vec[OB:OB + 1], vec[FG:FG + 1], vec[FS:FS + 1], grad_up[None], grad_ub, grad_down[None], vec[DB:DB + 1])


def solution(mesh):
    vec, mat = P("section", "dp"), P("section", "dp", None)
    rows = P("dp", None, None)
    out = P("dp", None, "section")
    return jax.shard_map(
        shards,
        mesh=mesh,
        in_specs=(rows, P("dp"), rows, vec, vec, mat, vec, mat, vec, vec, vec, mat, vec, mat, vec),
        out_specs=(out, out, vec, vec, mat, vec, mat, vec, vec, vec, mat, vec, mat, vec),
        check_vma=False,
    )
```

```python
import functools

import jax
import jax.numpy as jnp
from jax import lax
from jax.experimental import pallas as pl
from jax.experimental.pallas import tpu as pltpu
from jax.sharding import PartitionSpec as P

D = 768
HEADS = 12
FF = 3072
CAPTION = 40
ROWS = 288
HALF = 6
TAIL = 16
EPS = 1e-6
BF = jnp.bfloat16
F32 = jnp.float32
PAIRED = 2 * (D // HEADS)
VMEM_LIMIT = 60 * 2**20
WIDE = FF + 2 * D
AG, AS, BQ, BV, OB, FG, FS, DB, UB = 0, 1, 2, 3, 4, 5, 6, 7, 8

ANYS = pl.BlockSpec(memory_space=pl.ANY)
VM = pl.BlockSpec(memory_space=pltpu.VMEM)


def dot(a, b, ca=1, cb=0):
    return lax.dot_general(a, b, (((ca,), (cb,)), ((), ())), preferred_element_type=F32)


def spread_of(v):
    mean = jnp.mean(v, axis=-1, keepdims=True)
    cent = v - mean
    return cent, lax.rsqrt(jnp.mean(cent * cent, axis=-1, keepdims=True) + EPS)


def here():
    spot, core = lax.axis_index("dp"), lax.axis_index("section") % 2
    z, column = spot // 2, spot % 2
    middle = jnp.where((z == 1) | (z == 2), 1, 0)
    return [core, 1 - core, z, column, middle, core, 2 + middle]


def sending_slots(z, column):
    orders = ((3, 2, 1, 0), (2, 3, 1, 0), (0, 1, 3, 2), (0, 1, 2, 3))
    slots = []
    for j in range(8):
        a, b, c, d = (o[j // 2] for o in orders)
        slot = jnp.where(z == 0, a, jnp.where(z == 1, b, jnp.where(z == 2, c, d)))
        slots.append(slot + jnp.where(column == j % 2, 0, 4))
    return slots


def square(block):
    return block.reshape(D, D)


def weight_scratch(count):
    n, r, per = (8, D // 8, 2) if count > 1 else (1, D, 1)
    return [pltpu.VMEM((8, n, r, D), BF), pltpu.VMEM((4, per, D // per, D), BF), pltpu.VMEM((n, TAIL, D), BF),
            pltpu.SemaphoreType.DMA((13,))]


def start_weights(which, info, sets, scratch, order):
    wv, wd, tv, sems = scratch
    r = wv.shape[2]

    def start(block, j, part):
        if len(sets[0]) == 1:
            rows = block.at[pl.ds(part * r, r if part < 12 else TAIL)]
            dst = wv.at[part, 0] if part < 8 else wd.at[part - 8, 0] if part < 12 else tv.at[0]
            pltpu.make_async_copy(rows, dst, sems.at[part]).start()
        elif part == 12:
            pltpu.make_async_copy(block.at[pl.ds(10 * r, TAIL)], tv.at[j], sems.at[12]).start()
        elif part < 6:
            pltpu.make_async_copy(block.at[pl.ds(part * r, r)], wv.at[part, j], sems.at[part]).start()
        elif part == 8:
            b = j // 2
            pltpu.make_async_copy(block.at[pl.ds(6 * r, 4 * r)], wd.at[b, j % 2], sems.at[8 + b]).start()

    for number, blocks in enumerate(sets):

        @pl.when(info[which] == number)
        def _():
            if len(blocks) == 1:
                for part in order:
                    start(blocks[0], 0, part)
                return
            lines = [info[2], info[2] ^ 1, info[2] ^ info[6], info[2] ^ (info[6] ^ 1)]
            spots = [(blocks[4 * far + k], lines[k] * 2 + (info[3] ^ far)) for far in (0, 1) for k in range(4)]
            for part in order:
                if part in (6, 7):
                    for far in (0, 1):
                        for k in range(4):
                            rows = blocks[8 + k].at[pl.ds((2 * far + part - 6) * r, r)]
                            pltpu.make_async_copy(rows, wv.at[part, lines[k] * 2 + (info[3] ^ far)], sems.at[part]).start()
                    continue
                for block, j in spots:
                    start(block, j, part)

    waits = [pltpu.make_async_copy(wv.at[k], wv.at[k], sems.at[k]) for k in range(8)]
    waits += [pltpu.make_async_copy(wd.at[b], wd.at[b], sems.at[8 + b]) for b in range(4)]
    return waits + [pltpu.make_async_copy(tv, tv, sems.at[12])]


def vectors(tv):
    total = tv[0].astype(F32)
    for j in range(1, tv.shape[0]):
        total = total + tv[j].astype(F32)
    return total


def handing(core, keep, send, sems, waits):
    def hand_on(src, first, at):
        wide = src.shape[1]
        sem = sems.at[len(waits)]
        mine = (core == 0) == first

        @pl.when(mine)
        def _():
            pltpu.make_async_copy(src, keep.at[:, pl.ds(at, wide)], sem).start()

        @pl.when(jnp.logical_not(mine))
        def _():
            pltpu.make_async_copy(src, send.at[:, pl.ds(at, wide)], sem).start()

        waits.append(pltpu.make_async_copy(src, keep.at[:, pl.ds(at, wide)], sem))

    return hand_on


def forward_one(save, core, x, usable, copies, scratch, work, osems, saved, outs):
    wv, wd, tv, _ = scratch
    jn, ctx, act, gp, nrm, nt, vec = work
    if save:
        lse_ref, mid_ref, j_hbm, gp_hbm, keep, send = saved
        hand_on = handing(core, keep, send, osems, outs)

        def flush(src, dst):
            c = pltpu.make_async_copy(src, dst, osems.at[len(outs)])
            c.start()
            outs.append(c)

    copies[12].wait()
    vec[...] = vectors(tv)
    cent, inv = spread_of(x)
    nrm[...] = (cent * inv * vec[AG:AG + 1, :] + vec[AS:AS + 1, :]).astype(BF)
    if save:
        hand_on(nrm, True, D)
        hand_on(nrm, False, FF + D)
    for k in range(3):
        copies[k].wait()
        r = dot(nrm[...], square(wv[k]))
        if k == 0:
            r = r + vec[BQ:BQ + 1, :]
        if k == 2:
            r = r + vec[BV:BV + 1, :]
        jn[:, k * D:(k + 1) * D] = r.astype(BF)
    if save:
        flush(jn, j_hbm)
    lane = lax.broadcasted_iota(jnp.int32, (ROWS, PAIRED), 1)
    low = lane < PAIRED // 2
    lse = jnp.zeros((ROWS, PAIRED), F32)
    for i in range(HEADS // 2):
        at = i * PAIRED
        q2 = jn[:, at:at + PAIRED] * BF(0.125)
        k2 = jn[:, D + at:D + at + PAIRED]
        v2 = jn[:, 2 * D + at:2 * D + at + PAIRED]
        zero = jnp.zeros_like(q2)
        both = []
        for h in range(2):
            s = dot(jnp.where(low == (h == 0), q2, zero), k2, 1, 1)
            s = jnp.where(usable, s, -1e30)
            top = jnp.max(s, axis=-1, keepdims=True)
            e = jnp.exp(s - top)
            total = jnp.sum(e, axis=-1, keepdims=True)
            both.append(dot(e.astype(BF), v2) * (1.0 / total))
            if save:
                lse = jnp.where(lane == 2 * i + h, top + jnp.log(total), lse)
        ctx[:, at:at + PAIRED] = jnp.where(low, both[0], both[1]).astype(BF)
    if save:
        lse_ref[...] = lse
        hand_on(ctx, False, FF)
    for k in range(3, 12):
        copies[k].wait()
    middle = x + dot(ctx[...], square(wv[3])) + vec[OB:OB + 1, :]
    if save:
        mid_ref[...] = middle
    cent, inv = spread_of(middle)
    nt[...] = (cent * inv * vec[FG:FG + 1, :] + vec[FS:FS + 1, :]).astype(BF)
    if save:
        hand_on(nt, True, 0)
    acc = middle + vec[DB:DB + 1, :]
    for b in range(4):
        cols = slice(b * D, (b + 1) * D)
        h = dot(nt[...], square(wv[4 + b])) + vec[UB + b:UB + b + 1, :]
        phi = 0.5 + 0.5 * lax.erf(h * (0.5**0.5))
        a = (h * phi).astype(BF)
        if save:
            act[:, cols] = a
            gp[:, cols] = (phi + h * jnp.exp(-0.5 * h * h) * 0.3989422804014327).astype(BF)
        acc = acc + dot(a, square(wd[b]))
    if save:
        hand_on(act, False, 0)
        flush(gp, gp_hbm)
    return acc.astype(BF)


def forward_kernel(save, count, x_ref, came_ref, mask_ref, *rest):
    info = here()
    sets, rest = (rest[:count], rest[count:2 * count]), rest[2 * count:]
    wide = 15 if save else 2
    results, rest = rest[:wide], rest[wide:]
    scratch = [rest[0:4], rest[4:8]]
    rest = rest[8:]
    copies = [start_weights(s, info, sets, scratch[s], (12,) + tuple(range(12))) for s in range(2)]
    usable = mask_ref[0:1, :] > 0.5
    outs = []
    x = x_ref[...]
    if save:
        x = jnp.where(lax.axis_index("section") < 2, x, came_ref[...])
        results[14][...] = x
    for s in range(2):
        work, rest = rest[:7], rest[7:]
        saved = results[2 + 6 * s:8 + 6 * s] if save else ()
        x = forward_one(save, info[5], x.astype(F32), usable, copies[s], scratch[s], work, rest[7 * (1 - s)], saved, outs)
        results[s][...] = x
    for c in outs:
        c.wait()


def forward_stage(save, x, came, mask, wa, wb):
    def sd(cols, t=BF):
        return jax.ShapeDtypeStruct((ROWS, cols), t)

    shapes, specs = [sd(D)] * 2, [VM] * 2
    if save:
        shapes += [sd(PAIRED, F32), sd(D, F32), sd(3 * D), sd(FF), sd(WIDE), sd(WIDE)] * 2
        specs += ([VM, VM] + [ANYS] * 4) * 2
        shapes.append(sd(D))
        specs.append(VM)
    work = [pltpu.VMEM((ROWS, 3 * D), BF), pltpu.VMEM((ROWS, D), BF), pltpu.VMEM((ROWS, FF), BF),
            pltpu.VMEM((ROWS, FF), BF), pltpu.VMEM((ROWS, D), BF), pltpu.VMEM((ROWS, D), BF), pltpu.VMEM((16, D), F32)]
    return pl.pallas_call(
        functools.partial(forward_kernel, save, len(wa)),
        out_shape=shapes,
        in_specs=[VM, VM, VM] + [ANYS] * (2 * len(wa)),
        out_specs=specs,
        scratch_shapes=weight_scratch(len(wa)) * 2 + work * 2 + [pltpu.SemaphoreType.DMA((14,))],
        compiler_params=pltpu.CompilerParams(vmem_limit_bytes=VMEM_LIMIT),
        cost_estimate=pl.CostEstimate(flops=2 * ROWS * D * D * 26, bytes_accessed=48 * D * D + 2**23, transcendentals=0),
        name="forward_stage",
    )(x, came, mask, *wa, *wb)


def backward_one(save, core, g_ref, x_ref, lse_ref, mid_ref, j_hbm, gp_hbm, usable, copies, scratch, work, isems, osems, results,
                 waits):
    wv, wd, tv, _ = scratch
    jn, gp, dh, dj, b1, vec = work
    hand_on = lambda *a: None
    if save:
        gv_ref, keep_hbm, send_hbm = results
        hand_on = handing(core, keep_hbm, send_hbm, osems, waits)
    hand_on(g_ref, False, 0)
    copies[12].wait()
    vec[...] = vectors(tv)
    d_nt = None
    for b in range(4):
        cols = slice(b * D, (b + 1) * D)
        copies[8 + b].wait()
        if b == 0:
            pltpu.make_async_copy(gp_hbm, gp, isems.at[0]).wait()
        da = dot(g_ref[...], square(wd[b]), 1, 1)
        d = (da * gp[:, cols].astype(F32)).astype(BF)
        dh[:, cols] = d
        copies[4 + b].wait()
        part = dot(d, square(wv[4 + b]), 1, 1)
        d_nt = part if d_nt is None else d_nt + part
    hand_on(dh, True, 0)

    def norm_back(v, dy, gain, row):
        cent, inv = spread_of(v)
        hat = cent * inv
        if save:
            gv_ref[row:row + 1, :] = jnp.sum(dy * hat, axis=0, keepdims=True)
            gv_ref[row + 1:row + 2, :] = jnp.sum(dy, axis=0, keepdims=True)
        t = dy * gain
        return inv * (t - jnp.mean(t, axis=-1, keepdims=True) - hat * jnp.mean(t * hat, axis=-1, keepdims=True))

    d_mid = g_ref[...].astype(F32) + norm_back(mid_ref[...], d_nt, vec[FG:FG + 1, :], FG)
    b1[...] = d_mid.astype(BF)
    hand_on(b1, False, D)
    if save:
        for b in range(4):
            gv_ref[UB + b:UB + b + 1, :] = jnp.sum(dh[:, b * D:(b + 1) * D].astype(F32), axis=0, keepdims=True)
        gv_ref[DB:DB + 1, :] = jnp.sum(g_ref[...].astype(F32), axis=0, keepdims=True)
        gv_ref[OB:OB + 1, :] = jnp.sum(b1[...].astype(F32), axis=0, keepdims=True)
    copies[3].wait()
    d_ctx = dot(b1[...], square(wv[3]), 1, 1).astype(BF)
    pltpu.make_async_copy(j_hbm, jn, isems.at[1]).wait()
    for k in range(3):
        copies[k].wait()
    lane = lax.broadcasted_iota(jnp.int32, (ROWS, PAIRED), 1)
    low = lane < PAIRED // 2
    for i in range(HEADS // 2):
        at = i * PAIRED
        q2 = jn[:, at:at + PAIRED] * BF(0.125)
        k2 = jn[:, D + at:D + at + PAIRED]
        v2 = jn[:, 2 * D + at:2 * D + at + PAIRED]
        do2 = d_ctx[:, at:at + PAIRED]
        zero = jnp.zeros_like(q2)
        res = []
        for h in range(2):
            here = low == (h == 0)
            s = dot(jnp.where(here, q2, zero), k2, 1, 1)
            p = jnp.where(usable, jnp.exp(s - lse_ref[:, 2 * i + h:2 * i + h + 1]), 0.0)
            dp = dot(jnp.where(here, do2, zero), v2, 1, 1)
            inner = jnp.sum(p * dp, axis=-1, keepdims=True)
            dsc = (p * (dp - inner)).astype(BF)
            res.append((dot(dsc, k2) * 0.125, dot(dsc, q2, 0, 0), dot(p.astype(BF), do2, 0, 0)))
        for c in range(3):
            dj[:, c * D + at:c * D + at + PAIRED] = jnp.where(low, res[0][c], res[1][c]).astype(BF)
    hand_on(dj.at[:, pl.ds(0, 2 * D)], True, FF)
    hand_on(dj.at[:, pl.ds(2 * D, D)], False, 2 * D)
    if save:
        gv_ref[BQ:BQ + 1, :] = jnp.sum(dj[:, :D].astype(F32), axis=0, keepdims=True)
        gv_ref[BV:BV + 1, :] = jnp.sum(dj[:, 2 * D:].astype(F32), axis=0, keepdims=True)
        gv_ref[UB + 4:, :] = jnp.zeros((4, D), F32)
    d_n = dot(dj[:, :D], square(wv[0]), 1, 1)
    for k in (1, 2):
        d_n = d_n + dot(dj[:, k * D:(k + 1) * D], square(wv[k]), 1, 1)
    return (d_mid + norm_back(x_ref[...].astype(F32), d_n, vec[AG:AG + 1, :], AG)).astype(BF)


def backward_kernel(save, layers, count, g_ref, mask_ref, *rest):
    info = here()
    m = len(layers)
    kept, rest = [rest[5 * i:5 * i + 5] for i in range(m)], rest[5 * m:]
    rest = rest[1:] if save else rest
    sets, rest = (rest[:count], rest[count:2 * count]), rest[2 * count:]
    wide = 4 if save else 1
    results, rest = rest[:wide], rest[wide:]
    scratch, rest = [rest[4 * i:4 * i + 4] for i in range(m)], rest[4 * m:]
    work, (gs, isems, osems) = [rest[6 * i:6 * i + 6] for i in range(m)], rest[6 * m:]
    copies = []
    for i in range(m):
        pltpu.make_async_copy(kept[i][4], work[i][1], isems.at[i, 0]).start()
        copies.append(start_weights(layers[i], info, sets, scratch[i], (12, 8, 9, 10, 11, 4, 5, 6, 7, 3, 0, 1, 2)))
        pltpu.make_async_copy(kept[i][3], work[i][0], isems.at[i, 1]).start()
    usable = mask_ref[0:1, :] > 0.5
    waits = []
    for i in range(m):
        x_ref, lse_ref, mid_ref, j_hbm, gp_hbm = kept[i]
        g = backward_one(save, info[5], g_ref if i == 0 else gs, x_ref, lse_ref, mid_ref, j_hbm, gp_hbm, usable, copies[i],
                         scratch[i], work[i], isems.at[i], osems, results[1:], waits)
        if i + 1 < m:
            gs[...] = g
        else:
            results[0][...] = g
    for c in waits:
        c.wait()


def backward_layers(save, layers, g, mask, saved, wa, wb, behind):
    def sd(cols, t=BF, rows=ROWS):
        return jax.ShapeDtypeStruct((rows, cols), t)

    shapes, specs = [sd(D)], [VM]
    if save:
        shapes += [sd(D, F32, 16), sd(WIDE), sd(WIDE)]
        specs += [VM, ANYS, ANYS]
    m = len(layers)
    work = [pltpu.VMEM((ROWS, 3 * D), BF), pltpu.VMEM((ROWS, FF), BF), pltpu.VMEM((ROWS, FF), BF),
            pltpu.VMEM((ROWS, 3 * D), BF), pltpu.VMEM((ROWS, D), BF), pltpu.VMEM((16, D), F32)]
    kept = [a for s in layers for a in saved[s]]
    return pl.pallas_call(
        functools.partial(backward_kernel, save, layers, len(wa)),
        out_shape=shapes,
        in_specs=[VM, VM] + [VM, VM, VM, ANYS, ANYS] * m + [ANYS] * (save + 2 * len(wa)),
        out_specs=specs,
        scratch_shapes=weight_scratch(len(wa)) * m + work * m + [
            pltpu.VMEM((ROWS, D), BF), pltpu.SemaphoreType.DMA((m, 2)), pltpu.SemaphoreType.DMA((5,))],
        compiler_params=pltpu.CompilerParams(vmem_limit_bytes=VMEM_LIMIT),
        cost_estimate=pl.CostEstimate(flops=2 * ROWS * D * D * 14 * m, bytes_accessed=m * (24 * D * D + 2**23), transcendentals=0),
        name="backward_layers",
    )(g, mask, *kept, *([behind] if save else []), *wa, *wb)


def product_kernel(n, direct, behind, gv, fk_hbm, bk_hbm, fr_hbm, br_hbm, *rest):
    wide = n + 4 * (direct > 0)
    outs, rest = rest[:wide], rest[wide:]
    f, b, held, isems, osems = rest[:5]
    info = here()
    slots = sending_slots(info[2], info[3]) if n > 1 else [0]
    r = D // n
    flat = HALF - direct
    loads = {}

    def load(first, core):
        mine = range(2 if core == 0 else HALF) if first else range(HALF if core == 0 else 3)
        for k in mine:
            dst, own, other = (f, fk_hbm, fr_hbm) if first else (b, bk_hbm, br_hbm)
            sem = isems.at[0 if first else 1, k]
            for half, src in enumerate((own, other)):
                pltpu.make_async_copy(src.at[:, pl.ds(k * D, D)], dst.at[k, pl.ds(half * ROWS, ROWS)], sem).start()
            loads[core, first, k] = pltpu.make_async_copy(dst.at[k], dst.at[k], sem)

    def operand(first, core, k):
        wait = loads.pop((core, first, k), None)
        if wait is not None:
            wait.wait()
        return (f if first else b)[k]

    for j in range(n):
        held[j, flat * r:] = gv[...].astype(BF)
        pltpu.make_async_copy(held.at[j, pl.ds(flat * r, TAIL)], outs[j].at[pl.ds(flat * r, TAIL)], osems.at[0]).start()

    def store(c, val):
        if c >= flat:
            for j in range(n):
                rest[5][slots[j] % 4, slots[j] // 4, (c - flat) * r:(c - flat + 1) * r] = val[j * r:(j + 1) * r]
            if c == HALF - 1:
                for k in range(4):
                    for far in (0, 1):
                        rows = pl.ds(far * direct * r, direct * r)
                        pltpu.make_async_copy(rest[5].at[k, far], outs[n + k].at[rows], osems.at[0]).start()
            return
        for j in range(n):
            held[slots[j], c * r:(c + 1) * r] = val[j * r:(j + 1) * r]
        for j in range(n):
            rows = pl.ds(c * r, r)
            pltpu.make_async_copy(held.at[j, rows], outs[j].at[rows], osems.at[0]).start()

    def store_rows(c, val):
        for i in range(n // 4):
            held[slots[c * (n // 4) + i], :4 * r] = val[i * 4 * r:(i + 1) * 4 * r]
        if c == 3:
            for j in range(n):
                rows = pl.ds(0, 4 * r)
                pltpu.make_async_copy(held.at[j, rows], outs[j].at[rows], osems.at[0]).start()

    @pl.when(info[5] == 0)
    def _():
        load(True, 0)
        load(False, 0)
        for c in range(HALF):
            val = dot(operand(True, 0, 0 if c < 4 else 1), operand(False, 0, c), 0, 0).astype(BF)
            store(c, val)

    @pl.when(info[5] != 0)
    def _():
        load(False, 1)
        load(True, 1)
        for c in range(HALF):
            val = dot(operand(True, 1, c), operand(False, 1, 0 if c < 4 else c - 3), 0, 0).astype(BF)
            if c < 4 and n > 1:
                store_rows(c, val)
            else:
                store(c, val)

    for j in range(n):
        pltpu.make_async_copy(held.at[j], outs[j], osems.at[0]).wait()
    if direct:
        pltpu.make_async_copy(rest[5], rest[5], osems.at[0]).wait()


def weight_products(n, direct, behind, gv, fk, bk, fr, br):
    shape = ((HALF - direct) * (D // n) + TAIL, D)
    shapes = [jax.ShapeDtypeStruct(shape, BF)] * n
    scratch = [pltpu.VMEM((HALF, 2 * ROWS, D), BF), pltpu.VMEM((HALF, 2 * ROWS, D), BF), pltpu.VMEM((n,) + shape, BF),
               pltpu.SemaphoreType.DMA((2, HALF)), pltpu.SemaphoreType.DMA((1,))]
    if direct:
        shapes += [jax.ShapeDtypeStruct((2 * direct * (D // n), D), BF)] * 4
        scratch.append(pltpu.VMEM((4, 2, direct * (D // n), D), BF))
    return pl.pallas_call(
        functools.partial(product_kernel, n, direct),
        out_shape=shapes,
        in_specs=[ANYS, VM] + [ANYS] * 4,
        out_specs=[ANYS] * len(shapes),
        scratch_shapes=scratch,
        compiler_params=pltpu.CompilerParams(vmem_limit_bytes=VMEM_LIMIT),
        cost_estimate=pl.CostEstimate(flops=2 * 2 * ROWS * D * D * 6, bytes_accessed=2**24, transcendentals=0),
        name="weight_products",
    )(behind, gv, fk, bk, fr, br)


def pack_kernel(joint, output, up, down, ag, as_, jb, ob, fg, fs, db, ub, block_ref, pair_ref):
    r = output.shape[0]
    spot = lax.axis_index("dp")
    for k in range(3):
        block_ref[k * r:(k + 1) * r, :] = joint[:, k * D:(k + 1) * D].astype(BF)
    block_ref[3 * r:4 * r, :] = output[...].astype(BF)
    for k in range(2):
        block_ref[(4 + k) * r:(5 + k) * r, :] = up[:, k * D:(k + 1) * D].astype(BF)
        pair_ref[k * r:(k + 1) * r, :] = up[:, (2 + k) * D:(3 + k) * D].astype(BF)
    block_ref[6 * r:10 * r, :] = down[...].astype(BF)

    def placed(ref, at):
        wide = ref.shape[1]
        lane = lax.broadcasted_iota(jnp.int32, (wide, D), 1)
        entry = lax.broadcasted_iota(jnp.int32, (wide, D), 0)
        return dot(ref[...].astype(BF), (lane == entry + at * wide).astype(BF))

    zero = jnp.zeros((1, D), F32)
    jrow = placed(jb, spot % 4)
    urow = placed(ub, spot % 2)
    rows = [placed(ag, spot), placed(as_, spot)]
    rows += [jnp.where(spot // 4 == k, jrow, zero) for k in range(2)]
    rows += [placed(v, spot) for v in (ob, fg, fs, db)]
    rows += [jnp.where(spot // 2 == k, urow, zero) for k in range(4)] + [zero] * 4
    block_ref[10 * r:, :] = jnp.concatenate(rows).astype(BF)


def pack(*params):
    r = params[1].shape[0]
    return pl.pallas_call(
        pack_kernel,
        out_shape=[jax.ShapeDtypeStruct((10 * r + TAIL, D), BF), jax.ShapeDtypeStruct((2 * r, D), BF)],
        in_specs=[VM] * 12,
        out_specs=[VM, VM],
        compiler_params=pltpu.CompilerParams(vmem_limit_bytes=VMEM_LIMIT),
        name="pack",
    )(*params)


def finish_kernel(red0, red1, sent0, sent1, up, joint, out, down, ag, as_, jb, ob, fg, fs, db, ub):
    r = out.shape[0]
    spot, core = lax.axis_index("dp"), lax.axis_index("section") % 2

    def taken(rows, wide, at):
        entry = lax.broadcasted_iota(jnp.int32, (D, wide), 0)
        lane = lax.broadcasted_iota(jnp.int32, (D, wide), 1)
        pick = (entry == lane + at * wide).astype(F32)
        return lax.dot_general(rows, pick, (((1,), (0,)), ((), ())), precision=lax.Precision.HIGHEST,
                               preferred_element_type=F32)

    def write(a, b):
        for k in range(4):
            up[:, k * D:(k + 1) * D] = a[k * r:(k + 1) * r, :].astype(F32)
        for k in range(2):
            joint[:, k * D:(k + 1) * D] = a[(4 + k) * r:(5 + k) * r, :].astype(F32)
        joint[:, 2 * D:] = b[5 * r:6 * r, :].astype(F32)
        down[...] = b[:4 * r, :].astype(F32)
        out[...] = b[4 * r:5 * r, :].astype(F32)
        v = a[6 * r:, :].astype(F32) + b[6 * r:, :].astype(F32)
        own = taken(v, r, spot)
        for ref, row in ((ag, AG), (as_, AS), (ob, OB), (fg, FG), (fs, FS), (db, DB)):
            ref[...] = own[row:row + 1]
        half = taken(v, 2 * r, spot % 4)
        jb[...] = jnp.where(spot // 4 == 0, half[BQ:BQ + 1], half[BV:BV + 1])
        most = taken(v, 4 * r, spot % 2)
        place = spot // 2
        ub[...] = jnp.where(place == 0, most[UB:UB + 1], jnp.where(place == 1, most[UB + 1:UB + 2], jnp.where(
            place == 2, most[UB + 2:UB + 3], most[UB + 3:UB + 4])))

    @pl.when(core == 0)
    def _():
        write(red0, sent0)

    @pl.when(core != 0)
    def _():
        write(sent1, red1)


def finish(r, reduced, sent):
    shapes = [(r, FF), (r, 3 * D), (r, D), (4 * r, D), (1, r), (1, r), (1, 2 * r), (1, r), (1, r), (1, r), (1, r), (1, 4 * r)]
    return pl.pallas_call(
        finish_kernel,
        out_shape=[jax.ShapeDtypeStruct(shape, F32) for shape in shapes],
        in_specs=[VM] * 4,
        out_specs=[VM] * 12,
        compiler_params=pltpu.CompilerParams(vmem_limit_bytes=VMEM_LIMIT),
        name="finish",
    )(*reduced, *sent)


def moved(value, axis, by):
    peers = lax.axis_size(axis)
    return lax.ppermute(value, axis, [(i, i + by) for i in range(peers) if 0 <= i + by < peers])


def flipped(value, bit):
    peers = lax.axis_size("section")
    return lax.ppermute(value, "section", [(i, i ^ bit) for i in range(peers)])


def swapped(value):
    return flipped(value, 1)


def vector_tail(n, spot, attend_gain, attend_shift, joint_bias, output_bias, feed_gain, feed_shift, down_bias, up_bias):
    lane = jnp.arange(D)

    def row(v, times, at, live=True):
        return jnp.where((lane // v.shape[0] == at) & live, jnp.tile(v, times), 0.0)

    half, quarter = n // 2, n // 4
    rows = [row(attend_gain, n, spot), row(attend_shift, n, spot)]
    rows += [row(joint_bias, half, spot % half, spot // half == k) for k in range(2)]
    rows += [row(v, n, spot) for v in (output_bias, feed_gain, feed_shift, down_bias)]
    rows += [row(up_bias, quarter, spot % quarter, spot // quarter == k) for k in range(4)]
    return jnp.concatenate([jnp.stack(rows), jnp.zeros((4, D), F32)])


def pack_shard(joint, output, up, down, tail):
    pieces = [joint[:, k * D:(k + 1) * D] for k in range(3)] + [output]
    pieces += [up[:, k * D:(k + 1) * D] for k in range(4)]
    return jnp.concatenate(pieces + [down, tail]).astype(BF)


def kernel_form(n, g, tail):
    r = D // n
    cut = jnp.swapaxes(g[:, :8 * r].reshape(n, 8, r, D), 0, 1).reshape(8 * D, D)
    return [jnp.concatenate([cut, g[:, 8 * r:12 * r].reshape(FF, D), tail.astype(BF)])]


IN, OUT, MID, PAIR = ((0, 1), (3, 2)), ((1, 0), (2, 3)), ((1, 2), (2, 1)), ((0, 1), (1, 0), (2, 3), (3, 2))


class Links:
    def __init__(self, **depth):
        self.depth = {"x": depth["x"], "in": depth["z"], "mid": depth["z"], "out": depth["z"]}
        self.ended = {"x": [], "in": [], "mid": [], "out": []}

    def send(self, value, names, axis, pairs):
        for name in names:
            done = self.ended[name]
            if len(done) >= self.depth[name]:
                value = lax.optimization_barrier((value, done[-self.depth[name]]))[0]
        got = lax.ppermute(value, axis, pairs)
        for name in names:
            self.ended[name].append(got)
        return got

    def along(self, value, moves):
        names = {IN: ("in",), OUT: ("out",), MID: ("mid",), PAIR: ("out",)}[moves]
        return self.send(value, names, "dp", [(2 * a + x, 2 * b + x) for a, b in moves for x in range(2)])

    def across(self, value, core=None):
        if core is None:
            return self.send(value, ("x",), "dp", [(i, i ^ 1) for i in range(8)])
        places = [8 * s + i for s in range(lax.axis_size("section")) if s % 2 == core for i in range(8)]
        return self.send(value, ("x",), ("section", "dp"), [(i, i ^ 1) for i in places])


def gather_blocks(own, pair, middle):
    net = Links(x=1, z=9)
    one, mid = net.along(own, PAIR), net.along(own, MID)
    first = net.across(pair, 0)
    sent = [net.across(own)]
    first = first + net.across(pair, 1)
    both = jnp.concatenate([pair, first])
    far, back = net.along(mid, OUT), net.along(one, MID)
    sent.append(net.across(one))
    both_one, both_mid = net.along(both, PAIR), net.along(both, MID)
    last = net.along(back, OUT)
    third = jnp.where(middle, mid, far)
    sent.append(net.across(third))
    both_far, both_back = net.along(both_mid, OUT), net.along(both_one, MID)
    fourth = jnp.where(middle, back, last)
    sent.append(net.across(fourth))
    both_last = net.along(both_back, OUT)
    mine = [own, one, third, fourth] + sent
    mine += [both, both_one, jnp.where(middle, both_mid, both_far), jnp.where(middle, both_back, both_last)]
    return mine, [swapped(b) for b in mine]


def add(*terms):
    total = terms[0].astype(F32)
    for t in terms[1:]:
        total = total + t.astype(F32)
    return total.astype(BF)


def scatter_both(p, q, extra):
    chain, net = Links(x=1, z=9), Links(x=9, z=9)
    p[5], q[0] = lax.optimization_barrier((p[5], q[0]))
    ps = []
    for k in range(3):
        ps.append(jnp.concatenate([add(p[k], chain.across(p[4 + k])), p[8 + k]]))
        if k == 0:
            pa1 = chain.along(ps[0], IN)
        elif k == 1:
            pa2 = chain.along(ps[1], IN)
            pb2 = chain.along(add(ps[0], pa1), MID)
        else:
            pa3 = chain.along(ps[2], IN)
            pb3 = chain.along(add(ps[1], pa2), MID)
            pc3 = chain.along(add(ps[2], pb2), OUT)
    px3 = chain.across(p[7])
    x0 = net.across(q[4])
    s0 = add(q[0], x0)
    b, s0 = lax.optimization_barrier((q[5], s0))
    x1, a1 = net.across(b), net.along(s0, IN)
    s1, t0 = add(q[1], x1), add(s0, a1)
    b, own, s1, t0, extra = lax.optimization_barrier((q[6], q[7], s1, t0, extra))
    x2, a2, b2, x3 = net.across(b), net.along(s1, IN), net.along(t0, MID), net.across(own)
    s2, t1 = add(q[2], x2), add(s1, a2)
    u = add(s2, b2)
    s2, t1, u = lax.optimization_barrier((s2, t1, u))
    a3, b3, c3 = net.along(s2, IN), net.along(t1, MID), net.along(u, OUT)
    total = add(jnp.concatenate([add(p[3], px3), p[11]]), pa3, pb3, pc3)
    rows, pair = p[3].shape[0], p[11].shape[0] // 2
    late = add(total[rows:rows + pair], net.across(total[rows + pair:]))
    first = jnp.concatenate([total[:rows - TAIL], late, total[rows - TAIL:rows]])
    return first, add(q[3], x3, a3, b3, c3), extra


def shards(tokens, lengths, cotangent, attend_gain, attend_shift, joint_weight, joint_bias, output_weight,
           output_bias, feed_gain, feed_shift, up_weight, up_bias, down_weight, down_bias):
    n = lax.axis_size("dp")
    r = D // n
    lined = n == 8
    nk = n if lined else 1
    sections = lax.axis_size("section")
    stages = sections // 2
    index = lax.axis_index("section")
    core, stage = index % 2, index // 2
    seq = tokens.shape[1]
    spot = lax.axis_index("dp")
    z = spot // 2
    middle = (z == 1) | (z == 2)
    if lined:
        packed, pair = pack(joint_weight[0], output_weight[0], up_weight[0], down_weight[0], attend_gain, attend_shift,
                            joint_bias, output_bias, feed_gain, feed_shift, down_bias, up_bias)
        wa, wb = gather_blocks(packed, pair, middle)
    else:
        tail = vector_tail(n, spot, attend_gain[0], attend_shift[0], joint_bias[0], output_bias[0], feed_gain[0],
                           feed_shift[0], down_bias[0], up_bias[0])
        packed = pack_shard(joint_weight[0], output_weight[0], up_weight[0], down_weight[0], tail)
        gathered = lax.all_gather(packed, "dp")
        tails = lax.psum(tail.astype(BF).astype(F32), "dp")
        wa, wb = kernel_form(n, gathered, tails), kernel_form(n, swapped(gathered), swapped(tails))

    def own_pair(a):
        return lax.dynamic_index_in_dim(a, core, 0, False)

    def padded(a):
        return jnp.pad(a, ((0, ROWS - seq), (0, 0)))

    places = lax.broadcasted_iota(jnp.int32, (8, ROWS), 1)
    mask = (((places < own_pair(lengths)) | (places >= CAPTION)) & (places < seq)).astype(F32)
    own_tokens = padded(own_pair(tokens))
    own_cotangent = padded(own_pair(cotangent))

    came = own_tokens
    for _ in range(stages - 1):
        came = moved(forward_stage(False, came, came, mask, wa, wb)[1], "section", 2)
        if stages > 2:
            came = jnp.where(stage == 0, own_tokens, came)
    got = forward_stage(True, own_tokens, came, mask, wa, wb)
    x, leaving = got[14], got[1]
    saved = [(x, *got[2:6]), (got[0], *got[8:12])]
    kept = [got[6], got[12]]
    received = [swapped(got[7]), swapped(got[13])]

    g = own_cotangent
    for t in range(stages - 1):
        g = backward_layers(False, (1, 0), g, mask, saved, wa, wb, None)[0]
        g = jnp.where(stage == stages - 1, own_cotangent, moved(g, "section", -2))
    products, operands = [None, None], [None, None]
    behind = mask
    for s in (1, 0):
        g, gv, bk, bs = backward_layers(True, (s,), g, mask, saved, wa, wb, behind)
        operands[s] = gv, kept[s], bk, received[s], swapped(bs)
    behind = g
    for s in (1, 0):
        products[s] = list(weight_products(nk, 2 * s if lined else 0, behind, *operands[s]))
        behind = products[s][0]

    g, products[0][-1] = lax.optimization_barrier((g, products[0][-1]))
    ends = jnp.where(stage == 0, g, leaving)[:seq].reshape(seq, stages, 2, D // sections)
    kept_half = lax.dynamic_index_in_dim(ends, stage, 1, False)
    got_half = flipped(lax.dynamic_index_in_dim(ends, 1 - stage, 1, False), 2)
    halves = jnp.stack([jnp.where(stage == 0, got_half, kept_half), jnp.where(stage == 0, kept_half, got_half)])
    kept_part = lax.dynamic_index_in_dim(halves, core, 2, False)
    got_part = flipped(lax.dynamic_index_in_dim(halves, 1 - core, 2, False), 1)
    parts = jnp.stack([jnp.where(core == 0, kept_part, got_part), jnp.where(core == 0, got_part, kept_part)], axis=1)

    reduced = [None, None]
    if lined:
        reduced[1], reduced[0], parts = scatter_both(products[1], products[0], parts)
    else:
        for s in range(2):
            p = products[s][0]
            col = jnp.swapaxes(p[:HALF * D].reshape(HALF, n, r, D), 0, 1).reshape(n, HALF * r, D)
            row = jnp.concatenate([p[:4 * D].reshape(n, 4 * r, D), col[:, 4 * r:]], axis=1)
            total = lax.psum_scatter(jnp.where(core == 0, col, row), "dp", scatter_dimension=0)
            reduced[s] = jnp.concatenate([total, lax.psum(p[HALF * D:], "dp")])
    sent = [lax.ppermute(reduced[s], "section", [(i, i ^ 1) for i in range(sections) if i % 2 != s]) for s in range(2)]
    outputs, token_grad = parts[0], parts[1]
    if lined:
        up, joint, out, down, ag, as_, jb, ob, fg, fs, db, ub = finish(r, reduced, sent)
        return (outputs, token_grad, ag, as_, joint[None], jb, out[None], ob, fg, fs, up[None], ub, down[None], db)
    keep = jnp.where(core == 0, reduced[0], reduced[1])
    away = jnp.where(core == 0, sent[0], sent[1])
    first = jnp.where(core == 0, keep, away).astype(F32)
    second = jnp.where(core == 0, away, keep).astype(F32)
    grad_up = jnp.concatenate([first[k * r:(k + 1) * r] for k in range(4)], axis=1)
    grad_joint = jnp.concatenate([first[4 * r:5 * r], first[5 * r:6 * r], second[5 * r:6 * r]], axis=1)
    grad_down = second[:4 * r]
    grad_out = second[4 * r:5 * r]
    v = first[6 * r:] + second[6 * r:]
    half, quarter = n // 2, n // 4
    vec = lax.dynamic_slice(v, (0, r * spot), (16, r))
    grad_jb = lax.dynamic_slice(v, (BQ + spot // half, 2 * r * (spot % half)), (1, 2 * r))
    grad_ub = lax.dynamic_slice(v, (UB + spot // quarter, 4 * r * (spot % quarter)), (1, 4 * r))
    return (outputs, token_grad, vec[AG:AG + 1], vec[AS:AS + 1], grad_joint[None], grad_jb, grad_out[None],
            vec[OB:OB + 1], vec[FG:FG + 1], vec[FS:FS + 1], grad_up[None], grad_ub, grad_down[None], vec[DB:DB + 1])


def solution(mesh):
    vec, mat = P("section", "dp"), P("section", "dp", None)
    rows = P("dp", None, None)
    out = P("dp", None, "section")
    return jax.shard_map(
        shards,
        mesh=mesh,
        in_specs=(rows, P("dp"), rows, vec, vec, mat, vec, mat, vec, vec, vec, mat, vec, mat, vec),
        out_specs=(out, out, vec, vec, mat, vec, mat, vec, vec, vec, mat, vec, mat, vec),
        check_vma=False,
    )
```

```python
import functools

import jax
import jax.numpy as jnp
from jax import lax
from jax.experimental import pallas as pl
from jax.experimental.pallas import tpu as pltpu
from jax.sharding import PartitionSpec as P

D = 768
HEADS = 12
FF = 3072
CAPTION = 40
ROWS = 288
HALF = 6
TAIL = 16
EPS = 1e-6
BF = jnp.bfloat16
F32 = jnp.float32
PAIRED = 2 * (D // HEADS)
VMEM_LIMIT = 60 * 2**20
WIDE = FF + 2 * D
AG, AS, BQ, BV, OB, FG, FS, DB, UB = 0, 1, 2, 3, 4, 5, 6, 7, 8

ANYS = pl.BlockSpec(memory_space=pl.ANY)
VM = pl.BlockSpec(memory_space=pltpu.VMEM)


def dot(a, b, ca=1, cb=0):
    return lax.dot_general(a, b, (((ca,), (cb,)), ((), ())), preferred_element_type=F32)


def spread_of(v):
    mean = jnp.mean(v, axis=-1, keepdims=True)
    cent = v - mean
    return cent, lax.rsqrt(jnp.mean(cent * cent, axis=-1, keepdims=True) + EPS)


def here():
    spot, core = lax.axis_index("dp"), lax.axis_index("section") % 2
    z, column = spot // 2, spot % 2
    middle = jnp.where((z == 1) | (z == 2), 1, 0)
    return [core, 1 - core, z, column, middle, core, 2 + middle]


def sending_slots(z, column):
    orders = ((3, 2, 1, 0), (2, 3, 1, 0), (0, 1, 3, 2), (0, 1, 2, 3))
    slots = []
    for j in range(8):
        a, b, c, d = (o[j // 2] for o in orders)
        slot = jnp.where(z == 0, a, jnp.where(z == 1, b, jnp.where(z == 2, c, d)))
        slots.append(slot + jnp.where(column == j % 2, 0, 4))
    return slots


def square(block):
    return block.reshape(D, D)


def weight_scratch(count):
    n, r, per = (8, D // 8, 2) if count > 1 else (1, D, 1)
    return [pltpu.VMEM((8, n, r, D), BF), pltpu.VMEM((4, per, D // per, D), BF), pltpu.VMEM((n, TAIL, D), BF),
            pltpu.SemaphoreType.DMA((13,))]


def start_weights(which, info, sets, scratch, order):
    wv, wd, tv, sems = scratch
    r = wv.shape[2]

    def start(block, j, part):
        if len(sets[0]) == 1:
            rows = block.at[pl.ds(part * r, r if part < 12 else TAIL)]
            dst = wv.at[part, 0] if part < 8 else wd.at[part - 8, 0] if part < 12 else tv.at[0]
            pltpu.make_async_copy(rows, dst, sems.at[part]).start()
        elif part == 12:
            pltpu.make_async_copy(block.at[pl.ds(10 * r, TAIL)], tv.at[j], sems.at[12]).start()
        elif part < 6:
            pltpu.make_async_copy(block.at[pl.ds(part * r, r)], wv.at[part, j], sems.at[part]).start()
        elif part == 8:
            b = j // 2
            pltpu.make_async_copy(block.at[pl.ds(6 * r, 4 * r)], wd.at[b, j % 2], sems.at[8 + b]).start()

    for number, blocks in enumerate(sets):

        @pl.when(info[which] == number)
        def _():
            if len(blocks) == 1:
                for part in order:
                    start(blocks[0], 0, part)
                return
            lines = [info[2], info[2] ^ 1, info[2] ^ info[6], info[2] ^ (info[6] ^ 1)]
            spots = [(blocks[4 * far + k], lines[k] * 2 + (info[3] ^ far)) for far in (0, 1) for k in range(4)]
            for part in order:
                if part in (6, 7):
                    for far in (0, 1):
                        for k in range(4):
                            rows = blocks[8 + k].at[pl.ds((2 * far + part - 6) * r, r)]
                            pltpu.make_async_copy(rows, wv.at[part, lines[k] * 2 + (info[3] ^ far)], sems.at[part]).start()
                    continue
                for block, j in spots:
                    start(block, j, part)

    waits = [pltpu.make_async_copy(wv.at[k], wv.at[k], sems.at[k]) for k in range(8)]
    waits += [pltpu.make_async_copy(wd.at[b], wd.at[b], sems.at[8 + b]) for b in range(4)]
    return waits + [pltpu.make_async_copy(tv, tv, sems.at[12])]


def vectors(tv):
    total = tv[0].astype(F32)
    for j in range(1, tv.shape[0]):
        total = total + tv[j].astype(F32)
    return total


def handing(core, keep, send, sems, waits):
    def hand_on(src, first, at):
        wide = src.shape[1]
        sem = sems.at[len(waits)]
        mine = (core == 0) == first

        @pl.when(mine)
        def _():
            pltpu.make_async_copy(src, keep.at[:, pl.ds(at, wide)], sem).start()

        @pl.when(jnp.logical_not(mine))
        def _():
            pltpu.make_async_copy(src, send.at[:, pl.ds(at, wide)], sem).start()

        waits.append(pltpu.make_async_copy(src, keep.at[:, pl.ds(at, wide)], sem))

    return hand_on


def forward_one(save, core, x, usable, copies, scratch, work, osems, saved, outs):
    wv, wd, tv, _ = scratch
    jn, ctx, act, gp, nrm, nt, vec = work
    if save:
        lse_ref, mid_ref, j_hbm, gp_hbm, keep, send = saved
        hand_on = handing(core, keep, send, osems, outs)

        def flush(src, dst):
            c = pltpu.make_async_copy(src, dst, osems.at[len(outs)])
            c.start()
            outs.append(c)

    copies[12].wait()
    vec[...] = vectors(tv)
    cent, inv = spread_of(x)
    nrm[...] = (cent * inv * vec[AG:AG + 1, :] + vec[AS:AS + 1, :]).astype(BF)
    if save:
        hand_on(nrm, True, D)
        hand_on(nrm, False, FF + D)
    for k in range(3):
        copies[k].wait()
        r = dot(nrm[...], square(wv[k]))
        if k == 0:
            r = r + vec[BQ:BQ + 1, :]
        if k == 2:
            r = r + vec[BV:BV + 1, :]
        jn[:, k * D:(k + 1) * D] = r.astype(BF)
    if save:
        flush(jn, j_hbm)
    lane = lax.broadcasted_iota(jnp.int32, (ROWS, PAIRED), 1)
    low = lane < PAIRED // 2
    lse = jnp.zeros((ROWS, PAIRED), F32)
    for i in range(HEADS // 2):
        at = i * PAIRED
        q2 = jn[:, at:at + PAIRED] * BF(0.125)
        k2 = jn[:, D + at:D + at + PAIRED]
        v2 = jn[:, 2 * D + at:2 * D + at + PAIRED]
        zero = jnp.zeros_like(q2)
        both = []
        for h in range(2):
            s = dot(jnp.where(low == (h == 0), q2, zero), k2, 1, 1)
            s = jnp.where(usable, s, -1e30)
            top = jnp.max(s, axis=-1, keepdims=True)
            e = jnp.exp(s - top)
            total = jnp.sum(e, axis=-1, keepdims=True)
            both.append(dot(e.astype(BF), v2) * (1.0 / total))
            if save:
                lse = jnp.where(lane == 2 * i + h, top + jnp.log(total), lse)
        ctx[:, at:at + PAIRED] = jnp.where(low, both[0], both[1]).astype(BF)
    if save:
        lse_ref[...] = lse
        hand_on(ctx, False, FF)
    for k in range(3, 12):
        copies[k].wait()
    middle = x + dot(ctx[...], square(wv[3])) + vec[OB:OB + 1, :]
    if save:
        mid_ref[...] = middle
    cent, inv = spread_of(middle)
    nt[...] = (cent * inv * vec[FG:FG + 1, :] + vec[FS:FS + 1, :]).astype(BF)
    if save:
        hand_on(nt, True, 0)
    acc = middle + vec[DB:DB + 1, :]
    for b in range(4):
        cols = slice(b * D, (b + 1) * D)
        h = dot(nt[...], square(wv[4 + b])) + vec[UB + b:UB + b + 1, :]
        phi = 0.5 + 0.5 * lax.erf(h * (0.5**0.5))
        a = (h * phi).astype(BF)
        if save:
            act[:, cols] = a
            gp[:, cols] = (phi + h * jnp.exp(-0.5 * h * h) * 0.3989422804014327).astype(BF)
            hand_on(act.at[:, pl.ds(b * D, D)], False, b * D)
            flush(gp.at[:, pl.ds(b * D, D)], gp_hbm.at[:, pl.ds(b * D, D)])
        acc = acc + dot(a, square(wd[b]))
    return acc.astype(BF)


def forward_kernel(save, count, x_ref, came_ref, mask_ref, *rest):
    info = here()
    sets, rest = (rest[:count], rest[count:2 * count]), rest[2 * count:]
    wide = 15 if save else 2
    results, rest = rest[:wide], rest[wide:]
    scratch = [rest[0:4], rest[4:8]]
    rest = rest[8:]
    copies = [start_weights(s, info, sets, scratch[s], (12,) + tuple(range(12))) for s in range(2)]
    usable = mask_ref[0:1, :] > 0.5
    outs = []
    x = x_ref[...]
    if save:
        x = jnp.where(lax.axis_index("section") < 2, x, came_ref[...])
        results[14][...] = x
    for s in range(2):
        work, rest = rest[:7], rest[7:]
        saved = results[2 + 6 * s:8 + 6 * s] if save else ()
        x = forward_one(save, info[5], x.astype(F32), usable, copies[s], scratch[s], work, rest[7 * (1 - s)], saved, outs)
        results[s][...] = x
    for c in outs:
        c.wait()


def forward_stage(save, x, came, mask, wa, wb):
    def sd(cols, t=BF):
        return jax.ShapeDtypeStruct((ROWS, cols), t)

    shapes, specs = [sd(D)] * 2, [VM] * 2
    if save:
        shapes += [sd(PAIRED, F32), sd(D, F32), sd(3 * D), sd(FF), sd(WIDE), sd(WIDE)] * 2
        specs += ([VM, VM] + [ANYS] * 4) * 2
        shapes.append(sd(D))
        specs.append(VM)
    work = [pltpu.VMEM((ROWS, 3 * D), BF), pltpu.VMEM((ROWS, D), BF), pltpu.VMEM((ROWS, FF), BF),
            pltpu.VMEM((ROWS, FF), BF), pltpu.VMEM((ROWS, D), BF), pltpu.VMEM((ROWS, D), BF), pltpu.VMEM((16, D), F32)]
    return pl.pallas_call(
        functools.partial(forward_kernel, save, len(wa)),
        out_shape=shapes,
        in_specs=[VM, VM, VM] + [ANYS] * (2 * len(wa)),
        out_specs=specs,
        scratch_shapes=weight_scratch(len(wa)) * 2 + work * 2 + [pltpu.SemaphoreType.DMA((32,))],
        compiler_params=pltpu.CompilerParams(vmem_limit_bytes=VMEM_LIMIT),
        cost_estimate=pl.CostEstimate(flops=2 * ROWS * D * D * 26, bytes_accessed=48 * D * D + 2**23, transcendentals=0),
        name="forward_stage",
    )(x, came, mask, *wa, *wb)


def backward_one(save, core, g_ref, x_ref, lse_ref, mid_ref, j_hbm, gp_hbm, usable, copies, scratch, work, isems, osems, results,
                 waits):
    wv, wd, tv, _ = scratch
    jn, gp, dh, dj, b1, vec = work
    hand_on = lambda *a: None
    if save:
        gv_ref, keep_hbm, send_hbm = results
        hand_on = handing(core, keep_hbm, send_hbm, osems, waits)
    hand_on(g_ref, False, 0)
    copies[12].wait()
    vec[...] = vectors(tv)
    d_nt = None
    for b in range(4):
        cols = slice(b * D, (b + 1) * D)
        copies[8 + b].wait()
        if b == 0:
            pltpu.make_async_copy(gp_hbm, gp, isems.at[0]).wait()
        da = dot(g_ref[...], square(wd[b]), 1, 1)
        d = (da * gp[:, cols].astype(F32)).astype(BF)
        dh[:, cols] = d
        copies[4 + b].wait()
        part = dot(d, square(wv[4 + b]), 1, 1)
        d_nt = part if d_nt is None else d_nt + part
    hand_on(dh, True, 0)

    def norm_back(v, dy, gain, row):
        cent, inv = spread_of(v)
        hat = cent * inv
        if save:
            gv_ref[row:row + 1, :] = jnp.sum(dy * hat, axis=0, keepdims=True)
            gv_ref[row + 1:row + 2, :] = jnp.sum(dy, axis=0, keepdims=True)
        t = dy * gain
        return inv * (t - jnp.mean(t, axis=-1, keepdims=True) - hat * jnp.mean(t * hat, axis=-1, keepdims=True))

    d_mid = g_ref[...].astype(F32) + norm_back(mid_ref[...], d_nt, vec[FG:FG + 1, :], FG)
    b1[...] = d_mid.astype(BF)
    hand_on(b1, False, D)
    if save:
        for b in range(4):
            gv_ref[UB + b:UB + b + 1, :] = jnp.sum(dh[:, b * D:(b + 1) * D].astype(F32), axis=0, keepdims=True)
        gv_ref[DB:DB + 1, :] = jnp.sum(g_ref[...].astype(F32), axis=0, keepdims=True)
        gv_ref[OB:OB + 1, :] = jnp.sum(b1[...].astype(F32), axis=0, keepdims=True)
    copies[3].wait()
    d_ctx = dot(b1[...], square(wv[3]), 1, 1).astype(BF)
    pltpu.make_async_copy(j_hbm, jn, isems.at[1]).wait()
    for k in range(3):
        copies[k].wait()
    lane = lax.broadcasted_iota(jnp.int32, (ROWS, PAIRED), 1)
    low = lane < PAIRED // 2
    for i in range(HEADS // 2):
        at = i * PAIRED
        q2 = jn[:, at:at + PAIRED] * BF(0.125)
        k2 = jn[:, D + at:D + at + PAIRED]
        v2 = jn[:, 2 * D + at:2 * D + at + PAIRED]
        do2 = d_ctx[:, at:at + PAIRED]
        zero = jnp.zeros_like(q2)
        res = []
        for h in range(2):
            here = low == (h == 0)
            s = dot(jnp.where(here, q2, zero), k2, 1, 1)
            p = jnp.where(usable, jnp.exp(s - lse_ref[:, 2 * i + h:2 * i + h + 1]), 0.0)
            dp = dot(jnp.where(here, do2, zero), v2, 1, 1)
            inner = jnp.sum(p * dp, axis=-1, keepdims=True)
            dsc = (p * (dp - inner)).astype(BF)
            res.append((dot(dsc, k2) * 0.125, dot(dsc, q2, 0, 0), dot(p.astype(BF), do2, 0, 0)))
        for c in range(3):
            dj[:, c * D + at:c * D + at + PAIRED] = jnp.where(low, res[0][c], res[1][c]).astype(BF)
    hand_on(dj.at[:, pl.ds(0, 2 * D)], True, FF)
    hand_on(dj.at[:, pl.ds(2 * D, D)], False, 2 * D)
    if save:
        gv_ref[BQ:BQ + 1, :] = jnp.sum(dj[:, :D].astype(F32), axis=0, keepdims=True)
        gv_ref[BV:BV + 1, :] = jnp.sum(dj[:, 2 * D:].astype(F32), axis=0, keepdims=True)
        gv_ref[UB + 4:, :] = jnp.zeros((4, D), F32)
    d_n = dot(dj[:, :D], square(wv[0]), 1, 1)
    for k in (1, 2):
        d_n = d_n + dot(dj[:, k * D:(k + 1) * D], square(wv[k]), 1, 1)
    return (d_mid + norm_back(x_ref[...].astype(F32), d_n, vec[AG:AG + 1, :], AG)).astype(BF)


def backward_kernel(save, layers, count, g_ref, mask_ref, *rest):
    info = here()
    m = len(layers)
    kept, rest = [rest[5 * i:5 * i + 5] for i in range(m)], rest[5 * m:]
    rest = rest[1:] if save else rest
    sets, rest = (rest[:count], rest[count:2 * count]), rest[2 * count:]
    wide = 4 if save else 1
    results, rest = rest[:wide], rest[wide:]
    scratch, rest = [rest[4 * i:4 * i + 4] for i in range(m)], rest[4 * m:]
    work, (gs, isems, osems) = [rest[6 * i:6 * i + 6] for i in range(m)], rest[6 * m:]
    copies = []
    for i in range(m):
        pltpu.make_async_copy(kept[i][4], work[i][1], isems.at[i, 0]).start()
        copies.append(start_weights(layers[i], info, sets, scratch[i], (12, 8, 9, 10, 11, 4, 5, 6, 7, 3, 0, 1, 2)))
        pltpu.make_async_copy(kept[i][3], work[i][0], isems.at[i, 1]).start()
    usable = mask_ref[0:1, :] > 0.5
    waits = []
    for i in range(m):
        x_ref, lse_ref, mid_ref, j_hbm, gp_hbm = kept[i]
        g = backward_one(save, info[5], g_ref if i == 0 else gs, x_ref, lse_ref, mid_ref, j_hbm, gp_hbm, usable, copies[i],
                         scratch[i], work[i], isems.at[i], osems, results[1:], waits)
        if i + 1 < m:
            gs[...] = g
        else:
            results[0][...] = g
    for c in waits:
        c.wait()


def backward_layers(save, layers, g, mask, saved, wa, wb, behind):
    def sd(cols, t=BF, rows=ROWS):
        return jax.ShapeDtypeStruct((rows, cols), t)

    shapes, specs = [sd(D)], [VM]
    if save:
        shapes += [sd(D, F32, 16), sd(WIDE), sd(WIDE)]
        specs += [VM, ANYS, ANYS]
    m = len(layers)
    work = [pltpu.VMEM((ROWS, 3 * D), BF), pltpu.VMEM((ROWS, FF), BF), pltpu.VMEM((ROWS, FF), BF),
            pltpu.VMEM((ROWS, 3 * D), BF), pltpu.VMEM((ROWS, D), BF), pltpu.VMEM((16, D), F32)]
    kept = [a for s in layers for a in saved[s]]
    return pl.pallas_call(
        functools.partial(backward_kernel, save, layers, len(wa)),
        out_shape=shapes,
        in_specs=[VM, VM] + [VM, VM, VM, ANYS, ANYS] * m + [ANYS] * (save + 2 * len(wa)),
        out_specs=specs,
        scratch_shapes=weight_scratch(len(wa)) * m + work * m + [
            pltpu.VMEM((ROWS, D), BF), pltpu.SemaphoreType.DMA((m, 2)), pltpu.SemaphoreType.DMA((5,))],
        compiler_params=pltpu.CompilerParams(vmem_limit_bytes=VMEM_LIMIT),
        cost_estimate=pl.CostEstimate(flops=2 * ROWS * D * D * 14 * m, bytes_accessed=m * (24 * D * D + 2**23), transcendentals=0),
        name="backward_layers",
    )(g, mask, *kept, *([behind] if save else []), *wa, *wb)


def product_kernel(n, direct, behind, gv, fk_hbm, bk_hbm, fr_hbm, br_hbm, *rest):
    wide = n + 4 * (direct > 0)
    outs, rest = rest[:wide], rest[wide:]
    f, b, held, isems, osems = rest[:5]
    info = here()
    slots = sending_slots(info[2], info[3]) if n > 1 else [0]
    r = D // n
    flat = HALF - direct
    loads = {}

    def load(first, core):
        mine = range(2 if core == 0 else HALF) if first else range(HALF if core == 0 else 3)
        for k in mine:
            dst, own, other = (f, fk_hbm, fr_hbm) if first else (b, bk_hbm, br_hbm)
            sem = isems.at[0 if first else 1, k]
            for half, src in enumerate((own, other)):
                pltpu.make_async_copy(src.at[:, pl.ds(k * D, D)], dst.at[k, pl.ds(half * ROWS, ROWS)], sem).start()
            loads[core, first, k] = pltpu.make_async_copy(dst.at[k], dst.at[k], sem)

    def operand(first, core, k):
        wait = loads.pop((core, first, k), None)
        if wait is not None:
            wait.wait()
        return (f if first else b)[k]

    for j in range(n):
        held[j, flat * r:] = gv[...].astype(BF)
        pltpu.make_async_copy(held.at[j, pl.ds(flat * r, TAIL)], outs[j].at[pl.ds(flat * r, TAIL)], osems.at[0]).start()

    def store(c, val):
        if c >= flat:
            for j in range(n):
                rest[5][slots[j] % 4, slots[j] // 4, (c - flat) * r:(c - flat + 1) * r] = val[j * r:(j + 1) * r]
            if c == HALF - 1:
                for k in range(4):
                    for far in (0, 1):
                        rows = pl.ds(far * direct * r, direct * r)
                        pltpu.make_async_copy(rest[5].at[k, far], outs[n + k].at[rows], osems.at[0]).start()
            return
        for j in range(n):
            held[slots[j], c * r:(c + 1) * r] = val[j * r:(j + 1) * r]
        for j in range(n):
            rows = pl.ds(c * r, r)
            pltpu.make_async_copy(held.at[j, rows], outs[j].at[rows], osems.at[0]).start()

    def store_rows(c, val):
        for i in range(n // 4):
            held[slots[c * (n // 4) + i], :4 * r] = val[i * 4 * r:(i + 1) * 4 * r]
        if c == 3:
            for j in range(n):
                rows = pl.ds(0, 4 * r)
                pltpu.make_async_copy(held.at[j, rows], outs[j].at[rows], osems.at[0]).start()

    @pl.when(info[5] == 0)
    def _():
        load(True, 0)
        load(False, 0)
        for c in range(HALF):
            val = dot(operand(True, 0, 0 if c < 4 else 1), operand(False, 0, c), 0, 0).astype(BF)
            store(c, val)

    @pl.when(info[5] != 0)
    def _():
        load(False, 1)
        load(True, 1)
        for c in range(HALF):
            val = dot(operand(True, 1, c), operand(False, 1, 0 if c < 4 else c - 3), 0, 0).astype(BF)
            if c < 4 and n > 1:
                store_rows(c, val)
            else:
                store(c, val)

    for j in range(n):
        pltpu.make_async_copy(held.at[j], outs[j], osems.at[0]).wait()
    if direct:
        pltpu.make_async_copy(rest[5], rest[5], osems.at[0]).wait()


def weight_products(n, direct, behind, gv, fk, bk, fr, br):
    shape = ((HALF - direct) * (D // n) + TAIL, D)
    shapes = [jax.ShapeDtypeStruct(shape, BF)] * n
    scratch = [pltpu.VMEM((HALF, 2 * ROWS, D), BF), pltpu.VMEM((HALF, 2 * ROWS, D), BF), pltpu.VMEM((n,) + shape, BF),
               pltpu.SemaphoreType.DMA((2, HALF)), pltpu.SemaphoreType.DMA((1,))]
    if direct:
        shapes += [jax.ShapeDtypeStruct((2 * direct * (D // n), D), BF)] * 4
        scratch.append(pltpu.VMEM((4, 2, direct * (D // n), D), BF))
    return pl.pallas_call(
        functools.partial(product_kernel, n, direct),
        out_shape=shapes,
        in_specs=[ANYS, VM] + [ANYS] * 4,
        out_specs=[ANYS] * len(shapes),
        scratch_shapes=scratch,
        compiler_params=pltpu.CompilerParams(vmem_limit_bytes=VMEM_LIMIT),
        cost_estimate=pl.CostEstimate(flops=2 * 2 * ROWS * D * D * 6, bytes_accessed=2**24, transcendentals=0),
        name="weight_products",
    )(behind, gv, fk, bk, fr, br)


def pack_kernel(joint, output, up, down, ag, as_, jb, ob, fg, fs, db, ub, block_ref, pair_ref):
    r = output.shape[0]
    spot = lax.axis_index("dp")
    for k in range(3):
        block_ref[k * r:(k + 1) * r, :] = joint[:, k * D:(k + 1) * D].astype(BF)
    block_ref[3 * r:4 * r, :] = output[...].astype(BF)
    for k in range(2):
        block_ref[(4 + k) * r:(5 + k) * r, :] = up[:, k * D:(k + 1) * D].astype(BF)
        pair_ref[k * r:(k + 1) * r, :] = up[:, (2 + k) * D:(3 + k) * D].astype(BF)
    block_ref[6 * r:10 * r, :] = down[...].astype(BF)

    def placed(ref, at):
        wide = ref.shape[1]
        lane = lax.broadcasted_iota(jnp.int32, (wide, D), 1)
        entry = lax.broadcasted_iota(jnp.int32, (wide, D), 0)
        return dot(ref[...].astype(BF), (lane == entry + at * wide).astype(BF))

    zero = jnp.zeros((1, D), F32)
    jrow = placed(jb, spot % 4)
    urow = placed(ub, spot % 2)
    rows = [placed(ag, spot), placed(as_, spot)]
    rows += [jnp.where(spot // 4 == k, jrow, zero) for k in range(2)]
    rows += [placed(v, spot) for v in (ob, fg, fs, db)]
    rows += [jnp.where(spot // 2 == k, urow, zero) for k in range(4)] + [zero] * 4
    block_ref[10 * r:, :] = jnp.concatenate(rows).astype(BF)


def pack(*params):
    r = params[1].shape[0]
    return pl.pallas_call(
        pack_kernel,
        out_shape=[jax.ShapeDtypeStruct((10 * r + TAIL, D), BF), jax.ShapeDtypeStruct((2 * r, D), BF)],
        in_specs=[VM] * 12,
        out_specs=[VM, VM],
        compiler_params=pltpu.CompilerParams(vmem_limit_bytes=VMEM_LIMIT),
        name="pack",
    )(*params)


def finish_kernel(red0, red1, sent0, sent1, up, joint, out, down, ag, as_, jb, ob, fg, fs, db, ub):
    r = out.shape[0]
    spot, core = lax.axis_index("dp"), lax.axis_index("section") % 2

    def taken(rows, wide, at):
        entry = lax.broadcasted_iota(jnp.int32, (D, wide), 0)
        lane = lax.broadcasted_iota(jnp.int32, (D, wide), 1)
        pick = (entry == lane + at * wide).astype(F32)
        return lax.dot_general(rows, pick, (((1,), (0,)), ((), ())), precision=lax.Precision.HIGHEST,
                               preferred_element_type=F32)

    def write(a, b):
        for k in range(4):
            up[:, k * D:(k + 1) * D] = a[k * r:(k + 1) * r, :].astype(F32)
        for k in range(2):
            joint[:, k * D:(k + 1) * D] = a[(4 + k) * r:(5 + k) * r, :].astype(F32)
        joint[:, 2 * D:] = b[5 * r:6 * r, :].astype(F32)
        down[...] = b[:4 * r, :].astype(F32)
        out[...] = b[4 * r:5 * r, :].astype(F32)
        v = a[6 * r:, :].astype(F32) + b[6 * r:, :].astype(F32)
        own = taken(v, r, spot)
        for ref, row in ((ag, AG), (as_, AS), (ob, OB), (fg, FG), (fs, FS), (db, DB)):
            ref[...] = own[row:row + 1]
        half = taken(v, 2 * r, spot % 4)
        jb[...] = jnp.where(spot // 4 == 0, half[BQ:BQ + 1], half[BV:BV + 1])
        most = taken(v, 4 * r, spot % 2)
        place = spot // 2
        ub[...] = jnp.where(place == 0, most[UB:UB + 1], jnp.where(place == 1, most[UB + 1:UB + 2], jnp.where(
            place == 2, most[UB + 2:UB + 3], most[UB + 3:UB + 4])))

    @pl.when(core == 0)
    def _():
        write(red0, sent0)

    @pl.when(core != 0)
    def _():
        write(sent1, red1)


def finish(r, reduced, sent):
    shapes = [(r, FF), (r, 3 * D), (r, D), (4 * r, D), (1, r), (1, r), (1, 2 * r), (1, r), (1, r), (1, r), (1, r), (1, 4 * r)]
    return pl.pallas_call(
        finish_kernel,
        out_shape=[jax.ShapeDtypeStruct(shape, F32) for shape in shapes],
        in_specs=[VM] * 4,
        out_specs=[VM] * 12,
        compiler_params=pltpu.CompilerParams(vmem_limit_bytes=VMEM_LIMIT),
        name="finish",
    )(*reduced, *sent)


def moved(value, axis, by):
    peers = lax.axis_size(axis)
    return lax.ppermute(value, axis, [(i, i + by) for i in range(peers) if 0 <= i + by < peers])


def flipped(value, bit):
    peers = lax.axis_size("section")
    return lax.ppermute(value, "section", [(i, i ^ bit) for i in range(peers)])


def swapped(value):
    return flipped(value, 1)


def vector_tail(n, spot, attend_gain, attend_shift, joint_bias, output_bias, feed_gain, feed_shift, down_bias, up_bias):
    lane = jnp.arange(D)

    def row(v, times, at, live=True):
        return jnp.where((lane // v.shape[0] == at) & live, jnp.tile(v, times), 0.0)

    half, quarter = n // 2, n // 4
    rows = [row(attend_gain, n, spot), row(attend_shift, n, spot)]
    rows += [row(joint_bias, half, spot % half, spot // half == k) for k in range(2)]
    rows += [row(v, n, spot) for v in (output_bias, feed_gain, feed_shift, down_bias)]
    rows += [row(up_bias, quarter, spot % quarter, spot // quarter == k) for k in range(4)]
    return jnp.concatenate([jnp.stack(rows), jnp.zeros((4, D), F32)])


def pack_shard(joint, output, up, down, tail):
    pieces = [joint[:, k * D:(k + 1) * D] for k in range(3)] + [output]
    pieces += [up[:, k * D:(k + 1) * D] for k in range(4)]
    return jnp.concatenate(pieces + [down, tail]).astype(BF)


def kernel_form(n, g, tail):
    r = D // n
    cut = jnp.swapaxes(g[:, :8 * r].reshape(n, 8, r, D), 0, 1).reshape(8 * D, D)
    return [jnp.concatenate([cut, g[:, 8 * r:12 * r].reshape(FF, D), tail.astype(BF)])]


IN, OUT, MID, PAIR = ((0, 1), (3, 2)), ((1, 0), (2, 3)), ((1, 2), (2, 1)), ((0, 1), (1, 0), (2, 3), (3, 2))


class Links:
    def __init__(self, **depth):
        self.depth = {"x": depth["x"], "in": depth["z"], "mid": depth["z"], "out": depth["z"]}
        self.ended = {"x": [], "in": [], "mid": [], "out": []}

    def send(self, value, names, axis, pairs):
        for name in names:
            done = self.ended[name]
            if len(done) >= self.depth[name]:
                value = lax.optimization_barrier((value, done[-self.depth[name]]))[0]
        got = lax.ppermute(value, axis, pairs)
        for name in names:
            self.ended[name].append(got)
        return got

    def along(self, value, moves):
        names = {IN: ("in",), OUT: ("out",), MID: ("mid",), PAIR: ("out",)}[moves]
        return self.send(value, names, "dp", [(2 * a + x, 2 * b + x) for a, b in moves for x in range(2)])

    def across(self, value, core=None):
        if core is None:
            return self.send(value, ("x",), "dp", [(i, i ^ 1) for i in range(8)])
        places = [8 * s + i for s in range(lax.axis_size("section")) if s % 2 == core for i in range(8)]
        return self.send(value, ("x",), ("section", "dp"), [(i, i ^ 1) for i in places])


def gather_blocks(own, pair, middle, others):
    net = Links(x=1, z=9)
    one, mid = net.along(own, PAIR), net.along(own, MID)
    sent = [net.across(own)]
    first = net.across(pair)
    both = jnp.concatenate([pair, first])
    far, back = net.along(mid, OUT), net.along(one, MID)
    sent.append(net.across(one))
    both_one, both_mid = net.along(both, PAIR), net.along(both, MID)
    last = net.along(back, OUT)
    third = jnp.where(middle, mid, far)
    sent.append(net.across(third))
    fourth = jnp.where(middle, back, last)
    sent.append(net.across(fourth))
    both_one, both_mid, fourth = lax.optimization_barrier((both_one, both_mid, fourth))
    both_far, both_back = net.along(both_mid, OUT), net.along(both_one, MID)
    both_last = net.along(both_back, OUT)
    third, *others = lax.optimization_barrier((third, *others))
    mine = [own, one, third, fourth] + sent
    mine += [both, both_one, jnp.where(middle, both_mid, both_far), jnp.where(middle, both_back, both_last)]
    return mine, [swapped(b) for b in mine], others


def add(*terms):
    total = terms[0].astype(F32)
    for t in terms[1:]:
        total = total + t.astype(F32)
    return total.astype(BF)


def scatter_both(p, q, extra):
    chain, net = Links(x=1, z=9), Links(x=9, z=9)
    p[5], q[0] = lax.optimization_barrier((p[5], q[0]))
    ps = []
    for k in range(3):
        ps.append(jnp.concatenate([add(p[k], chain.across(p[4 + k])), p[8 + k]]))
        if k == 0:
            pa1 = chain.along(ps[0], IN)
        elif k == 1:
            pa2 = chain.along(ps[1], IN)
            pb2 = chain.along(add(ps[0], pa1), MID)
        else:
            pa3 = chain.along(ps[2], IN)
            pb3 = chain.along(add(ps[1], pa2), MID)
            pc3 = chain.along(add(ps[2], pb2), OUT)
    px3 = chain.across(p[7])
    x0 = net.across(q[4])
    s0 = add(q[0], x0)
    b, s0 = lax.optimization_barrier((q[5], s0))
    x1, a1 = net.across(b), net.along(s0, IN)
    s1, t0 = add(q[1], x1), add(s0, a1)
    b, own, s1, t0, extra = lax.optimization_barrier((q[6], q[7], s1, t0, extra))
    x2, a2, b2, x3 = net.across(b), net.along(s1, IN), net.along(t0, MID), net.across(own)
    s2, t1 = add(q[2], x2), add(s1, a2)
    u = add(s2, b2)
    s2, t1, u = lax.optimization_barrier((s2, t1, u))
    a3, b3, c3 = net.along(s2, IN), net.along(t1, MID), net.along(u, OUT)
    total = add(jnp.concatenate([add(p[3], px3), p[11]]), pa3, pb3, pc3)
    rows, pair = p[3].shape[0], p[11].shape[0] // 2
    late = add(total[rows:rows + pair], net.across(total[rows + pair:]))
    first = jnp.concatenate([total[:rows - TAIL], late, total[rows - TAIL:rows]])
    return first, add(q[3], x3, a3, b3, c3), extra


def shards(tokens, lengths, cotangent, attend_gain, attend_shift, joint_weight, joint_bias, output_weight,
           output_bias, feed_gain, feed_shift, up_weight, up_bias, down_weight, down_bias):
    n = lax.axis_size("dp")
    r = D // n
    lined = n == 8
    nk = n if lined else 1
    sections = lax.axis_size("section")
    stages = sections // 2
    index = lax.axis_index("section")
    core, stage = index % 2, index // 2
    seq = tokens.shape[1]
    spot = lax.axis_index("dp")
    z = spot // 2
    middle = (z == 1) | (z == 2)
    def own_pair(a):
        return lax.dynamic_index_in_dim(a, core, 0, False)

    def padded(a):
        return jnp.pad(a, ((0, ROWS - seq), (0, 0)))

    places = lax.broadcasted_iota(jnp.int32, (8, ROWS), 1)
    mask = (((places < own_pair(lengths)) | (places >= CAPTION)) & (places < seq)).astype(F32)
    own_tokens = padded(own_pair(tokens))
    own_cotangent = padded(own_pair(cotangent))

    if lined:
        packed, pair = pack(joint_weight[0], output_weight[0], up_weight[0], down_weight[0], attend_gain, attend_shift,
                            joint_bias, output_bias, feed_gain, feed_shift, down_bias, up_bias)
        wa, wb, others = gather_blocks(packed, pair, middle, (own_tokens, own_cotangent, mask))
        own_tokens, own_cotangent, mask = others
    else:
        tail = vector_tail(n, spot, attend_gain[0], attend_shift[0], joint_bias[0], output_bias[0], feed_gain[0],
                           feed_shift[0], down_bias[0], up_bias[0])
        packed = pack_shard(joint_weight[0], output_weight[0], up_weight[0], down_weight[0], tail)
        gathered = lax.all_gather(packed, "dp")
        tails = lax.psum(tail.astype(BF).astype(F32), "dp")
        wa, wb = kernel_form(n, gathered, tails), kernel_form(n, swapped(gathered), swapped(tails))

    came = own_tokens
    for _ in range(stages - 1):
        came = moved(forward_stage(False, came, came, mask, wa, wb)[1], "section", 2)
        if stages > 2:
            came = jnp.where(stage == 0, own_tokens, came)
    got = forward_stage(True, own_tokens, came, mask, wa, wb)
    x, leaving = got[14], got[1]
    saved = [(x, *got[2:6]), (got[0], *got[8:12])]
    kept = [got[6], got[12]]
    received = [swapped(got[7]), swapped(got[13])]

    g = own_cotangent
    for t in range(stages - 1):
        g = backward_layers(False, (1, 0), g, mask, saved, wa, wb, None)[0]
        g = jnp.where(stage == stages - 1, own_cotangent, moved(g, "section", -2))
    products, operands = [None, None], [None, None]
    behind = mask
    for s in (1, 0):
        g, gv, bk, bs = backward_layers(True, (s,), g, mask, saved, wa, wb, behind)
        operands[s] = gv, kept[s], bk, received[s], swapped(bs)
    behind = g
    for s in (1, 0):
        products[s] = list(weight_products(nk, 2 * s if lined else 0, behind, *operands[s]))
        behind = products[s][0]

    g, products[0][-1] = lax.optimization_barrier((g, products[0][-1]))
    ends = jnp.where(stage == 0, g, leaving)[:seq].reshape(seq, stages, 2, D // sections)
    kept_half = lax.dynamic_index_in_dim(ends, stage, 1, False)
    got_half = flipped(lax.dynamic_index_in_dim(ends, 1 - stage, 1, False), 2)
    halves = jnp.stack([jnp.where(stage == 0, got_half, kept_half), jnp.where(stage == 0, kept_half, got_half)])
    kept_part = lax.dynamic_index_in_dim(halves, core, 2, False)
    got_part = flipped(lax.dynamic_index_in_dim(halves, 1 - core, 2, False), 1)
    parts = jnp.stack([jnp.where(core == 0, kept_part, got_part), jnp.where(core == 0, got_part, kept_part)], axis=1)

    reduced = [None, None]
    if lined:
        reduced[1], reduced[0], parts = scatter_both(products[1], products[0], parts)
    else:
        for s in range(2):
            p = products[s][0]
            col = jnp.swapaxes(p[:HALF * D].reshape(HALF, n, r, D), 0, 1).reshape(n, HALF * r, D)
            row = jnp.concatenate([p[:4 * D].reshape(n, 4 * r, D), col[:, 4 * r:]], axis=1)
            total = lax.psum_scatter(jnp.where(core == 0, col, row), "dp", scatter_dimension=0)
            reduced[s] = jnp.concatenate([total, lax.psum(p[HALF * D:], "dp")])
    sent = [lax.ppermute(reduced[s], "section", [(i, i ^ 1) for i in range(sections) if i % 2 != s]) for s in range(2)]
    outputs, token_grad = parts[0], parts[1]
    if lined:
        up, joint, out, down, ag, as_, jb, ob, fg, fs, db, ub = finish(r, reduced, sent)
        return (outputs, token_grad, ag, as_, joint[None], jb, out[None], ob, fg, fs, up[None], ub, down[None], db)
    keep = jnp.where(core == 0, reduced[0], reduced[1])
    away = jnp.where(core == 0, sent[0], sent[1])
    first = jnp.where(core == 0, keep, away).astype(F32)
    second = jnp.where(core == 0, away, keep).astype(F32)
    grad_up = jnp.concatenate([first[k * r:(k + 1) * r] for k in range(4)], axis=1)
    grad_joint = jnp.concatenate([first[4 * r:5 * r], first[5 * r:6 * r], second[5 * r:6 * r]], axis=1)
    grad_down = second[:4 * r]
    grad_out = second[4 * r:5 * r]
    v = first[6 * r:] + second[6 * r:]
    half, quarter = n // 2, n // 4
    vec = lax.dynamic_slice(v, (0, r * spot), (16, r))
    grad_jb = lax.dynamic_slice(v, (BQ + spot // half, 2 * r * (spot % half)), (1, 2 * r))
    grad_ub = lax.dynamic_slice(v, (UB + spot // quarter, 4 * r * (spot % quarter)), (1, 4 * r))
    return (outputs, token_grad, vec[AG:AG + 1], vec[AS:AS + 1], grad_joint[None], grad_jb, grad_out[None],
            vec[OB:OB + 1], vec[FG:FG + 1], vec[FS:FS + 1], grad_up[None], grad_ub, grad_down[None], vec[DB:DB + 1])


def solution(mesh):
    vec, mat = P("section", "dp"), P("section", "dp", None)
    rows = P("dp", None, None)
    out = P("dp", None, "section")
    return jax.shard_map(
        shards,
        mesh=mesh,
        in_specs=(rows, P("dp"), rows, vec, vec, mat, vec, mat, vec, vec, vec, mat, vec, mat, vec),
        out_specs=(out, out, vec, vec, mat, vec, mat, vec, vec, vec, mat, vec, mat, vec),
        check_vma=False,
    )
```

```python
import functools

import jax
import jax.numpy as jnp
from jax import lax
from jax.experimental import pallas as pl
from jax.experimental.pallas import tpu as pltpu
from jax.sharding import PartitionSpec as P

D = 768
HEADS = 12
FF = 3072
CAPTION = 40
ROWS = 288
HALF = 6
TAIL = 16
EPS = 1e-6
BF = jnp.bfloat16
F32 = jnp.float32
PAIRED = 2 * (D // HEADS)
VMEM_LIMIT = 60 * 2**20
WIDE = FF + 2 * D
AG, AS, BQ, BV, OB, FG, FS, DB, UB = 0, 1, 2, 3, 4, 5, 6, 7, 8

ANYS = pl.BlockSpec(memory_space=pl.ANY)
VM = pl.BlockSpec(memory_space=pltpu.VMEM)


def dot(a, b, ca=1, cb=0):
    return lax.dot_general(a, b, (((ca,), (cb,)), ((), ())), preferred_element_type=F32)


def spread_of(v):
    mean = jnp.mean(v, axis=-1, keepdims=True)
    cent = v - mean
    return cent, lax.rsqrt(jnp.mean(cent * cent, axis=-1, keepdims=True) + EPS)


def here():
    spot, core = lax.axis_index("dp"), lax.axis_index("section") % 2
    z, column = spot // 2, spot % 2
    middle = jnp.where((z == 1) | (z == 2), 1, 0)
    return [core, 1 - core, z, column, middle, core, 2 + middle]


def sending_slots(z, column):
    orders = ((3, 2, 1, 0), (2, 3, 1, 0), (0, 1, 3, 2), (0, 1, 2, 3))
    slots = []
    for j in range(8):
        a, b, c, d = (o[j // 2] for o in orders)
        slot = jnp.where(z == 0, a, jnp.where(z == 1, b, jnp.where(z == 2, c, d)))
        slots.append(slot + jnp.where(column == j % 2, 0, 4))
    return slots


def square(block):
    return block.reshape(D, D)


def weight_scratch(count):
    n, r, per = (8, D // 8, 2) if count > 1 else (1, D, 1)
    return [pltpu.VMEM((8, n, r, D), BF), pltpu.VMEM((4, per, D // per, D), BF), pltpu.VMEM((n, TAIL, D), BF),
            pltpu.SemaphoreType.DMA((13,))]


def start_weights(which, info, sets, scratch, order):
    wv, wd, tv, sems = scratch
    r = wv.shape[2]

    def start(block, j, part):
        if len(sets[0]) == 1:
            rows = block.at[pl.ds(part * r, r if part < 12 else TAIL)]
            dst = wv.at[part, 0] if part < 8 else wd.at[part - 8, 0] if part < 12 else tv.at[0]
            pltpu.make_async_copy(rows, dst, sems.at[part]).start()
        elif part == 12:
            pltpu.make_async_copy(block.at[pl.ds(10 * r, TAIL)], tv.at[j], sems.at[12]).start()
        elif part < 6:
            pltpu.make_async_copy(block.at[pl.ds(part * r, r)], wv.at[part, j], sems.at[part]).start()
        elif part == 8:
            b = j // 2
            pltpu.make_async_copy(block.at[pl.ds(6 * r, 4 * r)], wd.at[b, j % 2], sems.at[8 + b]).start()

    for number, blocks in enumerate(sets):

        @pl.when(info[which] == number)
        def _():
            if len(blocks) == 1:
                for part in order:
                    start(blocks[0], 0, part)
                return
            lines = [info[2], info[2] ^ 1, info[2] ^ info[6], info[2] ^ (info[6] ^ 1)]
            spots = [(blocks[4 * far + k], lines[k] * 2 + (info[3] ^ far)) for far in (0, 1) for k in range(4)]
            for part in order:
                if part in (6, 7):
                    for far in (0, 1):
                        for k in range(4):
                            rows = blocks[8 + k].at[pl.ds((2 * far + part - 6) * r, r)]
                            pltpu.make_async_copy(rows, wv.at[part, lines[k] * 2 + (info[3] ^ far)], sems.at[part]).start()
                    continue
                for block, j in spots:
                    start(block, j, part)

    waits = [pltpu.make_async_copy(wv.at[k], wv.at[k], sems.at[k]) for k in range(8)]
    waits += [pltpu.make_async_copy(wd.at[b], wd.at[b], sems.at[8 + b]) for b in range(4)]
    return waits + [pltpu.make_async_copy(tv, tv, sems.at[12])]


def vectors(tv):
    total = tv[0].astype(F32)
    for j in range(1, tv.shape[0]):
        total = total + tv[j].astype(F32)
    return total


def handing(core, keep, send, sems, waits):
    def hand_on(src, first, at):
        wide = src.shape[1]
        sem = sems.at[len(waits)]
        mine = (core == 0) == first

        @pl.when(mine)
        def _():
            pltpu.make_async_copy(src, keep.at[:, pl.ds(at, wide)], sem).start()

        @pl.when(jnp.logical_not(mine))
        def _():
            pltpu.make_async_copy(src, send.at[:, pl.ds(at, wide)], sem).start()

        waits.append(pltpu.make_async_copy(src, keep.at[:, pl.ds(at, wide)], sem))

    return hand_on


def forward_one(save, core, x, usable, copies, scratch, work, osems, saved, outs):
    wv, wd, tv, _ = scratch
    jn, ctx, act, gp, nrm, nt, vec = work
    if save:
        lse_ref, mid_ref, j_hbm, gp_hbm, keep, send = saved
        hand_on = handing(core, keep, send, osems, outs)

        def flush(src, dst):
            c = pltpu.make_async_copy(src, dst, osems.at[len(outs)])
            c.start()
            outs.append(c)

    copies[12].wait()
    vec[...] = vectors(tv)
    cent, inv = spread_of(x)
    nrm[...] = (cent * inv * vec[AG:AG + 1, :] + vec[AS:AS + 1, :]).astype(BF)
    if save:
        hand_on(nrm, True, D)
        hand_on(nrm, False, FF + D)
    for k in range(3):
        copies[k].wait()
        r = dot(nrm[...], square(wv[k]))
        if k == 0:
            r = r + vec[BQ:BQ + 1, :]
        if k == 2:
            r = r + vec[BV:BV + 1, :]
        jn[:, k * D:(k + 1) * D] = r.astype(BF)
    if save:
        flush(jn, j_hbm)
    lane = lax.broadcasted_iota(jnp.int32, (ROWS, PAIRED), 1)
    low = lane < PAIRED // 2
    lse = jnp.zeros((ROWS, PAIRED), F32)
    for i in range(HEADS // 2):
        at = i * PAIRED
        q2 = jn[:, at:at + PAIRED] * BF(0.125)
        k2 = jn[:, D + at:D + at + PAIRED]
        v2 = jn[:, 2 * D + at:2 * D + at + PAIRED]
        zero = jnp.zeros_like(q2)
        both = []
        for h in range(2):
            s = dot(jnp.where(low == (h == 0), q2, zero), k2, 1, 1)
            s = jnp.where(usable, s, -1e30)
            top = jnp.max(s, axis=-1, keepdims=True)
            e = jnp.exp(s - top)
            total = jnp.sum(e, axis=-1, keepdims=True)
            both.append(dot(e.astype(BF), v2) * (1.0 / total))
            if save:
                lse = jnp.where(lane == 2 * i + h, top + jnp.log(total), lse)
        ctx[:, at:at + PAIRED] = jnp.where(low, both[0], both[1]).astype(BF)
    if save:
        lse_ref[...] = lse
        hand_on(ctx, False, FF)
    for k in range(3, 12):
        copies[k].wait()
    middle = x + dot(ctx[...], square(wv[3])) + vec[OB:OB + 1, :]
    if save:
        mid_ref[...] = middle
    cent, inv = spread_of(middle)
    nt[...] = (cent * inv * vec[FG:FG + 1, :] + vec[FS:FS + 1, :]).astype(BF)
    if save:
        hand_on(nt, True, 0)
    acc = middle + vec[DB:DB + 1, :]
    for b in range(4):
        cols = slice(b * D, (b + 1) * D)
        h = dot(nt[...], square(wv[4 + b])) + vec[UB + b:UB + b + 1, :]
        phi = 0.5 + 0.5 * lax.erf(h * (0.5**0.5))
        a = (h * phi).astype(BF)
        if save:
            act[:, cols] = a
            gp[:, cols] = (phi + h * jnp.exp(-0.5 * h * h) * 0.3989422804014327).astype(BF)
            hand_on(act.at[:, pl.ds(b * D, D)], False, b * D)
            flush(gp.at[:, pl.ds(b * D, D)], gp_hbm.at[:, pl.ds(b * D, D)])
        acc = acc + dot(a, square(wd[b]))
    return acc.astype(BF)


def forward_kernel(save, count, x_ref, came_ref, mask_ref, *rest):
    info = here()
    sets, rest = (rest[:count], rest[count:2 * count]), rest[2 * count:]
    wide = 15 if save else 2
    results, rest = rest[:wide], rest[wide:]
    scratch = [rest[0:4], rest[4:8]]
    rest = rest[8:]
    copies = [start_weights(s, info, sets, scratch[s], (12,) + tuple(range(12))) for s in range(2)]
    usable = mask_ref[0:1, :] > 0.5
    outs = []
    x = x_ref[...]
    if save:
        x = jnp.where(lax.axis_index("section") < 2, x, came_ref[...])
        results[14][...] = x
    for s in range(2):
        work, rest = rest[:7], rest[7:]
        saved = results[2 + 6 * s:8 + 6 * s] if save else ()
        x = forward_one(save, info[5], x.astype(F32), usable, copies[s], scratch[s], work, rest[7 * (1 - s)], saved, outs)
        results[s][...] = x
    for c in outs:
        c.wait()


def forward_stage(save, x, came, mask, wa, wb):
    def sd(cols, t=BF):
        return jax.ShapeDtypeStruct((ROWS, cols), t)

    shapes, specs = [sd(D)] * 2, [VM] * 2
    if save:
        shapes += [sd(PAIRED, F32), sd(D, F32), sd(3 * D), sd(FF), sd(WIDE), sd(WIDE)] * 2
        specs += ([VM, VM] + [ANYS] * 4) * 2
        shapes.append(sd(D))
        specs.append(VM)
    work = [pltpu.VMEM((ROWS, 3 * D), BF), pltpu.VMEM((ROWS, D), BF), pltpu.VMEM((ROWS, FF), BF),
            pltpu.VMEM((ROWS, FF), BF), pltpu.VMEM((ROWS, D), BF), pltpu.VMEM((ROWS, D), BF), pltpu.VMEM((16, D), F32)]
    return pl.pallas_call(
        functools.partial(forward_kernel, save, len(wa)),
        out_shape=shapes,
        in_specs=[VM, VM, VM] + [ANYS] * (2 * len(wa)),
        out_specs=specs,
        scratch_shapes=weight_scratch(len(wa)) * 2 + work * 2 + [pltpu.SemaphoreType.DMA((32,))],
        compiler_params=pltpu.CompilerParams(vmem_limit_bytes=VMEM_LIMIT),
        cost_estimate=pl.CostEstimate(flops=2 * ROWS * D * D * 26, bytes_accessed=48 * D * D + 2**23, transcendentals=0),
        name="forward_stage",
    )(x, came, mask, *wa, *wb)


def backward_one(save, core, g_ref, x_ref, lse_ref, mid_ref, j_hbm, gp_hbm, usable, copies, scratch, work, isems, osems, results,
                 waits):
    wv, wd, tv, _ = scratch
    jn, gp, dh, dj, b1, vec = work
    hand_on = lambda *a: None
    if save:
        gv_ref, keep_hbm, send_hbm = results
        hand_on = handing(core, keep_hbm, send_hbm, osems, waits)
    hand_on(g_ref, False, 0)
    copies[12].wait()
    vec[...] = vectors(tv)
    d_nt = None
    for b in range(4):
        cols = slice(b * D, (b + 1) * D)
        copies[8 + b].wait()
        if b == 0:
            pltpu.make_async_copy(gp_hbm, gp, isems.at[0]).wait()
        da = dot(g_ref[...], square(wd[b]), 1, 1)
        d = (da * gp[:, cols].astype(F32)).astype(BF)
        dh[:, cols] = d
        copies[4 + b].wait()
        part = dot(d, square(wv[4 + b]), 1, 1)
        d_nt = part if d_nt is None else d_nt + part
    hand_on(dh, True, 0)

    def norm_back(v, dy, gain, row):
        cent, inv = spread_of(v)
        hat = cent * inv
        if save:
            gv_ref[row:row + 1, :] = jnp.sum(dy * hat, axis=0, keepdims=True)
            gv_ref[row + 1:row + 2, :] = jnp.sum(dy, axis=0, keepdims=True)
        t = dy * gain
        return inv * (t - jnp.mean(t, axis=-1, keepdims=True) - hat * jnp.mean(t * hat, axis=-1, keepdims=True))

    d_mid = g_ref[...].astype(F32) + norm_back(mid_ref[...], d_nt, vec[FG:FG + 1, :], FG)
    b1[...] = d_mid.astype(BF)
    hand_on(b1, False, D)
    if save:
        for b in range(4):
            gv_ref[UB + b:UB + b + 1, :] = jnp.sum(dh[:, b * D:(b + 1) * D].astype(F32), axis=0, keepdims=True)
        gv_ref[DB:DB + 1, :] = jnp.sum(g_ref[...].astype(F32), axis=0, keepdims=True)
        gv_ref[OB:OB + 1, :] = jnp.sum(b1[...].astype(F32), axis=0, keepdims=True)
    copies[3].wait()
    d_ctx = dot(b1[...], square(wv[3]), 1, 1).astype(BF)
    pltpu.make_async_copy(j_hbm, jn, isems.at[1]).wait()
    for k in range(3):
        copies[k].wait()
    lane = lax.broadcasted_iota(jnp.int32, (ROWS, PAIRED), 1)
    low = lane < PAIRED // 2
    for i in range(HEADS // 2):
        at = i * PAIRED
        q2 = jn[:, at:at + PAIRED] * BF(0.125)
        k2 = jn[:, D + at:D + at + PAIRED]
        v2 = jn[:, 2 * D + at:2 * D + at + PAIRED]
        do2 = d_ctx[:, at:at + PAIRED]
        zero = jnp.zeros_like(q2)
        res = []
        for h in range(2):
            here = low == (h == 0)
            s = dot(jnp.where(here, q2, zero), k2, 1, 1)
            p = jnp.where(usable, jnp.exp(s - lse_ref[:, 2 * i + h:2 * i + h + 1]), 0.0)
            dp = dot(jnp.where(here, do2, zero), v2, 1, 1)
            inner = jnp.sum(p * dp, axis=-1, keepdims=True)
            dsc = (p * (dp - inner)).astype(BF)
            res.append((dot(dsc, k2) * 0.125, dot(dsc, q2, 0, 0), dot(p.astype(BF), do2, 0, 0)))
        for c in range(3):
            dj[:, c * D + at:c * D + at + PAIRED] = jnp.where(low, res[0][c], res[1][c]).astype(BF)
    hand_on(dj.at[:, pl.ds(0, 2 * D)], True, FF)
    hand_on(dj.at[:, pl.ds(2 * D, D)], False, 2 * D)
    if save:
        gv_ref[BQ:BQ + 1, :] = jnp.sum(dj[:, :D].astype(F32), axis=0, keepdims=True)
        gv_ref[BV:BV + 1, :] = jnp.sum(dj[:, 2 * D:].astype(F32), axis=0, keepdims=True)
        gv_ref[UB + 4:, :] = jnp.zeros((4, D), F32)
    d_n = dot(dj[:, :D], square(wv[0]), 1, 1)
    for k in (1, 2):
        d_n = d_n + dot(dj[:, k * D:(k + 1) * D], square(wv[k]), 1, 1)
    return (d_mid + norm_back(x_ref[...].astype(F32), d_n, vec[AG:AG + 1, :], AG)).astype(BF)


def backward_kernel(save, layers, count, g_ref, mask_ref, *rest):
    info = here()
    m = len(layers)
    kept, rest = [rest[5 * i:5 * i + 5] for i in range(m)], rest[5 * m:]
    rest = rest[1:] if save else rest
    sets, rest = (rest[:count], rest[count:2 * count]), rest[2 * count:]
    wide = 4 if save else 1
    results, rest = rest[:wide], rest[wide:]
    scratch, rest = [rest[4 * i:4 * i + 4] for i in range(m)], rest[4 * m:]
    work, (gs, isems, osems) = [rest[6 * i:6 * i + 6] for i in range(m)], rest[6 * m:]
    copies = []
    for i in range(m):
        pltpu.make_async_copy(kept[i][4], work[i][1], isems.at[i, 0]).start()
        copies.append(start_weights(layers[i], info, sets, scratch[i], (12, 8, 9, 10, 11, 4, 5, 6, 7, 3, 0, 1, 2)))
        pltpu.make_async_copy(kept[i][3], work[i][0], isems.at[i, 1]).start()
    usable = mask_ref[0:1, :] > 0.5
    waits = []
    for i in range(m):
        x_ref, lse_ref, mid_ref, j_hbm, gp_hbm = kept[i]
        g = backward_one(save, info[5], g_ref if i == 0 else gs, x_ref, lse_ref, mid_ref, j_hbm, gp_hbm, usable, copies[i],
                         scratch[i], work[i], isems.at[i], osems, results[1:], waits)
        if i + 1 < m:
            gs[...] = g
        else:
            results[0][...] = g
    for c in waits:
        c.wait()


def backward_layers(save, layers, g, mask, saved, wa, wb, behind):
    def sd(cols, t=BF, rows=ROWS):
        return jax.ShapeDtypeStruct((rows, cols), t)

    shapes, specs = [sd(D)], [VM]
    if save:
        shapes += [sd(D, F32, 16), sd(WIDE), sd(WIDE)]
        specs += [VM, ANYS, ANYS]
    m = len(layers)
    work = [pltpu.VMEM((ROWS, 3 * D), BF), pltpu.VMEM((ROWS, FF), BF), pltpu.VMEM((ROWS, FF), BF),
            pltpu.VMEM((ROWS, 3 * D), BF), pltpu.VMEM((ROWS, D), BF), pltpu.VMEM((16, D), F32)]
    kept = [a for s in layers for a in saved[s]]
    return pl.pallas_call(
        functools.partial(backward_kernel, save, layers, len(wa)),
        out_shape=shapes,
        in_specs=[VM, VM] + [VM, VM, VM, ANYS, ANYS] * m + [ANYS] * (save + 2 * len(wa)),
        out_specs=specs,
        scratch_shapes=weight_scratch(len(wa)) * m + work * m + [
            pltpu.VMEM((ROWS, D), BF), pltpu.SemaphoreType.DMA((m, 2)), pltpu.SemaphoreType.DMA((5,))],
        compiler_params=pltpu.CompilerParams(vmem_limit_bytes=VMEM_LIMIT),
        cost_estimate=pl.CostEstimate(flops=2 * 10**10, bytes_accessed=2**24, transcendentals=0),
        name="backward_layers",
    )(g, mask, *kept, *([behind] if save else []), *wa, *wb)


def product_kernel(n, direct, behind, gv, fk_hbm, bk_hbm, fr_hbm, br_hbm, *rest):
    wide = n + 4 * (direct > 0)
    outs, rest = rest[:wide], rest[wide:]
    f, b, held, isems, osems = rest[:5]
    info = here()
    slots = sending_slots(info[2], info[3]) if n > 1 else [0]
    r = D // n
    flat = HALF - direct
    loads = {}

    def load(first, core):
        mine = range(2 if core == 0 else HALF) if first else range(HALF if core == 0 else 3)
        for k in mine:
            dst, own, other = (f, fk_hbm, fr_hbm) if first else (b, bk_hbm, br_hbm)
            sem = isems.at[0 if first else 1, k]
            for half, src in enumerate((own, other)):
                pltpu.make_async_copy(src.at[:, pl.ds(k * D, D)], dst.at[k, pl.ds(half * ROWS, ROWS)], sem).start()
            loads[core, first, k] = pltpu.make_async_copy(dst.at[k], dst.at[k], sem)

    def operand(first, core, k):
        wait = loads.pop((core, first, k), None)
        if wait is not None:
            wait.wait()
        return (f if first else b)[k]

    for j in range(n):
        held[j, flat * r:] = gv[...].astype(BF)
        pltpu.make_async_copy(held.at[j, pl.ds(flat * r, TAIL)], outs[j].at[pl.ds(flat * r, TAIL)], osems.at[0]).start()

    def store(c, val):
        if c >= flat:
            for j in range(n):
                rest[5][slots[j] % 4, slots[j] // 4, (c - flat) * r:(c - flat + 1) * r] = val[j * r:(j + 1) * r]
            if c == HALF - 1:
                for k in range(4):
                    for far in (0, 1):
                        rows = pl.ds(far * direct * r, direct * r)
                        pltpu.make_async_copy(rest[5].at[k, far], outs[n + k].at[rows], osems.at[0]).start()
            return
        for j in range(n):
            held[slots[j], c * r:(c + 1) * r] = val[j * r:(j + 1) * r]
        for j in range(n):
            rows = pl.ds(c * r, r)
            pltpu.make_async_copy(held.at[j, rows], outs[j].at[rows], osems.at[0]).start()

    def store_rows(c, val):
        for i in range(n // 4):
            held[slots[c * (n // 4) + i], :4 * r] = val[i * 4 * r:(i + 1) * 4 * r]
        if c == 3:
            for j in range(n):
                rows = pl.ds(0, 4 * r)
                pltpu.make_async_copy(held.at[j, rows], outs[j].at[rows], osems.at[0]).start()

    @pl.when(info[5] == 0)
    def _():
        load(True, 0)
        load(False, 0)
        for c in range(HALF):
            val = dot(operand(True, 0, 0 if c < 4 else 1), operand(False, 0, c), 0, 0).astype(BF)
            store(c, val)

    @pl.when(info[5] != 0)
    def _():
        load(False, 1)
        load(True, 1)
        for c in range(HALF):
            val = dot(operand(True, 1, c), operand(False, 1, 0 if c < 4 else c - 3), 0, 0).astype(BF)
            if c < 4 and n > 1:
                store_rows(c, val)
            else:
                store(c, val)

    for j in range(n):
        pltpu.make_async_copy(held.at[j], outs[j], osems.at[0]).wait()
    if direct:
        pltpu.make_async_copy(rest[5], rest[5], osems.at[0]).wait()


def weight_products(n, direct, behind, gv, fk, bk, fr, br):
    shape = ((HALF - direct) * (D // n) + TAIL, D)
    shapes = [jax.ShapeDtypeStruct(shape, BF)] * n
    scratch = [pltpu.VMEM((HALF, 2 * ROWS, D), BF), pltpu.VMEM((HALF, 2 * ROWS, D), BF), pltpu.VMEM((n,) + shape, BF),
               pltpu.SemaphoreType.DMA((2, HALF)), pltpu.SemaphoreType.DMA((1,))]
    if direct:
        shapes += [jax.ShapeDtypeStruct((2 * direct * (D // n), D), BF)] * 4
        scratch.append(pltpu.VMEM((4, 2, direct * (D // n), D), BF))
    return pl.pallas_call(
        functools.partial(product_kernel, n, direct),
        out_shape=shapes,
        in_specs=[ANYS, VM] + [ANYS] * 4,
        out_specs=[ANYS] * len(shapes),
        scratch_shapes=scratch,
        compiler_params=pltpu.CompilerParams(vmem_limit_bytes=VMEM_LIMIT),
        cost_estimate=pl.CostEstimate(flops=13 * 10**9, bytes_accessed=2**24, transcendentals=0),
        name="weight_products",
    )(behind, gv, fk, bk, fr, br)


def pack_kernel(joint, output, up, down, ag, as_, jb, ob, fg, fs, db, ub, block_ref, pair_ref):
    r = output.shape[0]
    spot = lax.axis_index("dp")
    for k in range(3):
        block_ref[k * r:(k + 1) * r, :] = joint[:, k * D:(k + 1) * D].astype(BF)
    block_ref[3 * r:4 * r, :] = output[...].astype(BF)
    for k in range(2):
        block_ref[(4 + k) * r:(5 + k) * r, :] = up[:, k * D:(k + 1) * D].astype(BF)
        pair_ref[k * r:(k + 1) * r, :] = up[:, (2 + k) * D:(3 + k) * D].astype(BF)
    block_ref[6 * r:10 * r, :] = down[...].astype(BF)

    def placed(ref, at):
        wide = ref.shape[1]
        lane = lax.broadcasted_iota(jnp.int32, (wide, D), 1)
        entry = lax.broadcasted_iota(jnp.int32, (wide, D), 0)
        return dot(ref[...].astype(BF), (lane == entry + at * wide).astype(BF))

    zero = jnp.zeros((1, D), F32)
    jrow = placed(jb, spot % 4)
    urow = placed(ub, spot % 2)
    rows = [placed(ag, spot), placed(as_, spot)]
    rows += [jnp.where(spot // 4 == k, jrow, zero) for k in range(2)]
    rows += [placed(v, spot) for v in (ob, fg, fs, db)]
    rows += [jnp.where(spot // 2 == k, urow, zero) for k in range(4)] + [zero] * 4
    block_ref[10 * r:, :] = jnp.concatenate(rows).astype(BF)


def pack(*params):
    r = params[1].shape[0]
    return pl.pallas_call(
        pack_kernel,
        out_shape=[jax.ShapeDtypeStruct((10 * r + TAIL, D), BF), jax.ShapeDtypeStruct((2 * r, D), BF)],
        in_specs=[VM] * 12,
        out_specs=[VM, VM],
        compiler_params=pltpu.CompilerParams(vmem_limit_bytes=VMEM_LIMIT),
        name="pack",
    )(*params)


def finish_kernel(red0, red1, sent0, sent1, up, joint, out, down, ag, as_, jb, ob, fg, fs, db, ub, first, second, sems):
    r = out.shape[0]
    spot, core = lax.axis_index("dp"), lax.axis_index("section") % 2

    def taken(rows, wide, at):
        entry = lax.broadcasted_iota(jnp.int32, (D, wide), 0)
        lane = lax.broadcasted_iota(jnp.int32, (D, wide), 1)
        pick = (entry == lane + at * wide).astype(F32)
        return lax.dot_general(rows, pick, (((1,), (0,)), ((), ())), precision=lax.Precision.HIGHEST,
                               preferred_element_type=F32)

    def write(a, b):
        for k in range(4):
            up[:, k * D:(k + 1) * D] = a[k * r:(k + 1) * r, :].astype(F32)
        for k in range(2):
            joint[:, k * D:(k + 1) * D] = a[(4 + k) * r:(5 + k) * r, :].astype(F32)
        joint[:, 2 * D:] = b[5 * r:6 * r, :].astype(F32)
        down[...] = b[:4 * r, :].astype(F32)
        out[...] = b[4 * r:5 * r, :].astype(F32)
        v = a[6 * r:, :].astype(F32) + b[6 * r:, :].astype(F32)
        own = taken(v, r, spot)
        for ref, row in ((ag, AG), (as_, AS), (ob, OB), (fg, FG), (fs, FS), (db, DB)):
            ref[...] = own[row:row + 1]
        half = taken(v, 2 * r, spot % 4)
        jb[...] = jnp.where(spot // 4 == 0, half[BQ:BQ + 1], half[BV:BV + 1])
        most = taken(v, 4 * r, spot % 2)
        place = spot // 2
        ub[...] = jnp.where(place == 0, most[UB:UB + 1], jnp.where(place == 1, most[UB + 1:UB + 2], jnp.where(
            place == 2, most[UB + 2:UB + 3], most[UB + 3:UB + 4])))

    @pl.when(core == 0)
    def _():
        pltpu.make_async_copy(red0, first, sems.at[0]).start()
        pltpu.make_async_copy(sent0, second, sems.at[1]).start()

    @pl.when(core != 0)
    def _():
        pltpu.make_async_copy(sent1, first, sems.at[0]).start()
        pltpu.make_async_copy(red1, second, sems.at[1]).start()

    pltpu.make_async_copy(red0, first, sems.at[0]).wait()
    pltpu.make_async_copy(red0, second, sems.at[1]).wait()
    write(first, second)


def finish(r, reduced, sent):
    shapes = [(r, FF), (r, 3 * D), (r, D), (4 * r, D), (1, r), (1, r), (1, 2 * r), (1, r), (1, r), (1, r), (1, r), (1, 4 * r)]
    return pl.pallas_call(
        finish_kernel,
        out_shape=[jax.ShapeDtypeStruct(shape, F32) for shape in shapes],
        in_specs=[ANYS] * 4,
        out_specs=[VM] * 12,
        scratch_shapes=[pltpu.VMEM(reduced[0].shape, BF)] * 2 + [pltpu.SemaphoreType.DMA((2,))],
        compiler_params=pltpu.CompilerParams(vmem_limit_bytes=VMEM_LIMIT),
        name="finish",
    )(*reduced, *sent)


def moved(value, axis, by):
    peers = lax.axis_size(axis)
    return lax.ppermute(value, axis, [(i, i + by) for i in range(peers) if 0 <= i + by < peers])


def flipped(value, bit):
    peers = lax.axis_size("section")
    return lax.ppermute(value, "section", [(i, i ^ bit) for i in range(peers)])


def swapped(value):
    return flipped(value, 1)


def vector_tail(n, spot, attend_gain, attend_shift, joint_bias, output_bias, feed_gain, feed_shift, down_bias, up_bias):
    lane = jnp.arange(D)

    def row(v, times, at, live=True):
        return jnp.where((lane // v.shape[0] == at) & live, jnp.tile(v, times), 0.0)

    half, quarter = n // 2, n // 4
    rows = [row(attend_gain, n, spot), row(attend_shift, n, spot)]
    rows += [row(joint_bias, half, spot % half, spot // half == k) for k in range(2)]
    rows += [row(v, n, spot) for v in (output_bias, feed_gain, feed_shift, down_bias)]
    rows += [row(up_bias, quarter, spot % quarter, spot // quarter == k) for k in range(4)]
    return jnp.concatenate([jnp.stack(rows), jnp.zeros((4, D), F32)])


def pack_shard(joint, output, up, down, tail):
    pieces = [joint[:, k * D:(k + 1) * D] for k in range(3)] + [output]
    pieces += [up[:, k * D:(k + 1) * D] for k in range(4)]
    return jnp.concatenate(pieces + [down, tail]).astype(BF)


def kernel_form(n, g, tail):
    r = D // n
    cut = jnp.swapaxes(g[:, :8 * r].reshape(n, 8, r, D), 0, 1).reshape(8 * D, D)
    return [jnp.concatenate([cut, g[:, 8 * r:12 * r].reshape(FF, D), tail.astype(BF)])]


IN, OUT, MID, PAIR = ((0, 1), (3, 2)), ((1, 0), (2, 3)), ((1, 2), (2, 1)), ((0, 1), (1, 0), (2, 3), (3, 2))


class Links:
    def __init__(self, **depth):
        self.depth = {"x": depth["x"], "in": depth["z"], "mid": depth["z"], "out": depth["z"]}
        self.ended = {"x": [], "in": [], "mid": [], "out": []}

    def send(self, value, names, axis, pairs):
        for name in names:
            done = self.ended[name]
            if len(done) >= self.depth[name]:
                value = lax.optimization_barrier((value, done[-self.depth[name]]))[0]
        got = lax.ppermute(value, axis, pairs)
        for name in names:
            self.ended[name].append(got)
        return got

    def along(self, value, moves):
        names = {IN: ("in",), OUT: ("out",), MID: ("mid",), PAIR: ("out",)}[moves]
        return self.send(value, names, "dp", [(2 * a + x, 2 * b + x) for a, b in moves for x in range(2)])

    def across(self, value, core=None):
        if core is None:
            return self.send(value, ("x",), "dp", [(i, i ^ 1) for i in range(8)])
        places = [8 * s + i for s in range(lax.axis_size("section")) if s % 2 == core for i in range(8)]
        return self.send(value, ("x",), ("section", "dp"), [(i, i ^ 1) for i in places])


def gather_blocks(own, pair, middle, others):
    net = Links(x=1, z=9)
    one, mid = net.along(own, PAIR), net.along(own, MID)
    sent = [net.across(own)]
    first = net.across(pair)
    both = jnp.concatenate([pair, first])
    far, back = net.along(mid, OUT), net.along(one, MID)
    sent.append(net.across(one))
    both_one, both_mid = net.along(both, PAIR), net.along(both, MID)
    last = net.along(back, OUT)
    third = jnp.where(middle, mid, far)
    sent.append(net.across(third))
    fourth = jnp.where(middle, back, last)
    sent.append(net.across(fourth))
    both_one, both_mid, fourth = lax.optimization_barrier((both_one, both_mid, fourth))
    both_far, both_back = net.along(both_mid, OUT), net.along(both_one, MID)
    both_last = net.along(both_back, OUT)
    third, *others = lax.optimization_barrier((third, *others))
    mine = [own, one, third, fourth] + sent
    mine += [both, both_one, jnp.where(middle, both_mid, both_far), jnp.where(middle, both_back, both_last)]
    return mine, [swapped(b) for b in mine], others


def add(*terms):
    total = terms[0].astype(F32)
    for t in terms[1:]:
        total = total + t.astype(F32)
    return total.astype(BF)


def scatter_both(p, q, extra):
    chain, net = Links(x=1, z=9), Links(x=9, z=9)
    p[5], q[0] = lax.optimization_barrier((p[5], q[0]))
    ps = []
    for k in range(3):
        ps.append(jnp.concatenate([add(p[k], chain.across(p[4 + k])), p[8 + k]]))
        if k == 0:
            pa1 = chain.along(ps[0], IN)
        elif k == 1:
            pa2 = chain.along(ps[1], IN)
            pb2 = chain.along(add(ps[0], pa1), MID)
        else:
            pa3 = chain.along(ps[2], IN)
            pb3 = chain.along(add(ps[1], pa2), MID)
            pc3 = chain.along(add(ps[2], pb2), OUT)
    px3 = chain.across(p[7])
    x0 = net.across(q[4])
    s0 = add(q[0], x0)
    b, s0 = lax.optimization_barrier((q[5], s0))
    x1, a1 = net.across(b), net.along(s0, IN)
    s1, t0 = add(q[1], x1), add(s0, a1)
    b, own, s1, t0, extra = lax.optimization_barrier((q[6], q[7], s1, t0, extra))
    x2, a2, b2, x3 = net.across(b), net.along(s1, IN), net.along(t0, MID), net.across(own)
    s2, t1 = add(q[2], x2), add(s1, a2)
    u = add(s2, b2)
    s2, t1, u = lax.optimization_barrier((s2, t1, u))
    a3, b3, c3 = net.along(s2, IN), net.along(t1, MID), net.along(u, OUT)
    total = add(jnp.concatenate([add(p[3], px3), p[11]]), pa3, pb3, pc3)
    rows, pair = p[3].shape[0], p[11].shape[0] // 2
    late = add(total[rows:rows + pair], net.across(total[rows + pair:]))
    first = jnp.concatenate([total[:rows - TAIL], late, total[rows - TAIL:rows]])
    return first, add(q[3], x3, a3, b3, c3), extra


def shards(tokens, lengths, cotangent, attend_gain, attend_shift, joint_weight, joint_bias, output_weight,
           output_bias, feed_gain, feed_shift, up_weight, up_bias, down_weight, down_bias):
    n = lax.axis_size("dp")
    r = D // n
    lined = n == 8
    nk = n if lined else 1
    sections = lax.axis_size("section")
    stages = sections // 2
    index = lax.axis_index("section")
    core, stage = index % 2, index // 2
    seq = tokens.shape[1]
    spot = lax.axis_index("dp")
    z = spot // 2
    middle = (z == 1) | (z == 2)
    def own_pair(a):
        return lax.dynamic_index_in_dim(a, core, 0, False)

    def padded(a):
        return jnp.pad(a, ((0, ROWS - seq), (0, 0)))

    places = lax.broadcasted_iota(jnp.int32, (8, ROWS), 1)
    mask = (((places < own_pair(lengths)) | (places >= CAPTION)) & (places < seq)).astype(F32)
    own_tokens = padded(own_pair(tokens))
    own_cotangent = padded(own_pair(cotangent))

    if lined:
        packed, pair = pack(joint_weight[0], output_weight[0], up_weight[0], down_weight[0], attend_gain, attend_shift,
                            joint_bias, output_bias, feed_gain, feed_shift, down_bias, up_bias)
        wa, wb, others = gather_blocks(packed, pair, middle, (own_tokens, own_cotangent, mask))
        own_tokens, own_cotangent, mask = others
    else:
        tail = vector_tail(n, spot, attend_gain[0], attend_shift[0], joint_bias[0], output_bias[0], feed_gain[0],
                           feed_shift[0], down_bias[0], up_bias[0])
        packed = pack_shard(joint_weight[0], output_weight[0], up_weight[0], down_weight[0], tail)
        gathered = lax.all_gather(packed, "dp")
        tails = lax.psum(tail.astype(BF).astype(F32), "dp")
        wa, wb = kernel_form(n, gathered, tails), kernel_form(n, swapped(gathered), swapped(tails))

    came = own_tokens
    for _ in range(stages - 1):
        came = moved(forward_stage(False, came, came, mask, wa, wb)[1], "section", 2)
        if stages > 2:
            came = jnp.where(stage == 0, own_tokens, came)
    got = forward_stage(True, own_tokens, came, mask, wa, wb)
    x, leaving = got[14], got[1]
    saved = [(x, *got[2:6]), (got[0], *got[8:12])]
    kept = [got[6], got[12]]
    received = [swapped(got[7]), swapped(got[13])]

    g = own_cotangent
    for t in range(stages - 1):
        g = backward_layers(False, (1, 0), g, mask, saved, wa, wb, None)[0]
        g = jnp.where(stage == stages - 1, own_cotangent, moved(g, "section", -2))
    products, operands = [None, None], [None, None]
    behind = mask
    for s in (1, 0):
        g, gv, bk, bs = backward_layers(True, (s,), g, mask, saved, wa, wb, behind)
        operands[s] = gv, kept[s], bk, received[s], swapped(bs)
    behind = g
    for s in (1, 0):
        products[s] = list(weight_products(nk, 2 * s if lined else 0, behind, *operands[s]))
        behind = products[s][0]

    g, products[0][-1] = lax.optimization_barrier((g, products[0][-1]))
    ends = jnp.where(stage == 0, g, leaving)[:seq].reshape(seq, stages, 2, D // sections)
    kept_half = lax.dynamic_index_in_dim(ends, stage, 1, False)
    got_half = flipped(lax.dynamic_index_in_dim(ends, 1 - stage, 1, False), 2)
    halves = jnp.stack([jnp.where(stage == 0, got_half, kept_half), jnp.where(stage == 0, kept_half, got_half)])
    kept_part = lax.dynamic_index_in_dim(halves, core, 2, False)
    got_part = flipped(lax.dynamic_index_in_dim(halves, 1 - core, 2, False), 1)
    parts = jnp.stack([jnp.where(core == 0, kept_part, got_part), jnp.where(core == 0, got_part, kept_part)], axis=1)

    reduced = [None, None]
    if lined:
        reduced[1], reduced[0], parts = scatter_both(products[1], products[0], parts)
    else:
        for s in range(2):
            p = products[s][0]
            col = jnp.swapaxes(p[:HALF * D].reshape(HALF, n, r, D), 0, 1).reshape(n, HALF * r, D)
            row = jnp.concatenate([p[:4 * D].reshape(n, 4 * r, D), col[:, 4 * r:]], axis=1)
            total = lax.psum_scatter(jnp.where(core == 0, col, row), "dp", scatter_dimension=0)
            reduced[s] = jnp.concatenate([total, lax.psum(p[HALF * D:], "dp")])
    sent = [lax.ppermute(reduced[s], "section", [(i, i ^ 1) for i in range(sections) if i % 2 != s]) for s in range(2)]
    outputs, token_grad = parts[0], parts[1]
    if lined:
        up, joint, out, down, ag, as_, jb, ob, fg, fs, db, ub = finish(r, reduced, sent)
        return (outputs, token_grad, ag, as_, joint[None], jb, out[None], ob, fg, fs, up[None], ub, down[None], db)
    keep = jnp.where(core == 0, reduced[0], reduced[1])
    away = jnp.where(core == 0, sent[0], sent[1])
    first = jnp.where(core == 0, keep, away).astype(F32)
    second = jnp.where(core == 0, away, keep).astype(F32)
    grad_up = jnp.concatenate([first[k * r:(k + 1) * r] for k in range(4)], axis=1)
    grad_joint = jnp.concatenate([first[4 * r:5 * r], first[5 * r:6 * r], second[5 * r:6 * r]], axis=1)
    grad_down = second[:4 * r]
    grad_out = second[4 * r:5 * r]
    v = first[6 * r:] + second[6 * r:]
    half, quarter = n // 2, n // 4
    vec = lax.dynamic_slice(v, (0, r * spot), (16, r))
    grad_jb = lax.dynamic_slice(v, (BQ + spot // half, 2 * r * (spot % half)), (1, 2 * r))
    grad_ub = lax.dynamic_slice(v, (UB + spot // quarter, 4 * r * (spot % quarter)), (1, 4 * r))
    return (outputs, token_grad, vec[AG:AG + 1], vec[AS:AS + 1], grad_joint[None], grad_jb, grad_out[None],
            vec[OB:OB + 1], vec[FG:FG + 1], vec[FS:FS + 1], grad_up[None], grad_ub, grad_down[None], vec[DB:DB + 1])


def solution(mesh):
    vec, mat = P("section", "dp"), P("section", "dp", None)
    rows = P("dp", None, None)
    out = P("dp", None, "section")
    return jax.shard_map(
        shards,
        mesh=mesh,
        in_specs=(rows, P("dp"), rows, vec, vec, mat, vec, mat, vec, vec, vec, mat, vec, mat, vec),
        out_specs=(out, out, vec, vec, mat, vec, mat, vec, vec, vec, mat, vec, mat, vec),
        check_vma=False,
    )
```
